32 devices in a mesh: dp: 4 (over y, core), mp: 8 (over z, x).
Axes of the slice: x: 2, y: 2, z: 4, core: 2. Of those that a mesh axis runs over, the one named last changes fastest.
Arguments:
- tokens: bfloat16 [32, 2048, 512], P('dp', 'mp'), may hold values from -6 to 6
- lengths: int32 [32, 4], P('dp'), may hold values from 0 to 2048, as said below
- cotangent: bfloat16 [32, 2048, 512], P('dp', 'mp'), may hold values from -6 to 6
- norm1_gain: bfloat16 [512], replicated, may hold values from 0.5 to 1.5
- value_proj: bfloat16 [512, 1024], P(None, 'mp'), may hold values from -0.25 to 0.25
- gate_proj: bfloat16 [512, 1024], P(None, 'mp'), may hold values from -0.25 to 0.25
- gate_bias: float32 [1024], P('mp')
- conv_taps: float32 [4, 1024], P(None, 'mp'), may hold values from -3 to 3
- conv_bias: float32 [1024], P('mp'), may hold values from -3 to 3
- out_proj: bfloat16 [1024, 512], P('mp'), may hold values from -0.375 to 0.375
- norm2_gain: bfloat16 [512], replicated, may hold values from 0.5 to 1.5
- up_proj: bfloat16 [512, 2048], P(None, 'mp'), may hold values from -0.25 to 0.25
- down_proj: bfloat16 [2048, 512], P('mp'), may hold values from -0.1875 to 0.1875
Outputs:
- output: bfloat16 [32, 2048, 512], P('dp', 'mp')
- tokens_grad: float32 [32, 2048, 512], P('dp', 'mp')
- norm1_gain_grad: float32 [512], replicated
- value_proj_grad: float32 [512, 1024], P(None, 'mp')
- gate_proj_grad: float32 [512, 1024], P(None, 'mp')
- gate_bias_grad: float32 [1024], P('mp')
- conv_taps_grad: float32 [4, 1024], P(None, 'mp')
- conv_bias_grad: float32 [1024], P('mp')
- out_proj_grad: float32 [1024, 512], P('mp')
- norm2_gain_grad: float32 [512], replicated
- up_proj_grad: float32 [512, 2048], P(None, 'mp')
- down_proj_grad: float32 [2048, 512], P('mp')
The draws below stay inside these ranges and needn't reach their ends.
Inputs may be any that keep to these rules, and one draw needn't show every extreme that they name: Each row holds one to 4 sequences packed from position 0, each of 256 tokens or more, followed by empty slots of 0; a row's lengths sum to at most 2048, and row 0 is one sequence of 2048 tokens.
All inputs are finite; a program needn't handle non-finite values.
Results may differ from the reference program's by a relative error of at most 0.0085.
Values may be sent and summed in bfloat16 or wider, within the bound.
A program may use at most 384 MiB of HBM per device.

```python
import jax
import jax.numpy as jnp
from jax import lax

MODEL_WIDTH = 512
RECURRENT_WIDTH = 1024
F = 2048
KW = 4
ROW_LENGTH = 2048
SLOTS = 4
MIN_SEQ_LENGTH = 256
PADDED_ROWS = 32


def draw_lengths(key, part):
    first_key, second_key = jax.random.split(key)
    picked = jax.random.randint(first_key, (PADDED_ROWS, SLOTS), 0, 10)
    level = (picked >= 5).astype(jnp.int32) + (picked >= 8).astype(jnp.int32) + (picked >= 9).astype(jnp.int32)
    scale_factor = jnp.where(level == 0, 1, jnp.where(level == 1, 2, jnp.where(level == 2, 4, 8)))
    random_jitter = jax.random.randint(second_key, (PADDED_ROWS, SLOTS), 0, MIN_SEQ_LENGTH)
    drawn_lengths = jnp.minimum(MIN_SEQ_LENGTH * scale_factor + random_jitter, ROW_LENGTH)
    sequence_bounds = jnp.cumsum(drawn_lengths, axis=1)
    kept_tokens = jnp.where(sequence_bounds <= ROW_LENGTH, drawn_lengths, 0)
    row_index = jnp.arange(PADDED_ROWS)[:, None]
    slot_position = jnp.arange(SLOTS)[None, :]
    entire_row_mask = jnp.where(slot_position == 0, ROW_LENGTH, 0)
    return jnp.where(row_index == 0, entire_row_mask, kept_tokens).astype(jnp.int32)


def draw_gate_bias(key, part):
    pick_key, slower_random_key, fast_key = jax.random.split(jax.random.fold_in(key, 7), 3)
    slow_share = 0.5
    slow_pick = jax.random.uniform(pick_key, (RECURRENT_WIDTH,), jnp.float32) < slow_share
    slower_gate_bias = jnp.log(jax.random.uniform(slower_random_key, (RECURRENT_WIDTH,), jnp.float32, 0.3, 2.0) / ROW_LENGTH) - 0.5
    fast_bias = jax.random.uniform(fast_key, (RECURRENT_WIDTH,), jnp.float32, -3.5, 0.0)
    return jnp.where(slow_pick, slower_gate_bias, fast_bias).astype(jnp.float32)


def block_levels(own_key, shape, cuts, smallest, top_value):
    def one(dim, parts):
        steps = jax.random.uniform(jax.random.fold_in(jax.random.fold_in(own_key, 6), dim), (parts,), jnp.float32, smallest / len(cuts), top_value / len(cuts))
        return jnp.repeat(jnp.exp(steps), shape[dim] // parts).reshape((-1,) + (1,) * (len(shape) - dim - 1))

    loudness = one(*cuts[0])
    for cut in cuts[1:]:
        loudness = loudness * one(*cut)
    return loudness


def gaussian(own_key, extent, width, reach, cuts=(), kind=jnp.bfloat16):
    values = jax.random.normal(own_key, extent, jnp.float32) * width
    if len(cuts) > 0:
        values = block_levels(own_key, extent, cuts, -0.22, 0.18) * values
    return jnp.clip(values, min=-reach, max=reach).astype(kind)


def setup_inputs(seed: int = 0) -> dict:
    keys = jax.random.split(jax.random.key(seed), 14)
    tokens = gaussian(keys[0], (PADDED_ROWS, ROW_LENGTH, MODEL_WIDTH), 1.0, 6.0, ((0, 4), (1, 8)))
    lengths = draw_lengths(jax.random.fold_in(keys[13], 71), 0)
    cotangent = gaussian(keys[2], (PADDED_ROWS, ROW_LENGTH, MODEL_WIDTH), 1.0, 6.0, ((0, 4), (1, 8)))
    norm1_gain = jnp.clip(1.0 + 0.1 * jax.random.normal(keys[3], (MODEL_WIDTH,), jnp.float32), 0.5, 1.5).astype(jnp.bfloat16)
    value_proj = gaussian(keys[4], (MODEL_WIDTH, RECURRENT_WIDTH), MODEL_WIDTH ** -0.5, 0.25, ((1, 8),))
    gate_proj = gaussian(keys[5], (MODEL_WIDTH, RECURRENT_WIDTH), MODEL_WIDTH ** -0.5, 0.25, ((1, 8),))
    gate_bias = draw_gate_bias(jax.random.fold_in(keys[13], 71), 0)
    conv_taps = gaussian(keys[7], (KW, RECURRENT_WIDTH), KW ** -0.5, 3.0, ((1, 8),), jnp.float32)
    conv_bias = gaussian(keys[8], (RECURRENT_WIDTH,), 0.5, 3.0, ((0, 8),), jnp.float32)
    out_proj = gaussian(keys[9], (RECURRENT_WIDTH, MODEL_WIDTH), (RECURRENT_WIDTH // 4) ** -0.5, 0.375, ((0, 8),))
    norm2_gain = jnp.clip(1.0 + 0.1 * jax.random.normal(keys[10], (MODEL_WIDTH,), jnp.float32), 0.5, 1.5).astype(jnp.bfloat16)
    up_proj = gaussian(keys[11], (MODEL_WIDTH, F), MODEL_WIDTH ** -0.5, 0.25, ((1, 8),))
    down_proj = gaussian(keys[12], (F, MODEL_WIDTH), (F // 2) ** -0.5, 0.1875, ((0, 8),))
    return dict(tokens=tokens, lengths=lengths, cotangent=cotangent, norm1_gain=norm1_gain, value_proj=value_proj, gate_proj=gate_proj, gate_bias=gate_bias, conv_taps=conv_taps, conv_bias=conv_bias, out_proj=out_proj, norm2_gain=norm2_gain, up_proj=up_proj, down_proj=down_proj)


norm_eps = 1e-06

@jax.custom_vjp
def low(v):
    return lax.optimization_barrier(v.astype(jnp.bfloat16)).astype(jnp.float32)

@jax.custom_vjp
def low_back(v):
    return v

def low_keep(v):
    return (low(v), None)

def low_pass(kept_tokens, grad):
    return (grad,)

def back_keep(v):
    return (v, None)

def back_low(kept_tokens, grad):
    return (low(grad),)
low.defvjp(low_keep, low_pass)
low_back.defvjp(back_keep, back_low)

def layout(row_lengths):
    token_places = jnp.arange(ROW_LENGTH, dtype=jnp.int32)
    sequence_bounds = jnp.cumsum(row_lengths).astype(jnp.int32)
    segment_ids = lax.optimization_barrier(jnp.sum((token_places[:, None] >= sequence_bounds[None, :]).astype(jnp.int32), axis=1))
    inside = (token_places < sequence_bounds[SLOTS - 1]).astype(jnp.float32)
    return (segment_ids, inside)

def rms_norm(values, gain_vec):
    return values * lax.rsqrt(lax.optimization_barrier(jnp.mean(values * values, axis=-1, keepdims=True)) + norm_eps) * gain_vec

def product(left, right):
    return jnp.dot(left, right, precision=lax.Precision.HIGHEST)

def delayed(values, shift_by):
    return jnp.concatenate([jnp.zeros((shift_by,) + values.shape[1:], values.dtype), values[:values.shape[0] - shift_by]], axis=0)

def linked(earlier, latter):
    return (earlier[0] * latter[0], latter[0] * earlier[1] + latter[1])

def block(row_block, segment_ids, inside, params):
    gain_one, w_value, w_gate, gate_b, conv_w, conv_b, w_out, gain_two, w_up, w_down = params
    normed = low(rms_norm(row_block, gain_one))
    values = low_back(product(normed, w_value))
    gate_pre = low_back(product(normed, w_gate) + gate_b)
    mixed_in = conv_b + conv_w[0] * values
    for start_offset in range(1, KW):
        same_sequence = jnp.concatenate([jnp.zeros((start_offset,), jnp.float32), (segment_ids[start_offset:] == segment_ids[:ROW_LENGTH - start_offset]).astype(jnp.float32)])
        mixed_in = mixed_in + conv_w[start_offset] * delayed(values, start_offset) * same_sequence[:, None]
    gate_open = jax.nn.sigmoid(gate_pre)
    continue_flag = jnp.concatenate([jnp.zeros((1,), jnp.float32), (segment_ids[1:] == segment_ids[:ROW_LENGTH - 1]).astype(jnp.float32)])
    keep_rate = (1.0 - gate_open) * continue_flag[:, None]
    _, states = lax.associative_scan(linked, (keep_rate, gate_open * mixed_in), axis=0)
    branch = low_back(product(low(states), w_out))
    residual = row_block + branch
    normed_two = low(rms_norm(low(residual), gain_two))
    hidden_pre = low_back(product(normed_two, w_up))
    hidden = low(jax.nn.gelu(hidden_pre, approximate=False))
    feed_out = low_back(product(hidden, w_down))
    return (residual + feed_out) * inside[:, None]

def reference(tokens, lengths, cotangent, norm1_gain, value_proj, gate_proj, gate_bias, conv_taps, conv_bias, out_proj, norm2_gain, up_proj, down_proj):
    params = tuple((weight.astype(jnp.float32) for weight in (norm1_gain, value_proj, gate_proj, gate_bias, conv_taps, conv_bias, out_proj, norm2_gain, up_proj, down_proj)))

    def one_row(totals, inputs):
        row_block, row_lengths, row_cot = inputs
        segment_ids, inside = layout(row_lengths)

        def forward(row_in, weights):
            return block(row_in, segment_ids, inside, weights)
        result, pullback = jax.vjp(forward, row_block.astype(jnp.float32), params)
        row_grad, weight_grads = pullback(row_cot.astype(jnp.float32))
        totals = jax.tree.map(lambda total, extra: total + extra, totals, weight_grads)
        return (totals, (result.astype(jnp.bfloat16), row_grad))
    start_sums = jax.tree.map(jnp.zeros_like, params)
    totals, (output, tokens_grad) = lax.scan(one_row, start_sums, (tokens, lengths, cotangent))
    return (output, tokens_grad, totals[0], totals[1], totals[2], totals[3], totals[4], totals[5], totals[6], totals[7], totals[8], totals[9])
```

```python
import functools

import jax
import jax.numpy as jnp
from jax import lax
from jax.experimental import pallas as pl
from jax.experimental.pallas import tpu as pltpu
from jax.sharding import PartitionSpec as P

KW = 4
NORM_EPS = 1e-06
BP = 32
CT = 256
FT = 512
MIB = 2**20
F32 = jnp.float32
BF16 = jnp.bfloat16

ERF_A = (0.254829592, -0.284496736, 1.421413741, -1.453152027, 1.061405429)
ERF_P = 0.3275911 * 0.7071067811865476
INV_ROOT_TWO_PI = 0.3989422804014327


def gelu_parts(x):
    t = 1.0 / (1.0 + ERF_P * jnp.abs(x))
    e = jnp.exp(-0.5 * (x * x))
    poly = 0.5 * ERF_A[4]
    for a in (ERF_A[3], ERF_A[2], ERF_A[1], ERF_A[0]):
        poly = poly * t + 0.5 * a
    tail = poly * t * e
    cdf = jnp.where(x >= 0, 1.0 - tail, tail)
    return x * cdf, cdf + x * (e * INV_ROOT_TWO_PI)


def dist_of(bounds_ref, first, count):
    place = (lax.broadcasted_iota(jnp.int32, (count, 8, 128), 0) + first).astype(F32)
    start = jnp.zeros((count, 8, 128), F32)
    for s in range(bounds_ref.shape[0]):
        b = bounds_ref[s][None]
        start = jnp.where(b <= place, jnp.maximum(start, b), start)
    return (place - start).reshape(count * 8, 128)


def wide(d):
    return jnp.concatenate([d] * (CT // 128), axis=1)


def dot(a, b):
    return jnp.dot(a, b, preferred_element_type=F32)


def dot_nt(a, b):
    return lax.dot_general(a, b, (((1,), (1,)), ((), ())), preferred_element_type=F32)


def dot_tn(a, b):
    return lax.dot_general(a, b, (((0,), (0,)), ((), ())), preferred_element_type=F32)


def mixer_kernel(span, x_ref, xh_ref, wv_ref, wg_ref, gain_ref, gb_ref, taps_ref, cb_ref, bounds_ref,
                 vals_ref, g_ref, m_ref, s_ref, a_ref, vbuf, gbuf, dbuf):
    step = pl.program_id(0)
    rows = BP * 8
    width = wv_ref.shape[1]
    gain = gain_ref[...]

    def normed(x):
        x = x.astype(F32)
        inv = lax.rsqrt(jnp.mean(x * x, axis=1, keepdims=True) + NORM_EPS)
        return (x * inv * gain).astype(BF16)

    @pl.when(step == 0)
    def _():
        vbuf[0:32] = dot(normed(xh_ref[...]), wv_ref[...])
        s_ref[...] = jnp.zeros_like(s_ref)
        a_ref[...] = jnp.ones_like(a_ref)

    n = normed(x_ref[...])
    vbuf[32 : 32 + rows] = dot(n, wv_ref[...])
    gbuf[...] = dot(n, wg_ref[...])
    first = lax.axis_index("mp") * span + step * BP
    dbuf[...] = dist_of(bounds_ref, first, BP)
    for c in range(0, width, CT):
        lanes = slice(c, c + CT)
        taps = [jnp.broadcast_to(taps_ref[j : j + 1, lanes], (8, CT)) for j in range(KW)]
        bias = jnp.broadcast_to(gb_ref[:, lanes], (8, CT))
        cb = jnp.broadcast_to(cb_ref[:, lanes], (8, CT))
        state, decay = s_ref[:, lanes], a_ref[:, lanes]
        v1, v2, v3 = vbuf[24:32, lanes], vbuf[16:24, lanes], vbuf[8:16, lanes]
        for p in range(BP):
            at = slice(8 * p, 8 * p + 8)
            v0 = vbuf[32 + 8 * p : 40 + 8 * p, lanes]
            gate = jax.nn.sigmoid(gbuf[at, lanes] + bias)
            d = wide(dbuf[at])
            mixed = cb + taps[0] * v0
            mixed = mixed + jnp.where(d >= 1.0, taps[1] * v1, 0.0)
            mixed = mixed + jnp.where(d >= 2.0, taps[2] * v2, 0.0)
            mixed = mixed + jnp.where(d >= 3.0, taps[3] * v3, 0.0)
            linked = jnp.where(d >= 1.0, state, 0.0)
            state = linked + gate * (mixed - linked)
            decay = jnp.where(d >= 1.0, decay * (1.0 - gate), 0.0)
            g_ref[at, lanes] = gate
            m_ref[at, lanes] = mixed
            v1, v2, v3 = v0, v1, v2
        s_ref[:, lanes], a_ref[:, lanes] = state, decay
    for r in range(0, rows, 32):
        vals_ref[r : r + 32] = vbuf[32 + r : 64 + r].astype(BF16)
    vbuf[0:32] = vbuf[rows : rows + 32]


def feed_kernel(span, x_ref, cot_ref, g_ref, m_ref, s0_ref, wo_ref, wu_ref, wd_ref, gain_ref, bounds_ref,
                out_ref, sg_ref, z_ref, rg_ref, dwo_ref, dwu_ref, dwd_ref, dgain_ref, acc_ref, c2_ref,
                state_ref, dbuf, stb, hp, dh, hb, hg):
    step = pl.program_id(0)
    rows = BP * 8
    width, units = wo_ref.shape[0], wu_ref.shape[1]

    @pl.when(step == 0)
    def _():
        state_ref[...] = s0_ref[...]
        dwo_ref[...] = jnp.zeros_like(dwo_ref)
        dwu_ref[...] = jnp.zeros_like(dwu_ref)
        dwd_ref[...] = jnp.zeros_like(dwd_ref)
        dgain_ref[...] = jnp.zeros_like(dgain_ref)
        acc_ref[...] = jnp.zeros_like(acc_ref)
        c2_ref[...] = jnp.ones_like(c2_ref)

    first = lax.axis_index("mp") * span + step * BP
    dbuf[...] = dist_of(bounds_ref, first, BP)
    for c in range(0, width, CT):
        lanes = slice(c, c + CT)
        state = state_ref[:, lanes]
        for p in range(0, BP, 2):
            pair = []
            for q in (p, p + 1):
                at = slice(8 * q, 8 * q + 8)
                linked = jnp.where(wide(dbuf[at]) >= 1.0, state, 0.0)
                z = m_ref[at, lanes] - linked
                state = linked + g_ref[at, lanes] * z
                z_ref[at, lanes] = z
                pair.append(state)
            stb[8 * p : 8 * p + 16, lanes] = jnp.concatenate(pair, axis=0).astype(BF16)
        state_ref[:, lanes] = state

    gain = gain_ref[...]
    place = (lax.broadcasted_iota(jnp.int32, (BP, 8, 128), 0) + first).astype(F32)
    last = bounds_ref.shape[0] - 1
    inside = jnp.where(place < bounds_ref[last][None], 1.0, 0.0).reshape(rows, 128)[:, 0:1]
    residual = x_ref[...].astype(F32) + dot(stb[...], wo_ref[...])
    resid = residual.astype(BF16).astype(F32)
    inv = lax.rsqrt(jnp.mean(resid * resid, axis=1, keepdims=True) + NORM_EPS)
    unit = resid * inv
    n2 = (unit * gain).astype(BF16)
    grad_out = cot_ref[...].astype(F32) * inside
    fg = grad_out.astype(BF16)
    for f in range(0, units, FT):
        cols = slice(f, f + FT)
        hp[...] = dot(n2, wu_ref[:, cols])
        dh[...] = dot_nt(fg, wd_ref[cols, :])
        for r in range(0, rows, 16):
            at = slice(r, r + 16)
            hidden, slope = gelu_parts(hp[at])
            hb[at, cols] = hidden.astype(BF16)
            hg[at, cols] = (dh[at] * slope).astype(BF16)
    feed_out = dot(hb[...], wd_ref[...])
    out_ref[...] = ((residual + feed_out) * inside).astype(BF16)
    ngrad = dot_nt(hg[...], wu_ref[...])
    dwd_ref[...] += dot_tn(fg, hb[...])
    dwu_ref[...] += dot_tn(n2, hg[...])
    weighted = ngrad * gain
    inner = jnp.mean(weighted * unit, axis=1, keepdims=True)
    rgrad = grad_out + inv * (weighted - unit * inner)
    rg_ref[...] = rgrad
    dgain_ref[...] += jnp.sum((ngrad * unit).reshape(BP, 8, -1), axis=0)
    mix = rgrad.astype(BF16)
    dwo_ref[...] += dot_tn(mix, stb[...])
    sg_ref[...] = dot_nt(mix, wo_ref[...])
    for c in range(0, width, CT):
        lanes = slice(c, c + CT)
        acc, decay = acc_ref[:, lanes], c2_ref[:, lanes]
        for p in range(BP):
            at = slice(8 * p, 8 * p + 8)
            keep = jnp.where(wide(dbuf[at]) >= 1.0, 1.0 - g_ref[at, lanes], 0.0)
            if p < 3:
                keep = jnp.where(step == 0, 1.0, keep)
            decay = decay * keep
            term = decay * sg_ref[at, lanes]
            if p < 2:
                term = jnp.where(step == 0, 0.0, term)
            acc = acc + term
        acc_ref[:, lanes], c2_ref[:, lanes] = acc, decay


def back_kernel(span, blocks, x_ref, sg_ref, g_ref, z_ref, v_ref, rg_ref, u0_ref, gn_ref, wv_ref, wg_ref, gain_ref, taps_ref,
                bounds_ref, tg_ref, dwv_ref, dwg_ref, dgain_ref, sums_ref, u_ref, gdel, dbuf, vg, gpg):
    step = pl.program_id(0)
    rows = BP * 8
    width = wv_ref.shape[1]

    @pl.when(step == 0)
    def _():
        u_ref[...] = u0_ref[...]
        gdel[...] = gn_ref[...]
        dwv_ref[...] = jnp.zeros_like(dwv_ref)
        dwg_ref[...] = jnp.zeros_like(dwg_ref)
        dgain_ref[...] = jnp.zeros_like(dgain_ref)
        sums_ref[...] = jnp.zeros_like(sums_ref)

    first = lax.axis_index("mp") * span + (blocks - 1 - step) * BP
    dbuf[...] = dist_of(bounds_ref, first, BP + 4)
    for c in range(0, width, CT):
        lanes = slice(c, c + CT)
        taps = [jnp.broadcast_to(taps_ref[j : j + 1, lanes], (8, CT)) for j in range(KW)]
        u = u_ref[:, lanes]
        g1, g2, g3 = (gdel[8 * i : 8 * i + 8, lanes] for i in range(3))
        sums = [sums_ref[8 * i : 8 * i + 8, lanes] for i in range(KW + 2)]
        for p in range(BP - 2, -2, -2):
            vals = v_ref[8 * p : 8 * p + 16, lanes].astype(F32)
            vgs, gpgs = [None, None], [None, None]
            for k in (1, 0):
                q = p + k
                at = slice(8 * q, 8 * q + 8)
                gate = g_ref[at, lanes]
                carried = sg_ref[at, lanes] + u
                g0 = carried * gate
                gp = g0 * z_ref[at, lanes] * (1.0 - gate)
                u = jnp.where(wide(dbuf[at]) >= 1.0, carried - g0, 0.0)
                h1 = jnp.where(wide(dbuf[8 * q + 8 : 8 * q + 16]) >= 1.0, g1, 0.0)
                h2 = jnp.where(wide(dbuf[8 * q + 16 : 8 * q + 24]) >= 2.0, g2, 0.0)
                h3 = jnp.where(wide(dbuf[8 * q + 24 : 8 * q + 32]) >= 3.0, g3, 0.0)
                v = vals[8 * k : 8 * k + 8]
                vgs[k] = taps[0] * g0 + taps[1] * h1 + taps[2] * h2 + taps[3] * h3
                gpgs[k] = gp
                for j, h in enumerate((g0, h1, h2, h3)):
                    sums[j] = sums[j] + v * h
                sums[KW] = sums[KW] + g0
                sums[KW + 1] = sums[KW + 1] + gp.astype(BF16).astype(F32)
                g1, g2, g3 = g0, g1, g2
            vg[8 * p : 8 * p + 16, lanes] = jnp.concatenate(vgs, axis=0).astype(BF16)
            gpg[8 * p : 8 * p + 16, lanes] = jnp.concatenate(gpgs, axis=0).astype(BF16)
        u_ref[:, lanes] = u
        for i, g in enumerate((g1, g2, g3)):
            gdel[8 * i : 8 * i + 8, lanes] = g
        for i in range(KW + 2):
            sums_ref[8 * i : 8 * i + 8, lanes] = sums[i]

    gain = gain_ref[...]
    x = x_ref[...].astype(F32)
    inv = lax.rsqrt(jnp.mean(x * x, axis=1, keepdims=True) + NORM_EPS)
    unit = x * inv
    n1 = (unit * gain).astype(BF16)
    dwv_ref[...] += dot_tn(n1, vg[...])
    dwg_ref[...] += dot_tn(n1, gpg[...])
    ngrad = dot_nt(vg[...], wv_ref[...]) + dot_nt(gpg[...], wg_ref[...])
    weighted = ngrad * gain
    inner = jnp.mean(weighted * unit, axis=1, keepdims=True)
    tg_ref[...] = rg_ref[...] + inv * (weighted - unit * inner)
    dgain_ref[...] += jnp.sum((ngrad * unit).reshape(BP, 8, -1), axis=0)


def whole(shape):
    return pl.BlockSpec(shape, lambda i: (0,) * len(shape))


def per_device(tokens, lengths, cotangent, norm1_gain, value_proj, gate_proj, gate_bias, conv_taps, conv_bias, out_proj,
               norm2_gain, up_proj, down_proj):
    rows, span, dim = tokens.shape
    n_mp = lax.axis_size("mp")
    me = lax.axis_index("mp")
    total = rows * span
    blocks = span // BP
    tile = BP * 8

    bounds = [lengths[:, 0]]
    for s in range(1, lengths.shape[1]):
        bounds.append(bounds[-1] + lengths[:, s])
    bounds = jnp.broadcast_to(jnp.stack(bounds, 0).astype(F32)[:, :, None], (lengths.shape[1], rows, 128))

    def time_major(a):
        return jnp.transpose(a, (1, 0, 2)).reshape(-1, a.shape[2])

    def row_major(a):
        return jnp.transpose(a.reshape(span, rows, dim), (1, 0, 2))

    halo = lax.ppermute(tokens[:, span - 4 :], "mp", [(i, i + 1) for i in range(n_mp - 1)])
    x_tm, cot_tm, halo_tm = time_major(tokens), time_major(cotangent), time_major(halo)
    def gather(w, axis):
        return lax.all_gather(w, "mp", axis=axis, tiled=True)
    wv, wg, wo = gather(value_proj, 1), gather(gate_proj, 1), gather(out_proj, 0)
    wu, wd = gather(up_proj, 1), gather(down_proj, 0)
    gate_b, cbias = gather(gate_bias, 0)[None], gather(conv_bias, 0)[None]
    taps = gather(conv_taps, 1)
    gain1, gain2 = norm1_gain.astype(F32)[None], norm2_gain.astype(F32)[None]
    width, units = wv.shape[1], wu.shape[1]

    def blk(w):
        return pl.BlockSpec((tile, w), lambda i: (i, 0))

    def rblk(w):
        return pl.BlockSpec((tile, w), lambda i: (blocks - 1 - i, 0))

    params = pltpu.CompilerParams(vmem_limit_bytes=58 * MIB)

    def sds(shape, t=F32):
        return jax.ShapeDtypeStruct(shape, t)

    vals, gate, mixed, s_end, a_end = pl.pallas_call(
        functools.partial(mixer_kernel, span),
        grid=(blocks,),
        in_specs=[blk(dim), whole((32, dim)), whole((dim, width)), whole((dim, width)), whole((1, dim)), whole((1, width)),
                  whole((KW, width)), whole((1, width)), whole(bounds.shape)],
        out_specs=[blk(width), blk(width), blk(width), whole((8, width)), whole((8, width))],
        out_shape=[sds((total, width), BF16), sds((total, width)), sds((total, width)), sds((8, width)), sds((8, width))],
        scratch_shapes=[pltpu.VMEM((tile + 32, width), F32), pltpu.VMEM((tile, width), F32), pltpu.VMEM((tile, 128), F32)],
        compiler_params=params,
        name="mixer",
    )(x_tm, halo_tm, wv, wg, gain1, gate_b, taps, cbias, bounds)

    s_all, a_all = lax.all_gather(s_end, "mp"), lax.all_gather(a_end, "mp")
    carry = jnp.zeros_like(s_end)
    s0 = carry
    for i in range(n_mp - 1):
        carry = s_all[i] + a_all[i] * carry
        s0 = jnp.where(me == i + 1, carry, s0)

    out_tm, sg, z, rg, dwo, dwu, dwd, dgain2, acc, c2 = pl.pallas_call(
        functools.partial(feed_kernel, span),
        grid=(blocks,),
        in_specs=[blk(dim), blk(dim), blk(width), blk(width), whole((8, width)), whole((width, dim)), whole((dim, units)),
                  whole((units, dim)), whole((1, dim)), whole(bounds.shape)],
        out_specs=[blk(dim), blk(width), blk(width), blk(dim), whole((dim, width)), whole((dim, units)), whole((dim, units)),
                   whole((8, dim)), whole((8, width)), whole((8, width))],
        out_shape=[sds((total, dim), BF16), sds((total, width)), sds((total, width)), sds((total, dim)), sds((dim, width)),
                   sds((dim, units)), sds((dim, units)), sds((8, dim)), sds((8, width)), sds((8, width))],
        scratch_shapes=[pltpu.VMEM((8, width), F32), pltpu.VMEM((tile, 128), F32), pltpu.VMEM((tile, width), BF16),
                        pltpu.VMEM((tile, FT), F32), pltpu.VMEM((tile, FT), F32), pltpu.VMEM((tile, units), BF16),
                        pltpu.VMEM((tile, units), BF16)],
        compiler_params=params,
        name="feed",
    )(x_tm, cot_tm, gate, mixed, s0, wo, wu, wd, gain2, bounds)

    first = me * span
    place = (first + jnp.arange(3)).astype(F32)[:, None]
    link = jnp.zeros((3, rows), bool)
    starts = jnp.concatenate([jnp.zeros_like(bounds[:1, :, 0]), bounds[:, :, 0]], 0)
    link = ~jnp.any(starts[None] == place[:, None], axis=1)
    g3 = gate[: 3 * 8].reshape(3, 8, width)
    k3 = jnp.where(link[:, :, None], 1.0 - g3, 0.0)
    sg2 = sg[: 2 * 8].reshape(2, 8, width)
    acc1 = sg2[1] + k3[2] * acc
    acc0 = sg2[0] + k3[1] * acc1
    c1 = k3[2] * c2
    c0 = k3[1] * c1
    b_all = lax.all_gather(k3[0] * acc0, "mp")
    u = jnp.zeros_like(s_end)
    u0, u_next = u, u
    for i in range(n_mp - 1, 0, -1):
        u_next = jnp.where(me == i - 1, u, u_next)
        u = b_all[i] + a_all[i] * u
        u0 = jnp.where(me == i - 1, u, u0)
    message = jnp.stack([g3[0] * acc0, g3[1] * acc1, g3[2] * acc, g3[0] * c0, g3[1] * c1, g3[2] * c2])
    message = lax.ppermute(message, "mp", [(i + 1, i) for i in range(n_mp - 1)])
    g_next = (message[:3] + message[3:] * u_next).reshape(24, width)

    tg_tm, dwv, dwg, dgain1, sums = pl.pallas_call(
        functools.partial(back_kernel, span, blocks),
        grid=(blocks,),
        in_specs=[rblk(dim), rblk(width), rblk(width), rblk(width), rblk(width), rblk(dim), whole((8, width)), whole((24, width)),
                  whole((dim, width)), whole((dim, width)), whole((1, dim)), whole((KW, width)), whole(bounds.shape)],
        out_specs=[rblk(dim), whole((dim, width)), whole((dim, width)), whole((8, dim)), whole((8 * (KW + 2), width))],
        out_shape=[sds((total, dim)), sds((dim, width)), sds((dim, width)), sds((8, dim)), sds((8 * (KW + 2), width))],
        scratch_shapes=[pltpu.VMEM((8, width), F32), pltpu.VMEM((24, width), F32), pltpu.VMEM((tile + 32, 128), F32),
                        pltpu.VMEM((tile, width), BF16), pltpu.VMEM((tile, width), BF16)],
        compiler_params=params,
        name="back",
    )(x_tm, sg, gate, z, vals, rg, u0, g_next, wv, wg, gain1, taps, bounds)

    def total_cols(g):
        return lax.psum(lax.psum_scatter(g.astype(BF16), "mp", scatter_dimension=1, tiled=True).astype(F32), "dp")

    sums = jnp.sum(sums.reshape(KW + 2, 8, width), axis=1)
    sums = lax.psum(lax.psum_scatter(sums, "mp", scatter_dimension=1, tiled=True), "dp")
    gains = lax.psum(jnp.stack([dgain1.sum(0), dgain2.sum(0)]), ("dp", "mp"))
    return (
        row_major(out_tm),
        row_major(tg_tm),
        gains[0],
        total_cols(dwv),
        total_cols(dwg),
        sums[KW + 1],
        sums[:KW],
        sums[KW],
        total_cols(dwo).T,
        gains[1],
        total_cols(dwu),
        total_cols(dwd).T,
    )


def solution(mesh):
    in_specs = (
        P("dp", "mp", None),
        P("dp", None),
        P("dp", "mp", None),
        P(),
        P(None, "mp"),
        P(None, "mp"),
        P("mp"),
        P(None, "mp"),
        P("mp"),
        P("mp", None),
        P(),
        P(None, "mp"),
        P("mp", None),
    )
    out_specs = (
        P("dp", "mp", None),
        P("dp", "mp", None),
        P(),
        P(None, "mp"),
        P(None, "mp"),
        P("mp"),
        P(None, "mp"),
        P("mp"),
        P("mp", None),
        P(),
        P(None, "mp"),
        P("mp", None),
    )
    return jax.shard_map(per_device, mesh=mesh, in_specs=in_specs, out_specs=out_specs, check_vma=False)
```

```python
import functools

import jax
import jax.numpy as jnp
from jax import lax
from jax.experimental import pallas as pl
from jax.experimental.pallas import tpu as pltpu
from jax.sharding import PartitionSpec as P

KW = 4
NORM_EPS = 1e-06
BP = 32
CT = 256
FT = 512
MIB = 2**20
F32 = jnp.float32
BF16 = jnp.bfloat16
MESH = pl.DeviceIdType.MESH
ANY = pl.BlockSpec(memory_space=pl.ANY)

ERF_A = (0.254829592, -0.284496736, 1.421413741, -1.453152027, 1.061405429)
ERF_P = 0.3275911 * 0.7071067811865476
INV_ROOT_TWO_PI = 0.3989422804014327


def gelu_parts(x):
    t = 1.0 / (1.0 + ERF_P * jnp.abs(x))
    e = jnp.exp(-0.5 * (x * x))
    poly = 0.5 * ERF_A[4]
    for a in (ERF_A[3], ERF_A[2], ERF_A[1], ERF_A[0]):
        poly = poly * t + 0.5 * a
    tail = poly * t * e
    cdf = jnp.where(x >= 0, 1.0 - tail, tail)
    return x * cdf, cdf + x * (e * INV_ROOT_TWO_PI)


def dist_of(bounds_ref, first, count):
    place = (lax.broadcasted_iota(jnp.int32, (count, 8, 128), 0) + first).astype(F32)
    start = jnp.zeros((count, 8, 128), F32)
    for s in range(bounds_ref.shape[0]):
        b = bounds_ref[s][None]
        start = jnp.where(b <= place, jnp.maximum(start, b), start)
    return (place - start).reshape(count * 8, 128)


def wide(d, width=CT):
    return jnp.concatenate([d] * (width // 128), axis=1)


def dot(a, b):
    return jnp.dot(a, b, preferred_element_type=F32)


def dot_nt(a, b):
    return lax.dot_general(a, b, (((1,), (1,)), ((), ())), preferred_element_type=F32)


def dot_tn(a, b):
    return lax.dot_general(a, b, (((0,), (0,)), ((), ())), preferred_element_type=F32)


class Place:
    def __init__(self):
        self.n_mp, self.n_dp = lax.axis_size("mp"), lax.axis_size("dp")
        self.n_a = self.n_mp // 2
        self.dp, self.mp = lax.axis_index("dp"), lax.axis_index("mp")
        self.a, self.b = self.mp // 2, self.mp % 2
        self.y, self.c = (self.dp // 2) % 2, self.dp % 2
        self.base = self.dp - self.y * 2 - self.c
        self.q = self.y * 2 + self.c

    def line(self, da):
        return (self.dp, lax.rem(self.a + da + self.n_a, self.n_a) * 2 + self.b)

    def pair(self):
        return (self.dp, self.a * 2 + 1 - self.b)

    def beside(self):
        return (self.base + (1 - self.y) * 2 + self.c, self.mp)

    def twin(self):
        return (self.base + self.y * 2 + 1 - self.c, self.mp)

    def across(self):
        return (self.base + (1 - self.y) * 2 + 1 - self.c, self.mp)

    def other(self, dm):
        return (self.dp, lax.rem(self.mp + dm, self.n_mp))

    def partners(self):
        return [self.twin(), self.beside(), self.across()] + [self.other(dm) for dm in range(1, self.n_mp)]

    def barrier(self):
        bar = pltpu.get_barrier_semaphore()
        devices = self.partners()
        for d in devices:
            pl.semaphore_signal(bar, inc=1, device_id=d, device_id_type=MESH)
        pl.semaphore_wait(bar, len(devices))


def remote(src, dst, send, recv, device):
    return pltpu.make_async_remote_copy(src_ref=src, dst_ref=dst, send_sem=send, recv_sem=recv, device_id=device, device_id_type=MESH)


class Gather:
    def __init__(self, here, wall, first, rows, send, recv):
        self.h, self.wall, self.first, self.rows, self.send, self.recv = here, wall, first, rows, send, recv
        n_a = here.n_a
        self.z0, self.x0, self.y0, self.t0 = 0, n_a, 2 * n_a, 4 * n_a
        self.used = []

    def span(self, shard, q):
        n = self.rows // 4
        return self.wall.at[pl.ds(pl.multiple_of(self.first + shard * self.rows + q * n, 16), n)]

    def move(self, sem, shard, q, device):
        s = self.span(shard, q)
        remote(s, s, self.send.at[sem], self.recv.at[sem], device).start()
        self.used.append(sem)

    def landed(self, sem, shard, q):
        s = self.span(shard, q)
        remote(s, s, self.send.at[sem], self.recv.at[sem], self.h.pair()).wait_recv()

    def shard(self, da, other):
        h = self.h
        return lax.rem(h.a - da + h.n_a, h.n_a) * 2 + ((1 - h.b) if other else h.b)

    def slot(self, da, other):
        return 2 * da + (1 if other else 0)

    def open(self):
        h = self.h
        self.move(self.x0, h.mp, h.q, h.pair())
        for da in range(1, h.n_a):
            self.move(self.z0 + da, h.mp, h.q, h.line(da))

    def spread(self, da, other):
        h, s = self.h, self.shard(da, other)
        self.move(self.y0 + self.slot(da, other), s, h.q, h.beside())
        self.move(self.t0 + 2 * self.slot(da, other), s, h.q, h.twin())

    def from_line(self, da):
        h = self.h
        self.landed(self.z0 + da, self.shard(da, False), h.q)
        self.move(self.x0 + da, self.shard(da, False), h.q, h.pair())
        self.spread(da, False)

    def from_pair(self, da):
        self.landed(self.x0 + da, self.shard(da, True), self.h.q)
        self.spread(da, True)

    def from_beside(self, da, other):
        h, s = self.h, self.shard(da, other)
        q = (1 - h.y) * 2 + h.c
        self.landed(self.y0 + self.slot(da, other), s, q)
        self.move(self.t0 + 2 * self.slot(da, other) + 1, s, q, h.twin())

    def from_twin(self, da, other):
        h, s = self.h, self.shard(da, other)
        self.landed(self.t0 + 2 * self.slot(da, other), s, h.y * 2 + 1 - h.c)
        self.landed(self.t0 + 2 * self.slot(da, other) + 1, s, (1 - h.y) * 2 + 1 - h.c)

    def close(self):
        s = self.wall.at[pl.ds(self.first, self.rows // 4)]
        for sem in self.used:
            remote(s, s, self.send.at[sem], self.recv.at[sem], self.h.pair()).wait_send()


def front_kernel(span, x_ref, cot_ref, wv_in, wg_in, wo_in, wu_in, wd_in, small_in, gain1_ref, gain2_ref, bounds_ref,
                 out_ref, sg_ref, rg_ref, dgain_ref, acc_ref, c2_ref, aend_ref, send_ref, g_out, z_out, v_out, wv_out, wg_out,
                 du_out, dd_out, do_out,
                 wall, nbuf, gsc, msc, vsc, vbuf, gbuf, dbuf, smalls, halo, carry, state_ref, stb, hp, dh, hb, hg,
                 dwo, dwu, dwd, stage, w_send, w_recv, s_send, s_recv, h_sem, c_send, c_recv, l_sem, z_sem, st_sem):
    here = Place()
    n_mp, n_a = here.n_mp, here.n_a
    dim = x_ref.shape[1]
    local_c, local_f = wv_in.shape[1], wu_in.shape[1]
    width, units = local_c * n_mp, local_f * n_mp
    tile_c = 2 * local_c
    rows = BP * 8
    blocks = span // BP
    step = pl.program_id(0)
    sections, first = {}, 0
    for k, (name, count) in enumerate((("wu", local_f), ("wd", local_f), ("wv", local_c), ("wg", local_c), ("wo", local_c))):
        sections[name] = Gather(here, wall, first, count, w_send.at[k], w_recv.at[k])
        first += count * n_mp
    wv, wg, wo, wu, wd = (sections[name] for name in ("wv", "wg", "wo", "wu", "wd"))
    far = range(1, n_a)

    def tile_of(da):
        return lax.rem(here.a - da + n_a, n_a)

    def small_copy(dm):
        return remote(smalls.at[here.mp], smalls.at[here.mp], s_send.at[dm], s_recv.at[dm], here.other(dm))

    def halo_copy():
        return remote(x_ref.at[pl.ds(span * 8 - 32, 32)], halo, h_sem.at[0], h_sem.at[1], here.other(1))

    def carry_copy(dm, t):
        lanes = pl.ds(pl.multiple_of(tile_of(t) * tile_c, tile_c), tile_c)
        block = carry.at[here.mp, :, lanes]
        return remote(block, block, c_send.at[dm, t], c_recv.at[dm, t], (here.dp, here.mp + dm))

    def local_copies():
        own = [pltpu.make_async_copy(gsc, g_out, l_sem.at[0]), pltpu.make_async_copy(vsc, v_out, l_sem.at[1])]
        own += [pltpu.make_async_copy(wall.at[pl.ds(s.first, width)], o, l_sem.at[2 + i]) for i, (s, o) in enumerate(((wv, wv_out), (wg, wg_out)))]
        return own

    def z_copy(i):
        at = pl.ds(pl.multiple_of(i * rows, rows), rows)
        return pltpu.make_async_copy(msc.at[at], z_out.at[at], z_sem.at[i])

    def normed(x):
        x = x.astype(F32)
        inv = lax.rsqrt(jnp.mean(x * x, axis=1, keepdims=True) + NORM_EPS)
        return (x * inv * gain1_ref[...]).astype(BF16)

    @pl.when(step == 0)
    def _():
        here.barrier()
        for s, w, turn in ((wv, wv_in, True), (wg, wg_in, True), (wo, wo_in, False), (wu, wu_in, True), (wd, wd_in, False)):
            block = w[...].astype(F32)
            block = block.T if turn else block
            wall[pl.ds(pl.multiple_of(s.first + here.mp * s.rows, 16), s.rows)] = block.astype(BF16)
            if s is wg:
                wv.open()
                wg.open()
        smalls[here.mp] = small_in[...]
        halo_copy().start()
        for dm in range(1, n_mp):
            small_copy(dm).start()

        @pl.loop(0, blocks)
        def _(i):
            nbuf[pl.ds(pl.multiple_of(32 + i * rows, 16), rows)] = normed(x_ref[pl.ds(pl.multiple_of(i * rows, rows), rows)])

        halo_copy().wait_recv()
        nbuf[0:32] = normed(halo[...])
        for dm in range(1, n_mp):
            small_copy(dm).wait_recv()
        for s in (wv, wg):
            s.from_pair(0)
        for da in far:
            for s in (wv, wg):
                s.from_line(da)
        for s in (wo, wu, wd):
            s.open()
        for s in (wv, wg):
            s.from_beside(0, True)

    @pl.when(step < n_a)
    def _():
        for s in (wv, wg):
            s.from_twin(step, True)

            @pl.when(step > 0)
            def _():
                s.from_twin(step, False)

        tile = tile_of(step)
        lanes = pl.ds(pl.multiple_of(tile * tile_c, tile_c), tile_c)
        wv_t = wall[pl.ds(pl.multiple_of(wv.first + tile * tile_c, tile_c), tile_c)]
        wg_t = wall[pl.ds(pl.multiple_of(wg.first + tile * tile_c, tile_c), tile_c)]
        small = jnp.concatenate([smalls[2 * tile, :, 0:local_c], smalls[2 * tile + 1, :, 0:local_c]], axis=1)
        taps = [jnp.broadcast_to(small[j : j + 1], (8, tile_c)) for j in range(KW)]
        bias = jnp.broadcast_to(small[KW : KW + 1], (8, tile_c))
        cb = jnp.broadcast_to(small[KW + 1 : KW + 2], (8, tile_c))
        vbuf[0:32] = dot_nt(nbuf[0:32], wv_t)

        def body(i, held):
            state, decay = held
            at = pl.ds(pl.multiple_of(32 + i * rows, 16), rows)
            vbuf[32 : 32 + rows] = dot_nt(nbuf[at], wv_t)
            gbuf[...] = dot_nt(nbuf[at], wg_t)
            dbuf[0:rows] = dist_of(bounds_ref, here.mp * span + i * BP, BP)
            v1, v2, v3 = vbuf[24:32], vbuf[16:24], vbuf[8:16]
            values = []
            for p in range(BP):
                at = slice(8 * p, 8 * p + 8)
                out_at = pl.ds(pl.multiple_of(i * rows + 8 * p, 8), 8)
                v0 = vbuf[32 + 8 * p : 40 + 8 * p]
                gate = jax.nn.sigmoid(gbuf[at] + bias)
                d = wide(dbuf[at], tile_c)
                mixed = cb + taps[0] * v0
                mixed = mixed + jnp.where(d >= 1.0, taps[1] * v1, 0.0)
                mixed = mixed + jnp.where(d >= 2.0, taps[2] * v2, 0.0)
                mixed = mixed + jnp.where(d >= 3.0, taps[3] * v3, 0.0)
                linked = jnp.where(d >= 1.0, state, 0.0)
                state = linked + gate * (mixed - linked)
                decay = jnp.where(d >= 1.0, decay * (1.0 - gate), 0.0)
                gsc[out_at, lanes] = gate
                msc[out_at, lanes] = mixed
                values.append(v0)
                if p % 2:
                    pair_at = pl.ds(pl.multiple_of(i * rows + 8 * p - 8, 16), 16)
                    vsc[pair_at, lanes] = jnp.concatenate(values, axis=0).astype(BF16)
                    values = []
                v1, v2, v3 = v0, v1, v2
            vbuf[0:32] = vbuf[rows : rows + 32]
            return state, decay

        state, decay = lax.fori_loop(0, blocks, body, (jnp.zeros((8, tile_c), F32), jnp.ones((8, tile_c), F32)))
        carry[here.mp, 0:8, lanes] = state
        carry[here.mp, 8:16, lanes] = decay
        for dm in range(1, n_mp):

            @pl.when(here.mp + dm < n_mp)
            def _():
                carry_copy(dm, step).start()

        @pl.when(step == 0)
        def _():
            for da in far:
                for s in (wv, wg):
                    s.from_pair(da)
            for s in (wv, wg):
                for da in far:
                    s.from_beside(da, False)
            for s in (wv, wg):
                for da in far:
                    s.from_beside(da, True)

        @pl.when(step == min(1, n_a - 1))
        def _():
            wo.from_pair(0)
            for da in far:
                wo.from_line(da)
            for da in far:
                wo.from_pair(da)

        @pl.when(step == min(2, n_a - 1))
        def _():
            wo.from_beside(0, True)
            for da in far:
                wo.from_beside(da, False)
                wo.from_beside(da, True)
            wu.from_pair(0)
            for da in far:
                wu.from_line(da)

        @pl.when(step == min(3, n_a - 1))
        def _():
            for da in far:
                wu.from_pair(da)
            wu.from_beside(0, True)
            for da in far:
                wu.from_beside(da, False)
            wd.from_pair(0)
            for da in far:
                wd.from_line(da)

    @pl.when(step == n_a)
    def _():
        for da in far:
            wd.from_pair(da)
        for da in far:
            wu.from_beside(da, True)
        wd.from_beside(0, True)
        for da in far:
            wd.from_beside(da, False)
            wd.from_beside(da, True)
        for dm in range(1, n_mp):

            @pl.when(here.mp - dm >= 0)
            def _():
                for t in range(n_a):
                    carry_copy(dm, t).wait_recv()

        start = jnp.zeros((8, width), F32)
        state_ref[...] = lax.fori_loop(0, here.mp, lambda i, s: carry[i, 0:8] + carry[i, 8:16] * s, start)
        for s in (wo, wu, wd):
            s.from_twin(0, True)
            for da in far:
                s.from_twin(da, True)
                s.from_twin(da, False)
        for copy in local_copies():
            copy.start()
        dwo[...] = jnp.zeros_like(dwo)
        dwu[...] = jnp.zeros_like(dwu)
        dwd[...] = jnp.zeros_like(dwd)
        dgain_ref[...] = jnp.zeros_like(dgain_ref)
        acc_ref[...] = jnp.zeros_like(acc_ref)
        c2_ref[...] = jnp.ones_like(c2_ref)
        aend_ref[...] = carry[here.mp, 8:16]
        send_ref[...] = carry[here.mp, 0:8]

    @pl.when(step >= n_a)
    def _():
        i = step - n_a
        base = pl.multiple_of(i * rows, rows)
        place0 = here.mp * span + i * BP
        dbuf[0:rows] = dist_of(bounds_ref, place0, BP)
        for c in range(0, width, CT):
            lanes = slice(c, c + CT)
            state = state_ref[:, lanes]
            for p in range(0, BP, 2):
                pair = []
                for q in (p, p + 1):
                    at = pl.ds(pl.multiple_of(base + 8 * q, 8), 8)
                    linked = jnp.where(wide(dbuf[8 * q : 8 * q + 8]) >= 1.0, state, 0.0)
                    z = msc[at, lanes] - linked
                    state = linked + gsc[at, lanes] * z
                    msc[at, lanes] = z
                    pair.append(state)
                stb[8 * p : 8 * p + 16, lanes] = jnp.concatenate(pair, axis=0).astype(BF16)
            state_ref[:, lanes] = state
        z_copy(i).start()

        def part(s, lo=0, hi=None):
            return wall[s.first + lo : s.first + (s.rows * n_mp if hi is None else hi)]

        gain = gain2_ref[...]
        place = (lax.broadcasted_iota(jnp.int32, (BP, 8, 128), 0) + place0).astype(F32)
        last = bounds_ref.shape[0] - 1
        inside = jnp.where(place < bounds_ref[last][None], 1.0, 0.0).reshape(rows, 128)[:, 0:1]
        residual = x_ref[pl.ds(base, rows)].astype(F32) + dot(stb[...], part(wo))
        resid = residual.astype(BF16).astype(F32)
        inv = lax.rsqrt(jnp.mean(resid * resid, axis=1, keepdims=True) + NORM_EPS)
        unit = resid * inv
        n2 = (unit * gain).astype(BF16)
        grad_out = cot_ref[...].astype(F32) * inside
        fg = grad_out.astype(BF16)
        for f in range(0, units, FT):
            cols = slice(f, f + FT)
            hp[...] = dot_nt(n2, part(wu, f, f + FT))
            dh[...] = dot_nt(fg, part(wd, f, f + FT))
            for r in range(0, rows, 16):
                at = slice(r, r + 16)
                hidden, slope = gelu_parts(hp[at])
                hb[at, cols] = hidden.astype(BF16)
                hg[at, cols] = (dh[at] * slope).astype(BF16)
        feed_out = dot(hb[...], part(wd))
        out_ref[...] = ((residual + feed_out) * inside).astype(BF16)
        ngrad = dot(hg[...], part(wu))
        dwd[...] += dot_tn(fg, hb[...])
        dwu[...] += dot_tn(n2, hg[...])
        weighted = ngrad * gain
        inner = jnp.mean(weighted * unit, axis=1, keepdims=True)
        rgrad = grad_out + inv * (weighted - unit * inner)
        rg_ref[...] = rgrad
        dgain_ref[...] += jnp.sum((ngrad * unit).reshape(BP, 8, -1), axis=0)
        mix = rgrad.astype(BF16)
        dwo[...] += dot_tn(mix, stb[...])
        sg_ref[...] = dot_nt(mix, part(wo))
        for c in range(0, width, CT):
            lanes = slice(c, c + CT)
            acc, decay = acc_ref[:, lanes], c2_ref[:, lanes]
            for p in range(BP):
                at = slice(8 * p, 8 * p + 8)
                gate = gsc[pl.ds(pl.multiple_of(base + 8 * p, 8), 8), lanes]
                keep = jnp.where(wide(dbuf[at]) >= 1.0, 1.0 - gate, 0.0)
                if p < 3:
                    keep = jnp.where(i == 0, 1.0, keep)
                decay = decay * keep
                term = decay * sg_ref[at, lanes]
                if p < 2:
                    term = jnp.where(i == 0, 0.0, term)
                acc = acc + term
            acc_ref[:, lanes], c2_ref[:, lanes] = acc, decay

    @pl.when(step == n_a + blocks - 1)
    def _():
        for copy in local_copies():
            copy.wait()
        for i in range(blocks):
            z_copy(i).wait()
        for s in (wv, wg, wo, wu, wd):
            s.close()
        halo_copy().wait_send()
        for dm in range(1, n_mp):
            small_copy(dm).wait_send()

            @pl.when(here.mp + dm < n_mp)
            def _():
                for t in range(n_a):
                    carry_copy(dm, t).wait_send()

        k = 0
        for acc, out, local in ((dwu, du_out, local_f), (dwd, dd_out, local_f), (dwo, do_out, local_c)):
            for s in range(n_mp):
                def move(j, ref, out=out, local=local, s=s):
                    return pltpu.make_async_copy(ref.at[:, 0 : out.shape[2]], out.at[s], st_sem.at[j])
                if k >= 2:
                    st_prev[k % 2]().wait()
                else:
                    st_prev = [None, None] if k == 0 else st_prev
                stage[k % 2, :, 0:local] = acc[:, s * local : (s + 1) * local].astype(BF16)
                copy = functools.partial(move, k % 2, stage.at[k % 2])
                copy().start()
                st_prev[k % 2] = copy
                k += 1
        for copy in st_prev:
            copy().wait()


def back_kernel(span, blocks, x_ref, sg_ref, g_ref, z_ref, v_ref, rg_ref, u0_ref, gn_ref, wv_ref, wg_ref, gain_ref, taps_ref,
                bounds_ref, tg_ref, dwv_ref, dwg_ref, dgain_ref, sums_ref, u_ref, gdel, dbuf, vg, gpg):
    step = pl.program_id(0)
    rows = BP * 8
    width = wv_ref.shape[0]

    @pl.when(step == 0)
    def _():
        u_ref[...] = u0_ref[...]
        gdel[...] = gn_ref[...]
        dwv_ref[...] = jnp.zeros_like(dwv_ref)
        dwg_ref[...] = jnp.zeros_like(dwg_ref)
        dgain_ref[...] = jnp.zeros_like(dgain_ref)
        sums_ref[...] = jnp.zeros_like(sums_ref)

    first = lax.axis_index("mp") * span + (blocks - 1 - step) * BP
    dbuf[...] = dist_of(bounds_ref, first, BP + 4)
    for c in range(0, width, CT):
        lanes = slice(c, c + CT)
        taps = [jnp.broadcast_to(taps_ref[j : j + 1, lanes], (8, CT)) for j in range(KW)]
        u = u_ref[:, lanes]
        g1, g2, g3 = (gdel[8 * i : 8 * i + 8, lanes] for i in range(3))
        sums = [sums_ref[8 * i : 8 * i + 8, lanes] for i in range(KW + 2)]
        for p in range(BP - 2, -2, -2):
            vals = v_ref[8 * p : 8 * p + 16, lanes].astype(F32)
            vgs, gpgs = [None, None], [None, None]
            for k in (1, 0):
                q = p + k
                at = slice(8 * q, 8 * q + 8)
                gate = g_ref[at, lanes]
                carried = sg_ref[at, lanes] + u
                g0 = carried * gate
                gp = g0 * z_ref[at, lanes] * (1.0 - gate)
                u = jnp.where(wide(dbuf[at]) >= 1.0, carried - g0, 0.0)
                h1 = jnp.where(wide(dbuf[8 * q + 8 : 8 * q + 16]) >= 1.0, g1, 0.0)
                h2 = jnp.where(wide(dbuf[8 * q + 16 : 8 * q + 24]) >= 2.0, g2, 0.0)
                h3 = jnp.where(wide(dbuf[8 * q + 24 : 8 * q + 32]) >= 3.0, g3, 0.0)
                v = vals[8 * k : 8 * k + 8]
                vgs[k] = taps[0] * g0 + taps[1] * h1 + taps[2] * h2 + taps[3] * h3
                gpgs[k] = gp
                for j, h in enumerate((g0, h1, h2, h3)):
                    sums[j] = sums[j] + v * h
                sums[KW] = sums[KW] + g0
                sums[KW + 1] = sums[KW + 1] + gp.astype(BF16).astype(F32)
                g1, g2, g3 = g0, g1, g2
            vg[8 * p : 8 * p + 16, lanes] = jnp.concatenate(vgs, axis=0).astype(BF16)
            gpg[8 * p : 8 * p + 16, lanes] = jnp.concatenate(gpgs, axis=0).astype(BF16)
        u_ref[:, lanes] = u
        for i, g in enumerate((g1, g2, g3)):
            gdel[8 * i : 8 * i + 8, lanes] = g
        for i in range(KW + 2):
            sums_ref[8 * i : 8 * i + 8, lanes] = sums[i]

    gain = gain_ref[...]
    x = x_ref[...].astype(F32)
    inv = lax.rsqrt(jnp.mean(x * x, axis=1, keepdims=True) + NORM_EPS)
    unit = x * inv
    n1 = (unit * gain).astype(BF16)
    dwv_ref[...] += dot_tn(n1, vg[...])
    dwg_ref[...] += dot_tn(n1, gpg[...])
    ngrad = dot(vg[...], wv_ref[...]) + dot(gpg[...], wg_ref[...])
    weighted = ngrad * gain
    inner = jnp.mean(weighted * unit, axis=1, keepdims=True)
    tg_ref[...] = rg_ref[...] + inv * (weighted - unit * inner)
    dgain_ref[...] += jnp.sum((ngrad * unit).reshape(BP, 8, -1), axis=0)


def whole(shape):
    return pl.BlockSpec(shape, lambda i: (0,) * len(shape))


def resident(shape):
    return pl.BlockSpec(shape, lambda i: (0,) * len(shape), pipeline_mode=pl.Buffered(1))


def per_device(tokens, lengths, cotangent, norm1_gain, value_proj, gate_proj, gate_bias, conv_taps, conv_bias, out_proj,
               norm2_gain, up_proj, down_proj):
    rows, span, dim = tokens.shape
    n_mp = lax.axis_size("mp")
    n_a = n_mp // 2
    me = lax.axis_index("mp")
    total = rows * span
    blocks = span // BP
    tile = BP * 8
    local_c, local_f = value_proj.shape[1], up_proj.shape[1]
    width, units = local_c * n_mp, local_f * n_mp

    bounds = [lengths[:, 0]]
    for s in range(1, lengths.shape[1]):
        bounds.append(bounds[-1] + lengths[:, s])
    bounds = jnp.broadcast_to(jnp.stack(bounds, 0).astype(F32)[:, :, None], (lengths.shape[1], rows, 128))

    def time_major(a):
        return jnp.transpose(a, (1, 0, 2)).reshape(-1, a.shape[2])

    def row_major(a):
        return jnp.transpose(a.reshape(span, rows, dim), (1, 0, 2))

    x_tm, cot_tm = time_major(tokens), time_major(cotangent)
    pad_c, pad_f = max(local_c, 128), max(local_f, 128)
    small = jnp.concatenate([conv_taps, gate_bias[None], conv_bias[None], jnp.zeros((2, local_c), F32)], axis=0)
    small = jnp.pad(small, ((0, 0), (0, pad_c - local_c)))
    gain1, gain2 = norm1_gain.astype(F32)[None], norm2_gain.astype(F32)[None]

    def late(w):
        return pl.BlockSpec((tile, w), lambda i: (jnp.maximum(i - n_a, 0), 0))

    def rblk(w):
        return pl.BlockSpec((tile, w), lambda i: (blocks - 1 - i, 0))

    def sds(shape, t=F32):
        return jax.ShapeDtypeStruct(shape, t)

    dma = pltpu.SemaphoreType.DMA
    vmem = pltpu.VMEM
    tile_c = 2 * local_c
    out_tm, sg, rg, dgain2, acc, c2, a_end, s_end, gate, z, vals, wv, wg, dwu, dwd, dwo = pl.pallas_call(
        functools.partial(front_kernel, span),
        grid=(n_a + blocks,),
        in_specs=[resident((total, dim)), late(dim), resident(value_proj.shape), resident(gate_proj.shape), resident(out_proj.shape),
                  resident(up_proj.shape), resident(down_proj.shape), resident(small.shape), resident((1, dim)), resident((1, dim)),
                  resident(bounds.shape)],
        out_specs=[late(dim), late(width), late(dim), resident((8, dim)), resident((8, width)), resident((8, width)),
                   resident((8, width)), resident((8, width)), ANY, ANY, ANY, ANY, ANY, ANY, ANY, ANY],
        out_shape=[sds((total, dim), BF16), sds((total, width)), sds((total, dim)), sds((8, dim)), sds((8, width)), sds((8, width)),
                   sds((8, width)), sds((8, width)), sds((total, width)), sds((total, width)), sds((total, width), BF16),
                   sds((width, dim), BF16), sds((width, dim), BF16), sds((n_mp, dim, pad_f), BF16), sds((n_mp, dim, pad_f), BF16),
                   sds((n_mp, dim, pad_c), BF16)],
        scratch_shapes=[
            vmem((3 * width + 2 * units, dim), BF16), vmem((total + 32, dim), BF16), vmem((total, width), F32), vmem((total, width), F32),
            vmem((total, width), BF16), vmem((tile + 32, tile_c), F32), vmem((tile, tile_c), F32), vmem((tile, 128), F32),
            vmem((n_mp, 8, pad_c), F32), vmem((32, dim), BF16), vmem((n_mp, 16, width), F32), vmem((8, width), F32),
            vmem((tile, width), BF16), vmem((tile, FT), F32), vmem((tile, FT), F32), vmem((tile, units), BF16), vmem((tile, units), BF16),
            vmem((dim, width), F32), vmem((dim, units), F32), vmem((dim, units), F32), vmem((2, dim, pad_f), BF16),
            dma((5, 8 * n_a)), dma((5, 8 * n_a)), dma((n_mp,)), dma((n_mp,)), dma((2,)), dma((n_mp, n_a)), dma((n_mp, n_a)), dma((4,)),
            dma((blocks,)), dma((2,)),
        ],
        compiler_params=pltpu.CompilerParams(collective_id=0, has_side_effects=True, vmem_limit_bytes=60 * MIB),
        name="front",
    )(x_tm, cot_tm, value_proj, gate_proj, out_proj, up_proj, down_proj, small, gain1, gain2, bounds)

    a_all = lax.all_gather(a_end, "mp")
    taps = lax.all_gather(conv_taps, "mp", axis=1, tiled=True)
    first = me * span
    place = (first + jnp.arange(3)).astype(F32)[:, None]
    starts = jnp.concatenate([jnp.zeros_like(bounds[:1, :, 0]), bounds[:, :, 0]], 0)
    link = ~jnp.any(starts[None] == place[:, None], axis=1)
    g3 = gate[: 3 * 8].reshape(3, 8, width)
    k3 = jnp.where(link[:, :, None], 1.0 - g3, 0.0)
    sg2 = sg[: 2 * 8].reshape(2, 8, width)
    acc1 = sg2[1] + k3[2] * acc
    acc0 = sg2[0] + k3[1] * acc1
    c1 = k3[2] * c2
    c0 = k3[1] * c1
    b_all = lax.all_gather(k3[0] * acc0, "mp")
    u = jnp.zeros_like(s_end)
    u0, u_next = u, u
    for i in range(n_mp - 1, 0, -1):
        u_next = jnp.where(me == i - 1, u, u_next)
        u = b_all[i] + a_all[i] * u
        u0 = jnp.where(me == i - 1, u, u0)
    message = jnp.stack([g3[0] * acc0, g3[1] * acc1, g3[2] * acc, g3[0] * c0, g3[1] * c1, g3[2] * c2])
    message = lax.ppermute(message, "mp", [(i + 1, i) for i in range(n_mp - 1)])
    g_next = (message[:3] + message[3:] * u_next).reshape(24, width)

    tg_tm, dwv, dwg, dgain1, sums = pl.pallas_call(
        functools.partial(back_kernel, span, blocks),
        grid=(blocks,),
        in_specs=[rblk(dim), rblk(width), rblk(width), rblk(width), rblk(width), rblk(dim), whole((8, width)), whole((24, width)),
                  whole((width, dim)), whole((width, dim)), whole((1, dim)), whole((KW, width)), whole(bounds.shape)],
        out_specs=[rblk(dim), whole((dim, width)), whole((dim, width)), whole((8, dim)), whole((8 * (KW + 2), width))],
        out_shape=[sds((total, dim)), sds((dim, width)), sds((dim, width)), sds((8, dim)), sds((8 * (KW + 2), width))],
        scratch_shapes=[pltpu.VMEM((8, width), F32), pltpu.VMEM((24, width), F32), pltpu.VMEM((tile + 32, 128), F32),
                        pltpu.VMEM((tile, width), BF16), pltpu.VMEM((tile, width), BF16)],
        compiler_params=pltpu.CompilerParams(vmem_limit_bytes=58 * MIB),
        name="back",
    )(x_tm, sg, gate, z, vals, rg, u0, g_next, wv, wg, gain1, taps, bounds)

    def total_cols(g):
        return lax.psum(lax.psum_scatter(g.astype(BF16), "mp", scatter_dimension=1, tiled=True).astype(F32), "dp")

    def total_first(g):
        return lax.psum(lax.psum_scatter(g, "mp", scatter_dimension=0, tiled=False).astype(F32), "dp")

    sums = jnp.sum(sums.reshape(KW + 2, 8, width), axis=1)
    sums = lax.psum(lax.psum_scatter(sums, "mp", scatter_dimension=1, tiled=True), "dp")
    gains = lax.psum(jnp.stack([dgain1.sum(0), dgain2.sum(0)]), ("dp", "mp"))
    return (
        row_major(out_tm),
        row_major(tg_tm),
        gains[0],
        total_cols(dwv),
        total_cols(dwg),
        sums[KW + 1],
        sums[:KW],
        sums[KW],
        total_first(dwo)[:, :local_c].T,
        gains[1],
        total_first(dwu)[:, :local_f],
        total_first(dwd)[:, :local_f].T,
    )


def solution(mesh):
    in_specs = (
        P("dp", "mp", None),
        P("dp", None),
        P("dp", "mp", None),
        P(),
        P(None, "mp"),
        P(None, "mp"),
        P("mp"),
        P(None, "mp"),
        P("mp"),
        P("mp", None),
        P(),
        P(None, "mp"),
        P("mp", None),
    )
    out_specs = (
        P("dp", "mp", None),
        P("dp", "mp", None),
        P(),
        P(None, "mp"),
        P(None, "mp"),
        P("mp"),
        P(None, "mp"),
        P("mp"),
        P("mp", None),
        P(),
        P(None, "mp"),
        P("mp", None),
    )
    return jax.shard_map(per_device, mesh=mesh, in_specs=in_specs, out_specs=out_specs, check_vma=False)
```

```python
import functools

import jax
import jax.numpy as jnp
from jax import lax
from jax.experimental import pallas as pl
from jax.experimental.pallas import tpu as pltpu
from jax.sharding import PartitionSpec as P

KW = 4
NORM_EPS = 1e-06
BP = 32
CT = 256
FT = 512
MIB = 2**20
F32 = jnp.float32
BF16 = jnp.bfloat16
MESH = pl.DeviceIdType.MESH
ANY = pl.BlockSpec(memory_space=pl.ANY)

ERF_A = (0.254829592, -0.284496736, 1.421413741, -1.453152027, 1.061405429)
ERF_P = 0.3275911 * 0.7071067811865476
INV_ROOT_TWO_PI = 0.3989422804014327


def gelu_parts(x):
    t = 1.0 / (1.0 + ERF_P * jnp.abs(x))
    e = jnp.exp(-0.5 * (x * x))
    poly = 0.5 * ERF_A[4]
    for a in (ERF_A[3], ERF_A[2], ERF_A[1], ERF_A[0]):
        poly = poly * t + 0.5 * a
    tail = poly * t * e
    cdf = jnp.where(x >= 0, 1.0 - tail, tail)
    return x * cdf, cdf + x * (e * INV_ROOT_TWO_PI)


def dist_of(bounds_ref, first, count):
    place = (lax.broadcasted_iota(jnp.int32, (count, 8, 128), 0) + first).astype(F32)
    start = jnp.zeros((count, 8, 128), F32)
    for s in range(bounds_ref.shape[0]):
        b = bounds_ref[s][None]
        start = jnp.where(b <= place, jnp.maximum(start, b), start)
    return (place - start).reshape(count * 8, 128)


def wide(d, width=CT):
    return jnp.concatenate([d] * (width // 128), axis=1)


def dot(a, b):
    return jnp.dot(a, b, preferred_element_type=F32)


def dot_nt(a, b):
    return lax.dot_general(a, b, (((1,), (1,)), ((), ())), preferred_element_type=F32)


def dot_tn(a, b):
    return lax.dot_general(a, b, (((0,), (0,)), ((), ())), preferred_element_type=F32)


class Place:
    def __init__(self):
        self.n_mp, self.n_dp = lax.axis_size("mp"), lax.axis_size("dp")
        self.n_a = self.n_mp // 2
        self.dp, self.mp = lax.axis_index("dp"), lax.axis_index("mp")
        self.a, self.b = self.mp // 2, self.mp % 2
        self.y, self.c = (self.dp // 2) % 2, self.dp % 2
        self.base = self.dp - self.y * 2 - self.c
        self.q = self.c * 2 + self.y

    def line(self, da):
        return (self.dp, lax.rem(self.a + da + self.n_a, self.n_a) * 2 + self.b)

    def pair(self):
        return (self.dp, self.a * 2 + 1 - self.b)

    def beside(self):
        return (self.base + (1 - self.y) * 2 + self.c, self.mp)

    def twin(self):
        return (self.base + self.y * 2 + 1 - self.c, self.mp)

    def across(self):
        return (self.base + (1 - self.y) * 2 + 1 - self.c, self.mp)

    def other(self, dm):
        return (self.dp, lax.rem(self.mp + dm, self.n_mp))

    def partners(self):
        group = [(lax.rem(self.dp + k, self.n_dp), self.mp) for k in range(1, self.n_dp)]
        return group + [self.other(dm) for dm in range(1, self.n_mp)]

    def barrier(self):
        bar = pltpu.get_barrier_semaphore()
        devices = self.partners()
        for d in devices:
            pl.semaphore_signal(bar, inc=1, device_id=d, device_id_type=MESH)
        pl.semaphore_wait(bar, len(devices))


def remote(src, dst, send, recv, device):
    return pltpu.make_async_remote_copy(src_ref=src, dst_ref=dst, send_sem=send, recv_sem=recv, device_id=device, device_id_type=MESH)


class Gather:
    def __init__(self, here, wall, first, rows, send, recv):
        self.h, self.wall, self.first, self.rows, self.send, self.recv = here, wall, first, rows, send, recv
        n_a = here.n_a
        self.z0, self.x0, self.y0, self.t0 = 0, n_a, 2 * n_a, 4 * n_a
        self.used = []

    def span(self, shard, q):
        n = self.rows // 4
        return self.wall.at[pl.ds(pl.multiple_of(self.first + shard * self.rows + q * n, 16), n)]

    def move(self, sem, shard, q, device):
        s = self.span(shard, q)
        remote(s, s, self.send.at[sem], self.recv.at[sem], device).start()
        self.used.append(sem)

    def landed(self, sem, shard, q):
        s = self.span(shard, q)
        remote(s, s, self.send.at[sem], self.recv.at[sem], self.h.pair()).wait_recv()

    def shard(self, da, other):
        h = self.h
        return lax.rem(h.a - da + h.n_a, h.n_a) * 2 + ((1 - h.b) if other else h.b)

    def slot(self, da, other):
        return 2 * da + (1 if other else 0)

    def open(self):
        h = self.h
        self.move(self.x0, h.mp, h.q, h.pair())
        for da in range(1, h.n_a):
            self.move(self.z0 + da, h.mp, h.q, h.line(da))

    def spread(self, da, other):
        h, s = self.h, self.shard(da, other)
        self.move(self.y0 + self.slot(da, other), s, h.q, h.beside())
        self.move(self.t0 + 2 * self.slot(da, other), s, h.q, h.twin())

    def from_line(self, da):
        h = self.h
        self.landed(self.z0 + da, self.shard(da, False), h.q)
        self.move(self.x0 + da, self.shard(da, False), h.q, h.pair())
        self.spread(da, False)

    def from_pair(self, da):
        self.landed(self.x0 + da, self.shard(da, True), self.h.q)
        self.spread(da, True)

    def from_beside(self, da, other):
        h, s = self.h, self.shard(da, other)
        q = h.c * 2 + 1 - h.y
        self.landed(self.y0 + self.slot(da, other), s, q)
        self.move(self.t0 + 2 * self.slot(da, other) + 1, s, q, h.twin())

    def from_twin(self, da, other):
        h, s = self.h, self.shard(da, other)
        self.landed(self.t0 + 2 * self.slot(da, other), s, (1 - h.c) * 2 + h.y)
        self.landed(self.t0 + 2 * self.slot(da, other) + 1, s, (1 - h.c) * 2 + 1 - h.y)

    def close(self):
        s = self.wall.at[pl.ds(self.first, self.rows // 4)]
        for sem in self.used:
            remote(s, s, self.send.at[sem], self.recv.at[sem], self.h.pair()).wait_send()


def front_kernel(span, x_ref, cot_ref, wv_in, wg_in, wo_in, wu_in, wd_in, small_in, gain1_ref, gain2_ref, bounds_ref,
                 out_ref, sg_ref, rg_ref, dgain_ref, ba_ref, msg_ref, small_out, g_out, z_out, v_out, wv_out, wg_out, f_out,
                 wall, nbuf, gsc, msc, vsc, vbuf, gbuf, dbuf, smalls, halo, carry, state_ref, acc_ref, c2_ref, sg_head, stb, hp, dh, hb, hg,
                 dwo, dwu, dwd, stage, w_send, w_recv, s_send, s_recv, h_sem, c_send, c_recv, l_sem, z_sem, st_sem):
    here = Place()
    n_mp, n_a = here.n_mp, here.n_a
    dim = x_ref.shape[1]
    local_c, local_f = wv_in.shape[1], wu_in.shape[1]
    width, units = local_c * n_mp, local_f * n_mp
    tile_c = 2 * local_c
    rows = BP * 8
    blocks = span // BP
    step = pl.program_id(0)
    sections, first = {}, 0
    for k, (name, count) in enumerate((("wu", local_f), ("wd", local_f), ("wv", local_c), ("wg", local_c), ("wo", local_c))):
        sections[name] = Gather(here, wall, first, count, w_send.at[k], w_recv.at[k])
        first += count * n_mp
    wv, wg, wo, wu, wd = (sections[name] for name in ("wv", "wg", "wo", "wu", "wd"))
    far = range(1, n_a)

    def tile_of(da):
        return lax.rem(here.a - da + n_a, n_a)

    def small_copy(dm):
        return remote(smalls.at[here.mp], smalls.at[here.mp], s_send.at[dm], s_recv.at[dm], here.other(dm))

    def halo_copy():
        return remote(x_ref.at[pl.ds(span * 8 - 32, 32)], halo, h_sem.at[0], h_sem.at[1], here.other(1))

    def carry_copy(dm, t):
        lanes = pl.ds(pl.multiple_of(tile_of(t) * tile_c, tile_c), tile_c)
        block = carry.at[here.mp, :, lanes]
        return remote(block, block, c_send.at[dm, t], c_recv.at[dm, t], (here.dp, here.mp + dm))

    def local_copies():
        own = [pltpu.make_async_copy(gsc, g_out, l_sem.at[0]), pltpu.make_async_copy(vsc, v_out, l_sem.at[1])]
        own += [pltpu.make_async_copy(wall.at[pl.ds(s.first, width)], o, l_sem.at[2 + i]) for i, (s, o) in enumerate(((wv, wv_out), (wg, wg_out)))]
        return own

    def z_copy(i):
        at = pl.ds(pl.multiple_of(i * rows, rows), rows)
        return pltpu.make_async_copy(msc.at[at], z_out.at[at], z_sem.at[i])

    def normed(x):
        x = x.astype(F32)
        inv = lax.rsqrt(jnp.mean(x * x, axis=1, keepdims=True) + NORM_EPS)
        return (x * inv * gain1_ref[...]).astype(BF16)

    @pl.when(step == 0)
    def _():
        here.barrier()
        for s, w, turn in ((wv, wv_in, True), (wg, wg_in, True), (wo, wo_in, False), (wu, wu_in, True), (wd, wd_in, False)):
            block = w[...].astype(F32)
            block = block.T if turn else block
            wall[pl.ds(pl.multiple_of(s.first + here.mp * s.rows, 16), s.rows)] = block.astype(BF16)
            if s is wg:
                wv.open()
                wg.open()
        smalls[here.mp] = small_in[...]
        halo_copy().start()
        for dm in range(1, n_mp):
            small_copy(dm).start()

        @pl.loop(0, blocks)
        def _(i):
            nbuf[pl.ds(pl.multiple_of(32 + i * rows, 16), rows)] = normed(x_ref[pl.ds(pl.multiple_of(i * rows, rows), rows)])

        halo_copy().wait_recv()
        nbuf[0:32] = normed(halo[...])
        for dm in range(1, n_mp):
            small_copy(dm).wait_recv()
        for s in (wv, wg):
            s.from_pair(0)
        for da in far:
            for s in (wv, wg):
                s.from_line(da)
        for s in (wo, wu, wd):
            s.open()
        for s in (wv, wg):
            s.from_beside(0, True)

    @pl.when(step < n_a)
    def _():
        for s in (wv, wg):
            s.from_twin(step, True)

            @pl.when(step > 0)
            def _():
                s.from_twin(step, False)

        tile = tile_of(step)
        lanes = pl.ds(pl.multiple_of(tile * tile_c, tile_c), tile_c)
        wv_t = wall[pl.ds(pl.multiple_of(wv.first + tile * tile_c, tile_c), tile_c)]
        wg_t = wall[pl.ds(pl.multiple_of(wg.first + tile * tile_c, tile_c), tile_c)]
        small = jnp.concatenate([smalls[2 * tile, :, 0:local_c], smalls[2 * tile + 1, :, 0:local_c]], axis=1)
        taps = [jnp.broadcast_to(small[j : j + 1], (8, tile_c)) for j in range(KW)]
        bias = jnp.broadcast_to(small[KW : KW + 1], (8, tile_c))
        cb = jnp.broadcast_to(small[KW + 1 : KW + 2], (8, tile_c))
        vbuf[0:32] = dot_nt(nbuf[0:32], wv_t)

        def body(i, held):
            state, decay = held
            at = pl.ds(pl.multiple_of(32 + i * rows, 16), rows)
            vbuf[32 : 32 + rows] = dot_nt(nbuf[at], wv_t)
            gbuf[...] = dot_nt(nbuf[at], wg_t)
            dbuf[0:rows] = dist_of(bounds_ref, here.mp * span + i * BP, BP)
            v1, v2, v3 = vbuf[24:32], vbuf[16:24], vbuf[8:16]
            values = []
            for p in range(BP):
                at = slice(8 * p, 8 * p + 8)
                out_at = pl.ds(pl.multiple_of(i * rows + 8 * p, 8), 8)
                v0 = vbuf[32 + 8 * p : 40 + 8 * p]
                gate = jax.nn.sigmoid(gbuf[at] + bias)
                d = wide(dbuf[at], tile_c)
                mixed = cb + taps[0] * v0
                mixed = mixed + jnp.where(d >= 1.0, taps[1] * v1, 0.0)
                mixed = mixed + jnp.where(d >= 2.0, taps[2] * v2, 0.0)
                mixed = mixed + jnp.where(d >= 3.0, taps[3] * v3, 0.0)
                linked = jnp.where(d >= 1.0, state, 0.0)
                state = linked + gate * (mixed - linked)
                decay = jnp.where(d >= 1.0, decay * (1.0 - gate), 0.0)
                gsc[out_at, lanes] = gate
                msc[out_at, lanes] = mixed
                values.append(v0)
                if p % 2:
                    pair_at = pl.ds(pl.multiple_of(i * rows + 8 * p - 8, 16), 16)
                    vsc[pair_at, lanes] = jnp.concatenate(values, axis=0).astype(BF16)
                    values = []
                v1, v2, v3 = v0, v1, v2
            vbuf[0:32] = vbuf[rows : rows + 32]
            return state, decay

        state, decay = lax.fori_loop(0, blocks, body, (jnp.zeros((8, tile_c), F32), jnp.ones((8, tile_c), F32)))
        carry[here.mp, 0:8, lanes] = state
        carry[here.mp, 8:16, lanes] = decay
        for dm in range(1, n_mp):

            @pl.when(here.mp + dm < n_mp)
            def _():
                carry_copy(dm, step).start()

        @pl.when(step == 0)
        def _():
            for da in far:
                for s in (wv, wg):
                    s.from_pair(da)
            for s in (wv, wg):
                for da in far:
                    s.from_beside(da, False)
            for s in (wv, wg):
                for da in far:
                    s.from_beside(da, True)

        @pl.when(step == min(1, n_a - 1))
        def _():
            wo.from_pair(0)
            for da in far:
                wo.from_line(da)
            for da in far:
                wo.from_pair(da)

        @pl.when(step == min(2, n_a - 1))
        def _():
            wo.from_beside(0, True)
            for da in far:
                wo.from_beside(da, False)
                wo.from_beside(da, True)
            wu.from_pair(0)
            for da in far:
                wu.from_line(da)

        @pl.when(step == min(3, n_a - 1))
        def _():
            for da in far:
                wu.from_pair(da)
            wu.from_beside(0, True)
            for da in far:
                wu.from_beside(da, False)
            wd.from_pair(0)
            for da in far:
                wd.from_line(da)

    @pl.when(step == n_a)
    def _():
        for da in far:
            wd.from_pair(da)
        for da in far:
            wu.from_beside(da, True)
        wd.from_beside(0, True)
        for da in far:
            wd.from_beside(da, False)
            wd.from_beside(da, True)
        for dm in range(1, n_mp):

            @pl.when(here.mp - dm >= 0)
            def _():
                for t in range(n_a):
                    carry_copy(dm, t).wait_recv()

        start = jnp.zeros((8, width), F32)
        state_ref[...] = lax.fori_loop(0, here.mp, lambda i, s: carry[i, 0:8] + carry[i, 8:16] * s, start)
        for s in (wo, wu, wd):
            s.from_twin(0, True)
            for da in far:
                s.from_twin(da, True)
                s.from_twin(da, False)
        for copy in local_copies():
            copy.start()
        dwo[...] = jnp.zeros_like(dwo)
        dwu[...] = jnp.zeros_like(dwu)
        dwd[...] = jnp.zeros_like(dwd)
        dgain_ref[...] = jnp.zeros_like(dgain_ref)
        acc_ref[...] = jnp.zeros_like(acc_ref)
        c2_ref[...] = jnp.ones_like(c2_ref)
        small_out[...] = smalls[...]

    @pl.when(step >= n_a)
    def _():
        i = step - n_a
        base = pl.multiple_of(i * rows, rows)
        place0 = here.mp * span + i * BP
        dbuf[0:rows] = dist_of(bounds_ref, place0, BP)
        for c in range(0, width, CT):
            lanes = slice(c, c + CT)
            state = state_ref[:, lanes]
            for p in range(0, BP, 2):
                pair = []
                for q in (p, p + 1):
                    at = pl.ds(pl.multiple_of(base + 8 * q, 8), 8)
                    linked = jnp.where(wide(dbuf[8 * q : 8 * q + 8]) >= 1.0, state, 0.0)
                    z = msc[at, lanes] - linked
                    state = linked + gsc[at, lanes] * z
                    msc[at, lanes] = z
                    pair.append(state)
                stb[8 * p : 8 * p + 16, lanes] = jnp.concatenate(pair, axis=0).astype(BF16)
            state_ref[:, lanes] = state
        z_copy(i).start()

        def part(s, lo=0, hi=None):
            return wall[s.first + lo : s.first + (s.rows * n_mp if hi is None else hi)]

        gain = gain2_ref[...]
        place = (lax.broadcasted_iota(jnp.int32, (BP, 8, 128), 0) + place0).astype(F32)
        last = bounds_ref.shape[0] - 1
        inside = jnp.where(place < bounds_ref[last][None], 1.0, 0.0).reshape(rows, 128)[:, 0:1]
        residual = x_ref[pl.ds(base, rows)].astype(F32) + dot(stb[...], part(wo))
        resid = residual.astype(BF16).astype(F32)
        inv = lax.rsqrt(jnp.mean(resid * resid, axis=1, keepdims=True) + NORM_EPS)
        unit = resid * inv
        n2 = (unit * gain).astype(BF16)
        grad_out = cot_ref[...].astype(F32) * inside
        fg = grad_out.astype(BF16)
        for f in range(0, units, FT):
            cols = slice(f, f + FT)
            hp[...] = dot_nt(n2, part(wu, f, f + FT))
            dh[...] = dot_nt(fg, part(wd, f, f + FT))
            for r in range(0, rows, 16):
                at = slice(r, r + 16)
                hidden, slope = gelu_parts(hp[at])
                hb[at, cols] = hidden.astype(BF16)
                hg[at, cols] = (dh[at] * slope).astype(BF16)
        feed_out = dot(hb[...], part(wd))
        out_ref[...] = ((residual + feed_out) * inside).astype(BF16)
        ngrad = dot(hg[...], part(wu))
        dwd[...] += dot_tn(fg, hb[...])
        dwu[...] += dot_tn(n2, hg[...])
        weighted = ngrad * gain
        inner = jnp.mean(weighted * unit, axis=1, keepdims=True)
        rgrad = grad_out + inv * (weighted - unit * inner)
        rg_ref[...] = rgrad
        dgain_ref[...] += jnp.sum((ngrad * unit).reshape(BP, 8, -1), axis=0)
        mix = rgrad.astype(BF16)
        dwo[...] += dot_tn(mix, stb[...])
        sg_ref[...] = dot_nt(mix, part(wo))
        @pl.when(i == 0)
        def _():
            sg_head[...] = sg_ref[0:16]

        for c in range(0, width, CT):
            lanes = slice(c, c + CT)
            acc, decay = acc_ref[:, lanes], c2_ref[:, lanes]
            for p in range(BP):
                at = slice(8 * p, 8 * p + 8)
                gate = gsc[pl.ds(pl.multiple_of(base + 8 * p, 8), 8), lanes]
                keep = jnp.where(wide(dbuf[at]) >= 1.0, 1.0 - gate, 0.0)
                if p < 3:
                    keep = jnp.where(i == 0, 1.0, keep)
                decay = decay * keep
                term = decay * sg_ref[at, lanes]
                if p < 2:
                    term = jnp.where(i == 0, 0.0, term)
                acc = acc + term
            acc_ref[:, lanes], c2_ref[:, lanes] = acc, decay

    @pl.when(step == n_a + blocks - 1)
    def _():
        for copy in local_copies():
            copy.wait()
        for i in range(blocks):
            z_copy(i).wait()
        for s in (wv, wg, wo, wu, wd):
            s.close()
        halo_copy().wait_send()
        for dm in range(1, n_mp):
            small_copy(dm).wait_send()

            @pl.when(here.mp + dm < n_mp)
            def _():
                for t in range(n_a):
                    carry_copy(dm, t).wait_send()

        d3 = dist_of(bounds_ref, here.mp * span, 3)
        for c in range(0, width, CT):
            lanes = slice(c, c + CT)
            g3 = [gsc[8 * j : 8 * j + 8, lanes] for j in range(3)]
            k3 = [jnp.where(wide(d3[8 * j : 8 * j + 8]) >= 1.0, 1.0 - g3[j], 0.0) for j in range(3)]
            acc2, c2 = acc_ref[:, lanes], c2_ref[:, lanes]
            acc1, c1 = sg_head[8:16, lanes] + k3[2] * acc2, k3[2] * c2
            acc0, c0 = sg_head[0:8, lanes] + k3[1] * acc1, k3[1] * c1
            ba_ref[0:8, lanes] = k3[0] * acc0
            ba_ref[8:16, lanes] = carry[here.mp, 8:16, lanes]
            parts = [g3[0] * acc0, g3[1] * acc1, g3[2] * acc2, g3[0] * c0, g3[1] * c1, g3[2] * c2]
            for j in range(0, 6, 2):
                msg_ref[8 * j : 8 * j + 16, lanes] = jnp.concatenate(parts[j : j + 2], axis=0).astype(BF16)

        def out_copy(s):
            return pltpu.make_async_copy(stage.at[s % 2], f_out.at[s], st_sem.at[s % 2])

        for s in range(n_mp):
            if s >= 2:
                out_copy(s - 2).wait()
            for k, (acc, local) in enumerate(((dwu, local_f), (dwd, local_f), (dwo, local_c))):
                stage[s % 2, :, k * local_f : k * local_f + local] = acc[:, s * local : (s + 1) * local].astype(BF16)

            out_copy(s).start()
        for s in (n_mp - 2, n_mp - 1):
            out_copy(s).wait()


class Reduce:
    def __init__(self, here, other_half, own_half, r1, r2, r3, line_slot, da, send, recv):
        self.h, self.other_half, self.own_half = here, other_half, own_half
        self.r1, self.r2, self.r3, self.line_slot, self.da, self.send, self.recv = r1, r2, r3, line_slot, da, send, recv
        self.quarter = r2.shape[1]

    def copy(self, k):
        h, n = self.h, self.quarter
        if k == 0:
            src, dst, device = self.other_half(), self.r1, h.twin()
        elif k == 1:
            src, dst, device = self.r1.at[:, pl.ds(pl.multiple_of((1 - h.y) * n, n), n)], self.r2, h.beside()
        elif k == 2:
            src, dst, device = self.r2.at[1 - h.b], self.r3, h.pair()
        else:
            src, dst, device = self.r3, self.line_slot, h.line(self.da)
        return remote(src, dst, self.send.at[k], self.recv.at[k], device)

    def add(self, dst, src, rows, shift=0):
        step = 32

        @pl.loop(0, rows // step)
        def _(i):
            at = pl.ds(pl.multiple_of(i * step, step), step)
            dst[at] = (dst[at].astype(F32) + src[pl.ds(pl.multiple_of(shift + i * step, step), step)].astype(F32)).astype(BF16)

    def step1(self):
        self.copy(0).start()

    def step2(self):
        self.copy(0).wait_recv()
        for s in range(2):
            self.add(self.r1.at[s], self.own_half().at[s], 2 * self.quarter)
        self.copy(1).start()

    def step3(self):
        self.copy(1).wait_recv()
        for s in range(2):
            self.add(self.r2.at[s], self.r1.at[s], self.quarter, self.h.y * self.quarter)
        self.copy(2).start()

    def step4(self):
        self.copy(2).wait_recv()
        self.add(self.r3, self.r2.at[self.h.b], self.quarter)
        if self.da:
            self.copy(3).start()

    def close(self):
        for k in range(4 if self.da else 3):
            self.copy(k).wait_send()


class Finish:
    def __init__(self, here, units, slots, groups, whole_sum, send, recv):
        self.h, self.units, self.slots, self.groups, self.whole, self.send, self.recv = here, units, slots, groups, whole_sum, send, recv
        self.n = units[0].quarter

    def rows(self, q):
        return self.whole.at[pl.ds(pl.multiple_of(q * self.n, self.n), self.n)]

    def copy(self, k):
        h = self.h
        part = self.rows(h.q)
        return remote(part, part, self.send.at[k], self.recv.at[k], (h.twin(), h.beside(), h.across())[k])

    def group_copy(self, k):
        h = self.h
        mine = h.dp // 4
        block = self.groups.at[mine]
        device = (lax.rem(h.dp + 4 * k, h.n_dp), h.mp)
        return remote(block, block, self.send.at[2 + k], self.recv.at[2 + k], device)

    def sum_line(self):
        h = self.h
        n_groups = h.n_dp // 4
        for unit in self.units:
            if unit.da:
                unit.copy(3).wait_recv()
        step = 32
        dst = self.rows(h.q) if n_groups == 1 else self.groups.at[h.dp // 4]
        own = self.units[-1].r3

        @pl.loop(0, self.n // step)
        def _(i):
            at = pl.ds(pl.multiple_of(i * step, step), step)
            total = own[at].astype(F32)
            for k in range(h.n_a - 1):
                total = total + self.slots[k, at].astype(F32)
            dst[at] = total.astype(BF16)

        if n_groups > 1:
            for k in range(1, n_groups):
                self.group_copy(k).start()
            for k in range(1, n_groups):
                self.group_copy(k).wait_recv()
            mine = self.rows(h.q)

            @pl.loop(0, self.n // step)
            def _(i):
                at = pl.ds(pl.multiple_of(i * step, step), step)
                total = self.groups[0, at].astype(F32)
                for k in range(1, n_groups):
                    total = total + self.groups[k, at].astype(F32)
                mine[at] = total.astype(BF16)

        for k in range(3):
            self.copy(k).start()

    def write(self, out):
        for k in range(3):
            self.copy(k).wait_recv()
        step = 32

        @pl.loop(0, 4 * self.n // step)
        def _(i):
            at = pl.ds(pl.multiple_of(i * step, step), step)
            out[at] = self.whole[at].astype(F32)

    def close(self):
        for k in range(3):
            self.copy(k).wait_send()
        for k in range(1, self.h.n_dp // 4):
            self.group_copy(k).wait_send()


def back_kernel(span, x_ref, small_ref, dgain2_ref, ba_ref, msg_ref, gain_ref, bounds_ref, wv_ref, wg_ref,
                sg_in, g_in, z_in, v_in, rg_in, f_in,
                tg_ref, vg_grad, f_grad, small_grad, gain_grad,
                sgb, gb, zb, vb, vg, gpg, n1t, ngr, dbuf, bar_buf, msg_buf, u0_ref, gn_ref, sm, smr, sm2,
                st, v1, v2, v3, v4, vw, fown, f1, f2, f3, f4, fw, vgroups, fgroups,
                e_send, e_recv, in_sem, own_sem, rg_sem, f_send, f_recv, v_send, v_recv, ff_send, ff_recv, vf_send, vf_recv,
                m_send, m_recv, k_send, k_recv):
    here = Place()
    n_mp, n_a, n_dp = here.n_mp, here.n_a, here.n_dp
    total, dim = x_ref.shape
    width = wv_ref.shape[0]
    local_c = width // n_mp
    tile_c = 2 * local_c
    rows = BP * 8
    blocks = span // BP
    half = dim // 2
    own_rows = pl.ds(pl.multiple_of(here.c * half, half), half)
    other_rows = pl.ds(pl.multiple_of((1 - here.c) * half, half), half)

    def tile_of(t):
        return lax.rem(here.a + 1 + t, n_a)

    def lanes_of(t):
        return pl.ds(pl.multiple_of(tile_of(t) * tile_c, tile_c), tile_c)

    def ba_copy(dm):
        return remote(ba_ref, bar_buf.at[here.mp], e_send.at[dm], e_recv.at[dm], (here.dp, here.mp - dm))

    def msg_copy():
        return remote(msg_ref, msg_buf, e_send.at[0], e_recv.at[0], (here.dp, here.mp - 1))

    def inputs(t):
        slot, lanes = t % 2, lanes_of(t)
        pairs = ((sg_in, sgb), (g_in, gb), (z_in, zb), (v_in, vb))
        return [pltpu.make_async_copy(src.at[:, lanes], dst.at[slot], in_sem.at[slot, k]) for k, (src, dst) in enumerate(pairs)]

    def own_copy(t):
        return pltpu.make_async_copy(f_in.at[pl.ds(pl.multiple_of(2 * tile_of(t), 2), 2), own_rows], fown.at[t], own_sem.at[t])

    rg_copy = pltpu.make_async_copy(rg_in, tg_ref, rg_sem)

    def far(t):
        return (t + 1) % n_a

    f_units = [
        Reduce(here, (lambda t=t: f_in.at[pl.ds(pl.multiple_of(2 * tile_of(t), 2), 2), other_rows]), (lambda t=t: fown.at[t]),
               f1.at[t], f2.at[t], f3.at[t], f4.at[far(t) - 1] if far(t) else None, far(t), f_send.at[t], f_recv.at[t])
        for t in range(n_a)
    ]
    v_units = [
        Reduce(here, (lambda t=t: st.at[t, :, other_rows]), (lambda t=t: st.at[t, :, own_rows]),
               v1.at[t], v2.at[t], v3.at[t], v4.at[far(t) - 1] if far(t) else None, far(t), v_send.at[t], v_recv.at[t])
        for t in range(n_a)
    ]
    f_end = Finish(here, f_units, f4, fgroups, fw, ff_send, ff_recv)
    v_end = Finish(here, v_units, v4, vgroups, vw, vf_send, vf_recv)

    here.barrier()
    for dm in range(1, n_mp):

        @pl.when(here.mp - dm >= 0)
        def _():
            if dm == 1:
                msg_copy().start()
            ba_copy(dm).start()

    for copy in inputs(0):
        copy.start()
    for unit in f_units:
        unit.step1()
    for t in range(n_a):
        own_copy(t).start()
    rg_copy.start()

    sm[...] = jnp.zeros_like(sm)
    gain = gain_ref[...]
    dbuf[...] = dist_of(bounds_ref, here.mp * span, span + 4)

    def unit_of(i):
        x = x_ref[pl.ds(pl.multiple_of(i * rows, rows), rows)].astype(F32)
        inv = lax.rsqrt(jnp.mean(x * x, axis=1, keepdims=True) + NORM_EPS)
        return x * inv, inv

    for i in range(blocks):
        unit, _ = unit_of(i)
        n1t[:, i * rows : (i + 1) * rows] = (unit * gain).astype(BF16).astype(F32).T.astype(BF16)

    for t, unit in enumerate(f_units):
        own_copy(t).wait()
        unit.step2()

    for dm in range(1, n_mp):

        @pl.when(here.mp + dm < n_mp)
        def _():
            if dm == 1:
                msg_copy().wait_recv()
            ba_copy(dm).wait_recv()

    zero = jnp.zeros((8, width), F32)
    last = here.mp >= n_mp - 1
    u_next = lax.fori_loop(0, n_mp - 2 - here.mp, lambda j, u: bar_buf[n_mp - 1 - j, 0:8] + bar_buf[n_mp - 1 - j, 8:16] * u, zero)
    right = jnp.minimum(here.mp + 1, n_mp - 1)
    u0_ref[...] = jnp.where(last, 0.0, bar_buf[right, 0:8] + bar_buf[right, 8:16] * u_next)
    msg = msg_buf[...].astype(F32)
    for j in range(3):
        gn_ref[8 * j : 8 * j + 8] = jnp.where(last, 0.0, msg[8 * j : 8 * j + 8] + msg[24 + 8 * j : 32 + 8 * j] * u_next)

    def tile_pass(t, hook):
        slot, tile, lanes = t % 2, tile_of(t), lanes_of(t)
        for copy in inputs(t):
            copy.wait()
        if t + 1 < n_a:
            for copy in inputs(t + 1):
                copy.start()
        small = jnp.concatenate([small_ref[2 * tile, :, 0:local_c], small_ref[2 * tile + 1, :, 0:local_c]], axis=1)
        taps = [jnp.broadcast_to(small[j : j + 1], (8, tile_c)) for j in range(KW)]

        def body(i, held):
            u, g1, g2, g3 = held[:4]
            sums = list(held[4:])
            base = pl.multiple_of((blocks - 1 - i) * rows, rows)

            @pl.when(i == blocks // 2)
            def _():
                hook()

            def dist(q, least):
                return wide(dbuf[pl.ds(pl.multiple_of(base + 8 * q, 8), 8)], tile_c) >= least

            for p in range(BP - 2, -2, -2):
                pair_at = pl.ds(pl.multiple_of(base + 8 * p, 16), 16)
                vals = vb[slot, pair_at].astype(F32)
                vgs, gpgs = [None, None], [None, None]
                for k in (1, 0):
                    q = p + k
                    at = pl.ds(pl.multiple_of(base + 8 * q, 8), 8)
                    gate = gb[slot, at]
                    carried = sgb[slot, at] + u
                    g0 = carried * gate
                    gp = g0 * zb[slot, at] * (1.0 - gate)
                    u = jnp.where(dist(q, 1.0), carried - g0, 0.0)
                    h1 = jnp.where(dist(q + 1, 1.0), g1, 0.0)
                    h2 = jnp.where(dist(q + 2, 2.0), g2, 0.0)
                    h3 = jnp.where(dist(q + 3, 3.0), g3, 0.0)
                    v = vals[8 * k : 8 * k + 8]
                    vgs[k] = taps[0] * g0 + taps[1] * h1 + taps[2] * h2 + taps[3] * h3
                    gpgs[k] = gp
                    for j, h in enumerate((g0, h1, h2, h3)):
                        sums[j] = sums[j] + v * h
                    sums[KW + 1] = sums[KW + 1] + g0
                    sums[KW] = sums[KW] + gp.astype(BF16).astype(F32)
                    g1, g2, g3 = g0, g1, g2
                vg[pair_at] = jnp.concatenate(vgs, axis=0).astype(BF16)
                gpg[pair_at] = jnp.concatenate(gpgs, axis=0).astype(BF16)
            return (u, g1, g2, g3, *sums)

        start = [u0_ref[:, lanes]] + [gn_ref[8 * j : 8 * j + 8, lanes] for j in range(3)]
        held = lax.fori_loop(0, blocks, body, (*start, *[jnp.zeros((8, tile_c), F32)] * (KW + 2)))
        for j in range(KW + 2):
            sm[j : j + 1, lanes] = jnp.sum(held[4 + j], axis=0, keepdims=True)
        dv = dot(n1t[...], vg[...]).astype(BF16)
        dg = dot(n1t[...], gpg[...]).astype(BF16)
        for s in range(2):
            cols = slice(s * local_c, (s + 1) * local_c)
            st[t, s] = jnp.concatenate([dv[:, cols], dg[:, cols]], axis=1)
        v_units[t].step1()
        wv_t = wv_ref[pl.ds(pl.multiple_of(tile * tile_c, tile_c), tile_c)]
        wg_t = wg_ref[pl.ds(pl.multiple_of(tile * tile_c, tile_c), tile_c)]

        @pl.loop(0, blocks)
        def _(i):
            at = pl.ds(pl.multiple_of(i * rows, rows), rows)
            ngrad = dot(vg[at], wv_t) + dot(gpg[at], wg_t)
            if t > 0:
                ngrad = ngrad + ngr[at]
            if t < n_a - 1:
                ngr[at] = ngrad
            else:
                unit, inv = unit_of(i)
                weighted = ngrad * gain
                inner = jnp.mean(weighted * unit, axis=1, keepdims=True)
                tg_ref[at] = tg_ref[at] + inv * (weighted - unit * inner)
                part = jnp.sum((ngrad * unit).reshape(BP, 8, -1), axis=0)
                ngr[0:8] = jnp.where(i == 0, part, ngr[0:8] + part)

    stages = [[] for _ in range(2 * n_a)]
    def later(at, action):
        stages[min(at, 2 * n_a - 1)].append(action)

    for t in range(n_a):
        later(2 * t, f_units[t].step3)
        later(2 * t + 2, f_units[t].step4)
        later(2 * t + 2, v_units[t].step2)
        later(2 * t + 3, v_units[t].step3)
        later(2 * t + 4, v_units[t].step4)

    def run(k):
        for action in stages[k]:
            action()

    for t in range(n_a):
        if t == n_a - 1:
            rg_copy.wait()
        tile_pass(t, functools.partial(run, 2 * t))
        if t < n_a - 1:
            run(2 * t + 1)

    for k, g in enumerate((ngr[0:8], dgain2_ref[...])):
        row = jnp.sum(g, axis=0, keepdims=True)
        for j in range(dim // 128):
            at = k * (dim // 128) + j
            sm[at : at + 1, width : width + 128] = row[:, j * 128 : (j + 1) * 128]

    def sm_copy(k):
        return remote(sm, smr.at[here.dp], m_send.at[k], m_recv.at[k], (lax.rem(here.dp + k, n_dp), here.mp))

    for k in range(1, n_dp):
        sm_copy(k).start()
    smr[here.dp] = sm[...]
    for action in stages[2 * n_a - 1][:-1]:
        action()
    for k in range(1, n_dp):
        sm_copy(k).wait()
    sm_sum = smr[0]
    for k in range(1, n_dp):
        sm_sum = sm_sum + smr[k]
    sm[...] = sm_sum

    def tile_copies(dm):
        tile = lax.rem(here.mp + dm, n_mp) // 2
        lanes = pl.ds(pl.multiple_of(tile * tile_c, tile_c), tile_c)
        device = here.other(dm)
        return [remote(sm.at[:, lanes], sm2.at[here.mp, :, pl.ds(0, tile_c)], k_send.at[0, dm], k_recv.at[0, dm], device),
                remote(sm.at[:, pl.ds(width, 128)], sm2.at[here.mp, :, pl.ds(tile_c, 128)], k_send.at[1, dm], k_recv.at[1, dm], device)]

    for dm in range(1, n_mp):
        for copy in tile_copies(dm):
            copy.start()
    f_end.sum_line()
    stages[2 * n_a - 1][-1]()
    v_end.sum_line()
    own_lanes = pl.ds(pl.multiple_of(here.a * tile_c, tile_c), tile_c)
    sm2[here.mp] = jnp.concatenate([sm[:, own_lanes], sm[:, width : width + 128]], axis=1)
    for dm in range(1, n_mp):
        for copy in tile_copies(dm):
            copy.wait_recv()
    last_sum = sm2[0]
    for m in range(1, n_mp):
        last_sum = last_sum + sm2[m]
    small_grad[...] = last_sum[:, 0:tile_c]
    gain_grad[...] = last_sum[:, tile_c : tile_c + 128]
    f_end.write(f_grad)
    v_end.write(vg_grad)

    for unit in f_units + v_units + [f_end, v_end]:
        unit.close()
    for dm in range(1, n_mp):
        for copy in tile_copies(dm):
            copy.wait_send()

        @pl.when(here.mp - dm >= 0)
        def _():
            if dm == 1:
                msg_copy().wait_send()
            ba_copy(dm).wait_send()


def whole(shape):
    return pl.BlockSpec(shape, lambda i: (0,) * len(shape))


def resident(shape):
    return pl.BlockSpec(shape, lambda i: (0,) * len(shape), pipeline_mode=pl.Buffered(1))


def per_device(tokens, lengths, cotangent, norm1_gain, value_proj, gate_proj, gate_bias, conv_taps, conv_bias, out_proj,
               norm2_gain, up_proj, down_proj):
    rows, span, dim = tokens.shape
    n_mp = lax.axis_size("mp")
    n_a = n_mp // 2
    me = lax.axis_index("mp")
    total = rows * span
    blocks = span // BP
    tile = BP * 8
    local_c, local_f = value_proj.shape[1], up_proj.shape[1]
    width, units = local_c * n_mp, local_f * n_mp

    bounds = [lengths[:, 0]]
    for s in range(1, lengths.shape[1]):
        bounds.append(bounds[-1] + lengths[:, s])
    bounds = jnp.broadcast_to(jnp.stack(bounds, 0).astype(F32)[:, :, None], (lengths.shape[1], rows, 128))

    def time_major(a):
        return jnp.transpose(a, (1, 0, 2)).reshape(-1, a.shape[2])

    def row_major(a):
        return jnp.transpose(a.reshape(span, rows, dim), (1, 0, 2))

    x_tm, cot_tm = time_major(tokens), time_major(cotangent)
    pad_c, pad_f = max(local_c, 128), max(local_f, 128)
    small = jnp.concatenate([conv_taps, gate_bias[None], conv_bias[None], jnp.zeros((2, local_c), F32)], axis=0)
    small = jnp.pad(small, ((0, 0), (0, pad_c - local_c)))
    gain1, gain2 = norm1_gain.astype(F32)[None], norm2_gain.astype(F32)[None]

    def late(w):
        return pl.BlockSpec((tile, w), lambda i: (jnp.maximum(i - n_a, 0), 0))

    def rblk(w):
        return pl.BlockSpec((tile, w), lambda i: (blocks - 1 - i, 0))

    def sds(shape, t=F32):
        return jax.ShapeDtypeStruct(shape, t)

    dma = pltpu.SemaphoreType.DMA
    vmem = pltpu.VMEM
    tile_c = 2 * local_c
    pad = -(-(2 * local_f + local_c) // 128) * 128
    out_tm, sg, rg, dgain2, ba, msg, smalls, gate, z, vals, wv, wg, f_grads = pl.pallas_call(
        functools.partial(front_kernel, span),
        grid=(n_a + blocks,),
        in_specs=[resident((total, dim)), late(dim), resident(value_proj.shape), resident(gate_proj.shape), resident(out_proj.shape),
                  resident(up_proj.shape), resident(down_proj.shape), resident(small.shape), resident((1, dim)), resident((1, dim)),
                  resident(bounds.shape)],
        out_specs=[late(dim), late(width), late(dim), resident((8, dim)), resident((16, width)), resident((48, width)),
                   resident((n_mp, 8, pad_c)), ANY, ANY, ANY, ANY, ANY, ANY],
        out_shape=[sds((total, dim), BF16), sds((total, width)), sds((total, dim)), sds((8, dim)), sds((16, width)), sds((48, width), BF16),
                   sds((n_mp, 8, pad_c)), sds((total, width)), sds((total, width)), sds((total, width), BF16),
                   sds((width, dim), BF16), sds((width, dim), BF16), sds((n_mp, dim, pad), BF16)],
        scratch_shapes=[
            vmem((3 * width + 2 * units, dim), BF16), vmem((total + 32, dim), BF16), vmem((total, width), F32), vmem((total, width), F32),
            vmem((total, width), BF16), vmem((tile + 32, tile_c), F32), vmem((tile, tile_c), F32), vmem((tile, 128), F32),
            vmem((n_mp, 8, pad_c), F32), vmem((32, dim), BF16), vmem((n_mp, 16, width), F32), vmem((8, width), F32),
            vmem((8, width), F32), vmem((8, width), F32), vmem((16, width), F32),
            vmem((tile, width), BF16), vmem((tile, FT), F32), vmem((tile, FT), F32), vmem((tile, units), BF16), vmem((tile, units), BF16),
            vmem((dim, width), F32), vmem((dim, units), F32), vmem((dim, units), F32), vmem((2, dim, pad), BF16),
            dma((5, 8 * n_a)), dma((5, 8 * n_a)), dma((n_mp,)), dma((n_mp,)), dma((2,)), dma((n_mp, n_a)), dma((n_mp, n_a)), dma((4,)),
            dma((blocks,)), dma((2,)),
        ],
        compiler_params=pltpu.CompilerParams(collective_id=0, has_side_effects=True, vmem_limit_bytes=60 * MIB),
        name="front",
    )(x_tm, cot_tm, value_proj, gate_proj, out_proj, up_proj, down_proj, small, gain1, gain2, bounds)

    n_dp = lax.axis_size("dp")
    groups = n_dp // 4
    full = pl.BlockSpec(memory_space=pltpu.VMEM)
    half, quarter = dim // 2, dim // 4

    def buffers(w):
        return [vmem((n_a, 2, half, w), BF16), vmem((n_a, 2, quarter, w), BF16), vmem((n_a, quarter, w), BF16),
                vmem((n_a - 1, quarter, w), BF16), vmem((dim, w), BF16)]

    tg_tm, vg_grad, f_grad, small_grad, gain_grad = pl.pallas_call(
        functools.partial(back_kernel, span),
        in_specs=[full] * 9 + [ANY] * 6,
        out_specs=[full] * 5,
        out_shape=[sds((total, dim)), sds((dim, tile_c)), sds((dim, pad)), sds((8, tile_c)), sds((8, 128))],
        scratch_shapes=[
            vmem((2, total, tile_c), F32), vmem((2, total, tile_c), F32), vmem((2, total, tile_c), F32), vmem((2, total, tile_c), BF16),
            vmem((total, tile_c), BF16), vmem((total, tile_c), BF16), vmem((dim, total), BF16), vmem((total, dim), F32),
            vmem((total + 32, 128), F32), vmem((n_mp, 16, width), F32), vmem((48, width), BF16), vmem((8, width), F32),
            vmem((24, width), F32), vmem((8, width + 128), F32), vmem((n_dp, 8, width + 128), F32), vmem((n_mp, 8, tile_c + 128), F32),
            vmem((n_a, 2, dim, tile_c), BF16), *buffers(tile_c), vmem((n_a, 2, half, pad), BF16), *buffers(pad),
            vmem((groups, quarter, tile_c), BF16), vmem((groups, quarter, pad), BF16),
            dma((n_mp,)), dma((n_mp,)), dma((2, 4)), dma((n_a,)), dma, dma((n_a, 4)), dma((n_a, 4)), dma((n_a, 4)), dma((n_a, 4)),
            dma((2 + groups,)), dma((2 + groups,)), dma((2 + groups,)), dma((2 + groups,)), dma((n_dp,)), dma((n_dp,)),
            dma((2, n_mp)), dma((2, n_mp)),
        ],
        compiler_params=pltpu.CompilerParams(collective_id=1, has_side_effects=True, vmem_limit_bytes=60 * MIB),
        name="back",
    )(x_tm, smalls, dgain2, ba, msg, gain1, bounds, wv, wg, sg, gate, z, vals, rg, f_grads)

    gains = gain_grad.reshape(2, dim)
    mine = lax.dynamic_slice_in_dim(small_grad, (me % 2) * local_c, local_c, 1)
    return (
        row_major(out_tm),
        row_major(tg_tm),
        gains[0],
        vg_grad[:, :local_c],
        vg_grad[:, local_c : 2 * local_c],
        mine[KW],
        mine[:KW],
        mine[KW + 1],
        f_grad[:, 2 * local_f : 2 * local_f + local_c].T,
        gains[1],
        f_grad[:, :local_f],
        f_grad[:, local_f : 2 * local_f].T,
    )


def solution(mesh):
    in_specs = (
        P("dp", "mp", None),
        P("dp", None),
        P("dp", "mp", None),
        P(),
        P(None, "mp"),
        P(None, "mp"),
        P("mp"),
        P(None, "mp"),
        P("mp"),
        P("mp", None),
        P(),
        P(None, "mp"),
        P("mp", None),
    )
    out_specs = (
        P("dp", "mp", None),
        P("dp", "mp", None),
        P(),
        P(None, "mp"),
        P(None, "mp"),
        P("mp"),
        P(None, "mp"),
        P("mp"),
        P("mp", None),
        P(),
        P(None, "mp"),
        P("mp", None),
    )
    return jax.shard_map(per_device, mesh=mesh, in_specs=in_specs, out_specs=out_specs, check_vma=False)
```

```python
import functools

import jax
import jax.numpy as jnp
from jax import lax
from jax.experimental import pallas as pl
from jax.experimental.pallas import tpu as pltpu
from jax.sharding import PartitionSpec as P

KW = 4
NORM_EPS = 1e-06
BP = 32
CT = 256
FT = 512
MIB = 2**20
F32 = jnp.float32
BF16 = jnp.bfloat16
MESH = pl.DeviceIdType.MESH
ANY = pl.BlockSpec(memory_space=pl.ANY)

ERF_A = (0.254829592, -0.284496736, 1.421413741, -1.453152027, 1.061405429)
ERF_P = 0.3275911 * 0.7071067811865476
INV_ROOT_TWO_PI = 0.3989422804014327


def gelu_parts(x):
    t = 1.0 / (1.0 + ERF_P * jnp.abs(x))
    e = jnp.exp(-0.5 * (x * x))
    poly = 0.5 * ERF_A[4]
    for a in (ERF_A[3], ERF_A[2], ERF_A[1], ERF_A[0]):
        poly = poly * t + 0.5 * a
    tail = poly * t * e
    cdf = jnp.where(x >= 0, 1.0 - tail, tail)
    return x * cdf, cdf + x * (e * INV_ROOT_TWO_PI)


def dist_of(bounds_ref, first, count):
    place = (lax.broadcasted_iota(jnp.int32, (count, 8, 128), 0) + first).astype(F32)
    start = jnp.zeros((count, 8, 128), F32)
    for s in range(bounds_ref.shape[0]):
        b = bounds_ref[s][None]
        start = jnp.where(b <= place, jnp.maximum(start, b), start)
    return (place - start).reshape(count * 8, 128)


def wide(d, width=CT):
    return jnp.concatenate([d] * (width // 128), axis=1)


def dot(a, b):
    return jnp.dot(a, b, preferred_element_type=F32)


def dot_nt(a, b):
    return lax.dot_general(a, b, (((1,), (1,)), ((), ())), preferred_element_type=F32)


def dot_tn(a, b):
    return lax.dot_general(a, b, (((0,), (0,)), ((), ())), preferred_element_type=F32)


class Place:
    def __init__(self):
        self.n_mp, self.n_dp = lax.axis_size("mp"), lax.axis_size("dp")
        self.n_a = self.n_mp // 2
        self.dp, self.mp = lax.axis_index("dp"), lax.axis_index("mp")
        self.a, self.b = self.mp // 2, self.mp % 2
        self.y, self.c = (self.dp // 2) % 2, self.dp % 2
        self.base = self.dp - self.y * 2 - self.c
        self.q = self.c * 2 + self.y

    def line(self, da):
        return (self.dp, (self.a ^ da) * 2 + self.b)

    def diagonal(self, da):
        return (self.dp, (self.a ^ da) * 2 + 1 - self.b)

    def pair(self):
        return (self.dp, self.a * 2 + 1 - self.b)

    def beside(self):
        return (self.base + (1 - self.y) * 2 + self.c, self.mp)

    def twin(self):
        return (self.base + self.y * 2 + 1 - self.c, self.mp)

    def across(self):
        return (self.base + (1 - self.y) * 2 + 1 - self.c, self.mp)

    def other(self, dm):
        return (self.dp, lax.rem(self.mp + dm, self.n_mp))

    def partners(self):
        group = [(lax.rem(self.dp + k, self.n_dp), self.mp) for k in range(1, self.n_dp)]
        return group + [self.other(dm) for dm in range(1, self.n_mp)]

    def greet(self):
        for d in self.partners():
            pl.semaphore_signal(pltpu.get_barrier_semaphore(), inc=1, device_id=d, device_id_type=MESH)

    def await_all(self):
        pl.semaphore_wait(pltpu.get_barrier_semaphore(), len(self.partners()))


def remote(src, dst, send, recv, device):
    return pltpu.make_async_remote_copy(src_ref=src, dst_ref=dst, send_sem=send, recv_sem=recv, device_id=device, device_id_type=MESH)


class Gather:
    def __init__(self, here, wall, first, rows, send, recv, direct=False, routed=False):
        self.direct = direct
        self.routed = routed
        self.h, self.wall, self.first, self.rows, self.send, self.recv = here, wall, first, rows, send, recv
        n_a = here.n_a
        self.z0, self.x0, self.y0, self.t0 = 0, n_a, 2 * n_a, 4 * n_a
        self.used = []

    def span(self, shard, q, count=1):
        n = self.rows // 4
        return self.wall.at[pl.ds(pl.multiple_of(self.first + shard * self.rows + q * n, 16), count * n)]

    def move(self, sem, shard, q, device, count=1):
        s = self.span(shard, q, count)
        remote(s, s, self.send.at[sem], self.recv.at[sem], device).start()
        self.used.append((sem, count))

    def landed(self, sem, shard, q, count=1):
        s = self.span(shard, q, count)
        remote(s, s, self.send.at[sem], self.recv.at[sem], self.h.pair()).wait_recv()

    def shard(self, da, other):
        h = self.h
        return (h.a ^ da) * 2 + ((1 - h.b) if other else h.b)

    def slot(self, da, other):
        return 2 * da + (1 if other else 0)

    def open(self):
        h = self.h
        self.move(self.x0, h.mp, h.q, h.pair())
        for da in range(1, h.n_a):
            if self.direct:
                self.move(self.z0 + da, h.mp, 2 * h.c, h.line(da), 2)
            else:
                self.move(self.z0 + da, h.mp, h.q, h.line(da))
            if self.routed:
                self.move(self.x0 + da, h.mp, h.q, h.diagonal(da))

    def spread(self, da, other):
        h, s = self.h, self.shard(da, other)
        self.move(self.y0 + self.slot(da, other), s, h.q, h.beside())
        self.move(self.t0 + 2 * self.slot(da, other), s, h.q, h.twin())

    def from_line(self, da):
        h, s = self.h, self.shard(da, False)
        if self.direct:
            self.landed(self.z0 + da, s, 2 * h.c, 2)
            self.move(self.x0 + da, s, h.q, h.pair())
            self.move(self.t0 + 2 * self.slot(da, False), s, 2 * h.c, h.twin(), 2)
        else:
            self.landed(self.z0 + da, s, h.q)
            if not self.routed:
                self.move(self.x0 + da, s, h.q, h.pair())
            self.spread(da, False)

    def from_pair(self, da):
        self.landed(self.x0 + da, self.shard(da, True), self.h.q)
        self.spread(da, True)

    def from_beside(self, da, other):
        if self.direct and not other:
            return
        h, s = self.h, self.shard(da, other)
        q = h.c * 2 + 1 - h.y
        self.landed(self.y0 + self.slot(da, other), s, q)
        self.move(self.t0 + 2 * self.slot(da, other) + 1, s, q, h.twin())

    def from_twin(self, da, other):
        h, s = self.h, self.shard(da, other)
        if self.direct and not other:
            self.landed(self.t0 + 2 * self.slot(da, other), s, 2 * (1 - h.c), 2)
            return
        self.landed(self.t0 + 2 * self.slot(da, other), s, (1 - h.c) * 2 + h.y)
        self.landed(self.t0 + 2 * self.slot(da, other) + 1, s, (1 - h.c) * 2 + 1 - h.y)

    def close(self):
        for sem, count in self.used:
            s = self.wall.at[pl.ds(self.first, count * self.rows // 4)]
            remote(s, s, self.send.at[sem], self.recv.at[sem], self.h.pair()).wait_send()


class Reduce:
    def __init__(self, here, other_half, own_half, r1, r2, r3, line_slot, da, send, recv, pair_first=False):
        self.h, self.other_half, self.own_half, self.pair_first = here, other_half, own_half, pair_first
        self.r1, self.r2, self.r3, self.line_slot, self.da, self.send, self.recv = r1, r2, r3, line_slot, da, send, recv
        self.quarter = r2.shape[1]

    def copy(self, k):
        h = self.h
        if k == 0:
            src, dst, device = self.other_half(), self.r1, h.twin()
        elif k == 1 and self.pair_first:
            src, dst, device = self.r1.at[1 - h.b], self.r2, h.pair()
        elif k == 1:
            src, dst, device = self.r1.at[:, 1 - h.y], self.r2, h.beside()
        elif k == 2 and self.pair_first:
            src, dst, device = self.r2.at[1 - h.y], self.r3, h.beside()
        elif k == 2:
            src, dst, device = self.r2.at[1 - h.b], self.r3, h.pair()
        else:
            src, dst, device = self.r3, self.line_slot, h.line(self.da)
        return remote(src, dst, self.send.at[k], self.recv.at[k], device)

    def add(self, dst, src):
        step = 32

        @pl.loop(0, self.quarter // step)
        def _(i):
            at = pl.ds(pl.multiple_of(i * step, step), step)
            dst[at] = (dst[at].astype(F32) + src[at].astype(F32)).astype(BF16)

    def step1(self):
        self.copy(0).start()

    def step2(self):
        self.copy(0).wait_recv()
        own = self.own_half()
        for s in range(2):
            for y in range(2):
                self.add(self.r1.at[s, y], own.at[s, y])
        self.copy(1).start()

    def step3(self):
        self.copy(1).wait_recv()
        for s in range(2):
            self.add(self.r2.at[s], self.r1.at[self.h.b, s] if self.pair_first else self.r1.at[s, self.h.y])
        self.copy(2).start()

    def step4(self):
        self.copy(2).wait_recv()
        self.add(self.r3, self.r2.at[self.h.y if self.pair_first else self.h.b])
        if self.da:
            self.copy(3).start()

    def close(self):
        for k in range(4 if self.da else 3):
            self.copy(k).wait_send()


class Finish:
    def __init__(self, here, units, slots, groups, whole_sum, send, recv):
        self.h, self.units, self.slots, self.groups, self.whole, self.send, self.recv = here, units, slots, groups, whole_sum, send, recv
        self.n = units[0].quarter

    def rows(self, q):
        return self.whole.at[pl.ds(pl.multiple_of(q * self.n, self.n), self.n)]

    def copy(self, k):
        h = self.h
        part = self.rows(h.q)
        return remote(part, part, self.send.at[k], self.recv.at[k], (h.twin(), h.beside(), h.across())[k])

    def group_copy(self, k):
        h = self.h
        mine = h.dp // 4
        block = self.groups.at[mine]
        device = (lax.rem(h.dp + 4 * k, h.n_dp), h.mp)
        return remote(block, block, self.send.at[2 + k], self.recv.at[2 + k], device)

    def sum_line(self):
        h = self.h
        n_groups = h.n_dp // 4
        for unit in self.units:
            if unit.da:
                unit.copy(3).wait_recv()
        step = 32
        dst = self.rows(h.q) if n_groups == 1 else self.groups.at[h.dp // 4]
        own = self.units[-1].r3

        @pl.loop(0, self.n // step)
        def _(i):
            at = pl.ds(pl.multiple_of(i * step, step), step)
            total = own[at].astype(F32)
            for k in range(h.n_a - 1):
                total = total + self.slots[k, at].astype(F32)
            dst[at] = total.astype(BF16)

        if n_groups > 1:
            for k in range(1, n_groups):
                self.group_copy(k).start()
            for k in range(1, n_groups):
                self.group_copy(k).wait_recv()
            mine = self.rows(h.q)

            @pl.loop(0, self.n // step)
            def _(i):
                at = pl.ds(pl.multiple_of(i * step, step), step)
                total = self.groups[0, at].astype(F32)
                for k in range(1, n_groups):
                    total = total + self.groups[k, at].astype(F32)
                mine[at] = total.astype(BF16)

        for k in range(3):
            self.copy(k).start()

    def write(self, out):
        for k in range(3):
            self.copy(k).wait_recv()
        step = 32

        @pl.loop(0, 4 * self.n // step)
        def _(i):
            at = pl.ds(pl.multiple_of(i * step, step), step)
            out[at] = self.whole[at].astype(F32)

    def close(self):
        for k in range(3):
            self.copy(k).wait_send()
        for k in range(1, self.h.n_dp // 4):
            self.group_copy(k).wait_send()


def fill_bounds(bounds_ref, len_in):
    diagonal = lax.broadcasted_iota(jnp.int32, (8, 8), 0) == lax.broadcasted_iota(jnp.int32, (8, 8), 1)
    end = jnp.zeros((8, 1), F32)
    for s in range(bounds_ref.shape[0]):
        end = end + jnp.sum(jnp.where(diagonal, len_in[s : s + 1].astype(F32), 0.0), axis=1, keepdims=True)
        bounds_ref[s] = jnp.broadcast_to(end, (8, 128))


def to_time_major(parts):
    block = jnp.stack([p.astype(F32) for p in parts], axis=0)
    return jnp.swapaxes(block, 0, 1).reshape(-1, block.shape[-1])


def to_row_major(block):
    return jnp.swapaxes(block.reshape(-1, 8, block.shape[-1]), 0, 1)


def front_kernel(span, cot_ref, wv_in, wg_in, wo_in, wu_in, wd_in, taps_in, gb_in, cb_in, gain_in, len_in, x_in,
                 out_ref, dgain_ref, b_ref, msg_ref, a_out, small_out, h_grad, x_out, g_out, z_out, v_out, sg_out, rg_out, wv_out, wg_out,
                 f_out,
                 wall, x_tm, nbuf, gsc, msc, vsc, rbuf, ngp, vbuf, gbuf, dbuf, smalls, halo, carry, state_ref, acc_ref, c2_ref,
                 sg_head, bounds_ref, gain1_ref, gain2_ref, hp, dh, hb, hg, dwo, du, dd, stage, st, r1, r2, r3, r4, rw, rgroups,
                 w_send, w_recv, s_send, s_recv, h_sem, c_send, c_recv, l_sem, t_sem, z_sem, sg_sem, rg_sem, st_sem, x_sem,
                 r_send, r_recv, e_send, e_recv, d_send, d_recv):
    here = Place()
    n_mp, n_a = here.n_mp, here.n_a
    dim = x_tm.shape[1]
    local_c, local_h = wv_in.shape[1], wu_in.shape[1] // 2
    width, units = local_c * n_mp, local_h * n_mp
    tile_c = 2 * local_c
    rows = BP * 8
    blocks = span // BP
    step = pl.program_id(0)
    sections, first = {}, 0
    for k, (name, count) in enumerate((("wu1", local_h), ("wd1", local_h), ("wu2", local_h), ("wd2", local_h),
                                       ("wv", local_c), ("wg", local_c), ("wo", local_c))):
        sections[name] = Gather(here, wall, first, count, w_send.at[k], w_recv.at[k], routed=name == "wo")
        first += count * n_mp
    wv, wg, wo = (sections[name] for name in ("wv", "wg", "wo"))
    ffn1, ffn2 = [sections["wu1"], sections["wd1"]], [sections["wu2"], sections["wd2"]]
    far = range(1, n_a)

    def tile_of(da):
        return here.a ^ da

    def lanes_of(t):
        return pl.ds(pl.multiple_of(tile_of(t) * tile_c, tile_c), tile_c)

    def small_copy(dm):
        return remote(smalls.at[here.mp], smalls.at[here.mp], s_send.at[dm], s_recv.at[dm], here.other(dm))

    def halo_copy():
        return remote(x_tm.at[pl.ds(span * 8 - 32, 32)], halo, h_sem.at[0], h_sem.at[1], here.other(1))

    def carry_copy(dm, t):
        block = carry.at[here.mp, :, lanes_of(t)]
        return remote(block, block, c_send.at[dm, t], c_recv.at[dm, t], (here.dp, here.mp + dm))

    def decay_copy(dm):
        block = carry.at[here.mp, 8:16]
        return remote(block, block, d_send.at[dm], d_recv.at[dm], (here.dp, here.mp - dm))

    def raw_copies():
        return [pltpu.make_async_copy(x_in.at[r], vsc.at[pl.ds(r * span, span), pl.ds(0, dim)], x_sem.at[r]) for r in range(8)]

    def tile_copies(t):
        lanes = lanes_of(t)
        return [pltpu.make_async_copy(gsc.at[:, lanes], g_out.at[:, lanes], t_sem.at[0, t]),
                pltpu.make_async_copy(vsc.at[:, lanes], v_out.at[:, lanes], t_sem.at[1, t])]

    def weight_copies():
        return [pltpu.make_async_copy(wall.at[pl.ds(s.first, width)], o, l_sem.at[1 + i]) for i, (s, o) in enumerate(((wv, wv_out), (wg, wg_out)))]

    def x_copy():
        return pltpu.make_async_copy(x_tm, x_out, l_sem.at[0])

    def block_copy(src, dst, sem, i):
        at = pl.ds(pl.multiple_of(i * rows, rows), rows)
        return pltpu.make_async_copy(src.at[at], dst.at[at], sem.at[i])

    z_copy = functools.partial(block_copy, msc, z_out, z_sem)
    sg_copy = functools.partial(block_copy, msc, sg_out, sg_sem)
    rg_copy = functools.partial(block_copy, ngp, rg_out, rg_sem)

    own_rows, other_rows = pl.ds(2 * here.c, 2), pl.ds(2 * (1 - here.c), 2)

    def shards(t):
        return pl.ds(pl.multiple_of(2 * (here.a ^ further(t)), 2), 2)

    def further(t):
        return (t + 1) % n_a

    h_units = [
        Reduce(here, (lambda t=t: st.at[shards(t), other_rows]), (lambda t=t: st.at[shards(t), own_rows]),
               r1.at[t], r2.at[t], r3.at[t], r4.at[further(t) - 1] if further(t) else None, further(t), r_send.at[t], r_recv.at[t], t % 2 == 1)
        for t in range(n_a)
    ]
    h_end = Finish(here, h_units, r4, rgroups, rw, e_send, e_recv)

    parts = min(4, blocks)
    moves = [[[] for _ in range(n_a)] for _ in range(parts)]

    def plan(t, i, *actions):
        moves[min(i, parts - 1)][min(t, n_a - 1)].extend(actions)

    def each(group, method, *args):
        return [functools.partial(getattr(s, method), *args) for s in group]

    mixer = (wv, wg)
    for da in far:
        plan(0, da - 1, *each(mixer, "from_pair", da))
        plan(0, da, *each(mixer, "from_beside", da, False))
        plan(0 if da < 2 else 1, 3 if da < 2 else 2 * da - 4, *each(mixer, "from_beside", da, True))
        plan(1, 1, *each([wo], "from_line", da), *each([wo], "from_pair", da))
        plan(1, 3, *each(ffn1, "from_line", da))
        plan(2, 1, *each([wo], "from_beside", da, False), *each([wo], "from_beside", da, True))
        plan(2, 3, *each(ffn1, "from_pair", da))
        plan(3, 1, *each(ffn1, "from_beside", da, False))
        plan(3, 3, *each(ffn1, "from_beside", da, True))
    plan(0, 1, *each([wo], "open"))
    plan(0, 3, *each(ffn1, "open"))
    plan(1, 1, *each([wo], "from_pair", 0))
    plan(1, 3, *each(ffn1, "from_pair", 0))
    plan(2, 1, *each([wo], "from_beside", 0, True))
    plan(3, 1, *each(ffn1, "from_beside", 0, True))
    plan(3, 3, *each(ffn2, "open"))

    def advance(i):
        for t in range(n_a):
            if moves[i][t]:

                @pl.when(step == t)
                def _():
                    for action in moves[i][t]:
                        action()

    def normed(x):
        inv = lax.rsqrt(jnp.mean(x * x, axis=1, keepdims=True) + NORM_EPS)
        return (x * inv * gain1_ref[...]).astype(BF16)

    @pl.when(step == 0)
    def _():
        for copy in raw_copies():
            copy.start()
        here.greet()
        fill_bounds(bounds_ref, len_in)
        gain1_ref[...] = gain_in[0:1]
        gain2_ref[...] = gain_in[1:2]
        for s, w in ((wv, wv_in), (wg, wg_in)):
            wall[pl.ds(pl.multiple_of(s.first + here.mp * s.rows, 16), s.rows)] = w[...].astype(F32).T.astype(BF16)
        here.await_all()
        wv.open()
        wg.open()
        smalls[here.mp] = jnp.zeros(smalls.shape[1:], F32)
        smalls[here.mp, 0:KW, 0:local_c] = taps_in[...]
        smalls[here.mp, KW : KW + 1, 0:local_c] = gb_in[...]
        smalls[here.mp, KW + 1 : KW + 2, 0:local_c] = cb_in[...]
        for dm in range(1, n_mp):
            small_copy(dm).start()

        def put(s, block):
            wall[pl.ds(pl.multiple_of(s.first + here.mp * s.rows, 16), s.rows)] = block

        put(wo, wo_in[...])
        up = wu_in[...].astype(F32).T.astype(BF16)
        for k, both in enumerate((ffn1, ffn2)):
            put(both[0], up[k * local_h : (k + 1) * local_h])
            put(both[1], wd_in[k * local_h : (k + 1) * local_h])

        def take(i):
            block = to_time_major([vsc[pl.ds(pl.multiple_of(r * span + i * BP, BP), BP), 0:dim] for r in range(8)])
            x_tm[pl.ds(pl.multiple_of(i * rows, rows), rows)] = block.astype(BF16)
            nbuf[pl.ds(pl.multiple_of(32 + i * rows, 16), rows)] = normed(block)

        for copy in raw_copies():
            copy.wait()
        take(blocks - 1)
        halo_copy().start()

        @pl.loop(0, blocks - 1)
        def _(i):
            take(i)

            @pl.when(i == min(2, blocks - 2))
            def _():
                for action in each(mixer, "from_pair", 0):
                    action()

        for action in each(mixer, "from_beside", 0, True):
            action()
        for da in far:
            for action in each(mixer, "from_line", da):
                action()
        x_copy().start()
        halo_copy().wait_recv()
        nbuf[0:32] = normed(halo[...].astype(F32))
        for dm in range(1, n_mp):
            small_copy(dm).wait_recv()

    @pl.when(step < n_a)
    def _():
        for s in (wv, wg):
            s.from_twin(step, True)

            @pl.when(step > 0)
            def _():
                s.from_twin(step, False)

        tile, lanes = tile_of(step), lanes_of(step)
        wv_t = wall[pl.ds(pl.multiple_of(wv.first + tile * tile_c, tile_c), tile_c)]
        wg_t = wall[pl.ds(pl.multiple_of(wg.first + tile * tile_c, tile_c), tile_c)]
        small = jnp.concatenate([smalls[2 * tile, :, 0:local_c], smalls[2 * tile + 1, :, 0:local_c]], axis=1)
        taps = [jnp.broadcast_to(small[j : j + 1], (8, tile_c)) for j in range(KW)]
        bias = jnp.broadcast_to(small[KW : KW + 1], (8, tile_c))
        cb = jnp.broadcast_to(small[KW + 1 : KW + 2], (8, tile_c))
        vbuf[0:32] = dot_nt(nbuf[0:32], wv_t)

        def body(i, held):
            state, decay = held
            at = pl.ds(pl.multiple_of(32 + i * rows, 16), rows)
            vbuf[32 : 32 + rows] = dot_nt(nbuf[at], wv_t)
            gbuf[...] = dot_nt(nbuf[at], wg_t)
            dbuf[0:rows] = dist_of(bounds_ref, here.mp * span + i * BP, BP)
            v1, v2, v3 = vbuf[24:32], vbuf[16:24], vbuf[8:16]
            values = []
            for p in range(BP):
                at = slice(8 * p, 8 * p + 8)
                out_at = pl.ds(pl.multiple_of(i * rows + 8 * p, 8), 8)
                v0 = vbuf[32 + 8 * p : 40 + 8 * p]
                gate = jax.nn.sigmoid(gbuf[at] + bias)
                d = wide(dbuf[at], tile_c)
                mixed = cb + taps[0] * v0
                mixed = mixed + jnp.where(d >= 1.0, taps[1] * v1, 0.0)
                mixed = mixed + jnp.where(d >= 2.0, taps[2] * v2, 0.0)
                mixed = mixed + jnp.where(d >= 3.0, taps[3] * v3, 0.0)
                linked = jnp.where(d >= 1.0, state, 0.0)
                state = linked + gate * (mixed - linked)
                decay = jnp.where(d >= 1.0, decay * (1.0 - gate), 0.0)
                gsc[out_at, lanes] = gate
                msc[out_at, lanes] = mixed
                values.append(v0)
                if p % 2:
                    pair_at = pl.ds(pl.multiple_of(i * rows + 8 * p - 8, 16), 16)
                    vsc[pair_at, lanes] = jnp.concatenate(values, axis=0).astype(BF16)
                    values = []
                v1, v2, v3 = v0, v1, v2
            vbuf[0:32] = vbuf[rows : rows + 32]
            return state, decay

        held = (jnp.zeros((8, tile_c), F32), jnp.ones((8, tile_c), F32))
        for part_no in range(parts):
            held = lax.fori_loop(part_no * blocks // parts, (part_no + 1) * blocks // parts, body, held)
            if part_no < parts - 1:
                advance(part_no)
        state, decay = held
        carry[here.mp, 0:8, lanes] = state
        carry[here.mp, 8:16, lanes] = decay
        for dm in range(1, n_mp):

            @pl.when(here.mp + dm < n_mp)
            def _():
                carry_copy(dm, step).start()

        for copy in tile_copies(step):
            copy.start()
        advance(parts - 1)

        @pl.when(step == n_a - 1)
        def _():
            for dm in range(1, n_mp):

                @pl.when(here.mp - dm >= 0)
                def _():
                    decay_copy(dm).start()

    def from_twin(s):
        s.from_twin(0, True)
        for da in far:
            s.from_twin(da, True)
            s.from_twin(da, False)

    @pl.when(step == n_a)
    def _():
        for copy in weight_copies():
            copy.start()
        for dm in range(1, n_mp):

            @pl.when(here.mp - dm >= 0)
            def _():
                for t in range(n_a):
                    carry_copy(dm, t).wait_recv()

        start = jnp.zeros((8, width), F32)
        state_ref[...] = lax.fori_loop(0, here.mp, lambda i, s: carry[i, 0:8] + carry[i, 8:16] * s, start)
        for s in [wo] + ffn1:
            from_twin(s)
        for t in range(n_a):
            for copy in tile_copies(t):
                copy.wait()
        x_copy().wait()
        halo_copy().wait_send()
        dwo[...] = jnp.zeros_like(dwo)
        du[...] = jnp.zeros_like(du)
        dd[...] = jnp.zeros_like(dd)
        dgain_ref[...] = jnp.zeros_like(dgain_ref)
        acc_ref[...] = jnp.zeros_like(acc_ref)
        c2_ref[...] = jnp.ones_like(c2_ref)
        small_out[...] = smalls[...]

    def part(s, lo=0, hi=None):
        return wall[s.first + lo : s.first + (s.rows * n_mp if hi is None else hi)]

    def inside_of(i):
        place = (lax.broadcasted_iota(jnp.int32, (BP, 8, 128), 0) + (here.mp * span + i * BP)).astype(F32)
        last = bounds_ref.shape[0] - 1
        return jnp.where(place < bounds_ref[last][None], 1.0, 0.0).reshape(rows, 128)[:, 0:1]

    def feed(n2, fg, up, down):
        tile_f = min(FT, units)
        for f in range(0, units, tile_f):
            cols = slice(f, f + tile_f)
            hp[...] = dot_nt(n2, part(up, f, f + tile_f))
            dh[...] = dot_nt(fg, part(down, f, f + tile_f))
            for r in range(0, rows, 16):
                at = slice(r, r + 16)
                hidden, slope = gelu_parts(hp[at])
                hb[at, cols] = hidden.astype(BF16)
                hg[at, cols] = (dh[at] * slope).astype(BF16)
        out, ngrad = dot(hb[...], part(down)), dot(hg[...], part(up))
        dd[...] += dot_tn(fg, hb[...])
        du[...] += dot_tn(n2, hg[...])
        return out, ngrad

    @pl.when((step >= n_a) & (step < n_a + blocks))
    def _():
        i = step - n_a
        base = pl.multiple_of(i * rows, rows)
        dbuf[0:rows] = dist_of(bounds_ref, here.mp * span + i * BP, BP)
        for c in range(0, width, CT):
            lanes = slice(c, c + CT)
            state = state_ref[:, lanes]
            for p in range(0, BP, 2):
                pair = []
                for q in (p, p + 1):
                    at = pl.ds(pl.multiple_of(base + 8 * q, 8), 8)
                    linked = jnp.where(wide(dbuf[8 * q : 8 * q + 8]) >= 1.0, state, 0.0)
                    z = msc[at, lanes] - linked
                    state = linked + gsc[at, lanes] * z
                    msc[at, lanes] = z
                    pair.append(state)
                vsc[pl.ds(pl.multiple_of(base + 8 * p, 16), 16), lanes] = jnp.concatenate(pair, axis=0).astype(BF16)
            state_ref[:, lanes] = state
        z_copy(i).start()
        at = pl.ds(base, rows)
        residual = x_tm[at].astype(F32) + dot(vsc[at], part(wo))
        resid_b = residual.astype(BF16)
        x_tm[at] = resid_b
        resid = resid_b.astype(F32)
        inv = lax.rsqrt(jnp.mean(resid * resid, axis=1, keepdims=True) + NORM_EPS)
        n2 = (resid * inv * gain2_ref[...]).astype(BF16)
        nbuf[pl.ds(pl.multiple_of(32 + base, 16), rows)] = n2
        fg = (to_time_major([cot_ref[r] for r in range(8)]) * inside_of(i)).astype(BF16)
        out, ngrad = feed(n2, fg, *ffn1)
        rbuf[at] = residual + out
        ngp[at] = ngrad

        def when_a(k, *calls):
            @pl.when(i == min(k, blocks - 1))
            def _():
                for method, *args in calls:
                    for action in each(ffn2, method, *args):
                        action()

        when_a(2, ("from_pair", 0), *[("from_line", da) for da in far])
        when_a(4, *[("from_pair", da) for da in far])
        when_a(6, ("from_beside", 0, True), *[("from_beside", da, False) for da in far], *[("from_beside", da, True) for da in far])

    @pl.when(step == n_a + blocks - 1)
    def _():
        for s in range(n_mp):
            cols = slice(s * local_h, (s + 1) * local_h)
            both = jnp.concatenate([du[:, cols].astype(BF16), dd[:, cols].astype(BF16)], axis=1)
            st[s] = both.reshape(st.shape[1:])
        for unit in h_units:
            unit.step1()
        du[...] = jnp.zeros_like(du)
        dd[...] = jnp.zeros_like(dd)
        for s in ffn2:
            from_twin(s)

    @pl.when(step >= n_a + blocks)
    def _():
        i = step - n_a - blocks
        base = pl.multiple_of(i * rows, rows)
        at = pl.ds(base, rows)
        dbuf[0:rows] = dist_of(bounds_ref, here.mp * span + i * BP, BP)
        inside = inside_of(i)
        grad_out = to_time_major([cot_ref[r] for r in range(8)]) * inside
        fg = grad_out.astype(BF16)
        out, ngrad = feed(nbuf[pl.ds(pl.multiple_of(32 + base, 16), rows)], fg, *ffn2)
        out_ref[...] = to_row_major((rbuf[at] + out) * inside).astype(BF16)
        ngrad = ngp[at] + ngrad
        resid = x_tm[at].astype(F32)
        inv = lax.rsqrt(jnp.mean(resid * resid, axis=1, keepdims=True) + NORM_EPS)
        unit = resid * inv
        weighted = ngrad * gain2_ref[...]
        inner = jnp.mean(weighted * unit, axis=1, keepdims=True)
        rgrad = grad_out + inv * (weighted - unit * inner)
        ngp[at] = rgrad
        rg_copy(i).start()
        dgain_ref[...] += jnp.sum((ngrad * unit).reshape(BP, 8, -1), axis=0)
        mix = rgrad.astype(BF16)
        dwo[...] += dot_tn(mix, vsc[at])
        z_copy(i).wait()
        msc[at] = dot_nt(mix, part(wo))
        sg_copy(i).start()

        @pl.when(i == 0)
        def _():
            sg_head[...] = msc[0:16]

        for c in range(0, width, CT):
            lanes = slice(c, c + CT)
            acc, decay = acc_ref[:, lanes], c2_ref[:, lanes]
            for p in range(BP):
                one = pl.ds(pl.multiple_of(base + 8 * p, 8), 8)
                keep = jnp.where(wide(dbuf[8 * p : 8 * p + 8]) >= 1.0, 1.0 - gsc[one, lanes], 0.0)
                if p < 3:
                    keep = jnp.where(i == 0, 1.0, keep)
                decay = decay * keep
                term = decay * msc[one, lanes]
                if p < 2:
                    term = jnp.where(i == 0, 0.0, term)
                acc = acc + term
            acc_ref[:, lanes], c2_ref[:, lanes] = acc, decay

        def when(k, actions):
            @pl.when(i == min(k, blocks - 2))
            def _():
                for action in actions:
                    action()

        when(0, [unit.step2 for unit in h_units])
        when(2, [unit.step3 for unit in h_units[: n_a // 2]])
        when(3, [unit.step3 for unit in h_units[n_a // 2 :]] + [unit.step4 for unit in h_units[: n_a // 2]])
        when(4, [unit.step4 for unit in h_units[n_a // 2 :]])
        when(6, [h_end.sum_line])

    @pl.when(step == n_a + 2 * blocks - 1)
    def _():
        d3 = dist_of(bounds_ref, here.mp * span, 3)
        for c in range(0, width, CT):
            lanes = slice(c, c + CT)
            g3 = [gsc[8 * j : 8 * j + 8, lanes] for j in range(3)]
            k3 = [jnp.where(wide(d3[8 * j : 8 * j + 8]) >= 1.0, 1.0 - g3[j], 0.0) for j in range(3)]
            acc2, c2 = acc_ref[:, lanes], c2_ref[:, lanes]
            acc1, c1 = sg_head[8:16, lanes] + k3[2] * acc2, k3[2] * c2
            acc0, c0 = sg_head[0:8, lanes] + k3[1] * acc1, k3[1] * c1
            b_ref[0:16, lanes] = jnp.concatenate([k3[0] * acc0, jnp.zeros_like(acc0)], axis=0).astype(BF16)
            parts = [g3[0] * acc0, g3[1] * acc1, g3[2] * acc2, g3[0] * c0, g3[1] * c1, g3[2] * c2]
            for j in range(0, 6, 2):
                msg_ref[8 * j : 8 * j + 16, lanes] = jnp.concatenate(parts[j : j + 2], axis=0).astype(BF16)

        def out_copy(s):
            return pltpu.make_async_copy(stage.at[s % 2], f_out.at[s], st_sem.at[s % 2])

        for s in range(n_mp):
            if s >= 2:
                out_copy(s - 2).wait()
            for k, (acc, local) in enumerate(((du, local_h), (dd, local_h), (dwo, local_c))):
                block = acc[:, s * local : (s + 1) * local].astype(BF16)
                stage[s % 2, :, :, k * local_h : k * local_h + local] = block.reshape(4, dim // 4, local)
            out_copy(s).start()
        h_end.write(h_grad)
        for s in (n_mp - 2, n_mp - 1):
            out_copy(s).wait()
        for copy in weight_copies():
            copy.wait()
        for i in range(blocks):
            sg_copy(i).wait()
            rg_copy(i).wait()
        for s in [wv, wg, wo] + ffn1 + ffn2:
            s.close()
        for unit in h_units:
            unit.close()
        h_end.close()
        for dm in range(1, n_mp):
            small_copy(dm).wait_send()

            @pl.when(here.mp - dm >= 0)
            def _():
                decay_copy(dm).wait_send()

            @pl.when(here.mp + dm < n_mp)
            def _():
                decay_copy(dm).wait_recv()
                for t in range(n_a):
                    carry_copy(dm, t).wait_send()

        a_out[...] = carry[:, 8:16]


def back_kernel(span, small_ref, dgain2_ref, b_ref, msg_ref, a_ref, gain_in, len_in, x_in, wv_in, wg_in,
                sg_in, g_in, z_in, v_in, rg_in, f_in,
                tg_ref, vg_grad, f_grad, small_grad, gain_grad,
                sgb, gb, zb, vb, vg, gpg, n1t, rgb, dbuf, bar_buf, msg_buf, u0_ref, gn_ref, sm, smr, sm2,
                st, v1, v2, v3, v4, vw, vgroups, fown, f1, f2, f3, f4, fw, fgroups,
                dg1, ga, gar, gs, gbr, bounds_ref, gain_ref, x_ref, wv_ref, wg_ref, w_sem,
                e_send, e_recv, in_sem, own_sem, rg_sem, f_send, f_recv, v_send, v_recv, ff_send, ff_recv, vf_send, vf_recv,
                m_send, m_recv, k_send, k_recv, g_send, g_recv):
    here = Place()
    n_mp, n_a, n_dp = here.n_mp, here.n_a, here.n_dp
    total, dim = x_ref.shape
    width = wv_ref.shape[0]
    local_c = width // n_mp
    tile_c = 2 * local_c
    rows = BP * 8
    blocks = span // BP
    own_rows, other_rows = pl.ds(2 * here.c, 2), pl.ds(2 * (1 - here.c), 2)

    def tile_of(t):
        return here.a ^ far(t)

    def lanes_of(t):
        return pl.ds(pl.multiple_of(tile_of(t) * tile_c, tile_c), tile_c)

    def ba_copy(dm):
        return remote(b_ref, bar_buf.at[here.mp], e_send.at[dm], e_recv.at[dm], (here.dp, here.mp - dm))

    def msg_copy():
        return remote(msg_ref, msg_buf, e_send.at[0], e_recv.at[0], (here.dp, here.mp - 1))

    def inputs(t):
        slot, lanes = t % 2, lanes_of(t)
        pairs = ((sg_in, sgb), (g_in, gb), (z_in, zb), (v_in, vb))
        return [pltpu.make_async_copy(src.at[:, lanes], dst.at[slot], in_sem.at[slot, k]) for k, (src, dst) in enumerate(pairs)]

    def own_copy(t):
        return pltpu.make_async_copy(f_in.at[pl.ds(pl.multiple_of(2 * tile_of(t), 2), 2), own_rows], fown.at[t], own_sem.at[t])

    rg_copy = pltpu.make_async_copy(rg_in, rgb, rg_sem)

    def far(t):
        return (t + 1) % n_a

    f_units = [
        Reduce(here, (lambda t=t: f_in.at[pl.ds(pl.multiple_of(2 * tile_of(t), 2), 2), other_rows]), (lambda t=t: fown.at[t]),
               f1.at[t], f2.at[t], f3.at[t], f4.at[far(t) - 1] if far(t) else None, far(t), f_send.at[t], f_recv.at[t], t % 2 == 1)
        for t in range(n_a)
    ]
    v_units = [
        Reduce(here, (lambda t=t: st.at[t, :, other_rows]), (lambda t=t: st.at[t, :, own_rows]),
               v1.at[t], v2.at[t], v3.at[t], v4.at[far(t) - 1] if far(t) else None, far(t), v_send.at[t], v_recv.at[t], True)
        for t in range(n_a)
    ]
    f_end = Finish(here, f_units, f4, fgroups, fw, ff_send, ff_recv)
    v_end = Finish(here, v_units, v4, vgroups, vw, vf_send, vf_recv)

    here.greet()
    weight_copies = [pltpu.make_async_copy(src, dst, w_sem.at[k]) for k, (src, dst) in enumerate(((x_in, x_ref), (wv_in, wv_ref), (wg_in, wg_ref)))]
    for copy in weight_copies:
        copy.start()
    fill_bounds(bounds_ref, len_in)
    gain_ref[...] = gain_in[0:1]
    here.await_all()
    for dm in range(1, n_mp):

        @pl.when(here.mp - dm >= 0)
        def _():
            ba_copy(dm).start()
            if dm == 1:
                msg_copy().start()

    for copy in inputs(0):
        copy.start()
    for unit in f_units:
        unit.step1()
    for t in range(n_a):
        own_copy(t).start()
    rg_copy.start()

    sm[...] = jnp.zeros_like(sm)
    gain = gain_ref[...]
    dbuf[...] = dist_of(bounds_ref, here.mp * span, span + 4)

    def unit_of(i):
        x = x_ref[pl.ds(pl.multiple_of(i * rows, rows), rows)].astype(F32)
        inv = lax.rsqrt(jnp.mean(x * x, axis=1, keepdims=True) + NORM_EPS)
        return x * inv, inv

    for copy in weight_copies:
        copy.wait()
    for i in range(blocks):
        unit, _ = unit_of(i)
        n1t[:, i * rows : (i + 1) * rows] = (unit * gain).astype(BF16).astype(F32).T.astype(BF16)

    for t, unit in enumerate(f_units):
        own_copy(t).wait()
        unit.step2()

    for dm in range(1, n_mp):

        @pl.when(here.mp + dm < n_mp)
        def _():
            if dm == 1:
                msg_copy().wait_recv()
            ba_copy(dm).wait_recv()

    zero = jnp.zeros((8, width), F32)
    last = here.mp >= n_mp - 1
    def start_of(m):
        return bar_buf[m].astype(F32)[0:8]

    u_next = lax.fori_loop(0, n_mp - 2 - here.mp, lambda j, u: start_of(n_mp - 1 - j) + a_ref[n_mp - 1 - j] * u, zero)
    right = jnp.minimum(here.mp + 1, n_mp - 1)
    u0_ref[...] = jnp.where(last, 0.0, start_of(right) + a_ref[right] * u_next)
    msg = msg_buf[...].astype(F32)
    for j in range(3):
        gn_ref[8 * j : 8 * j + 8] = jnp.where(last, 0.0, msg[8 * j : 8 * j + 8] + msg[24 + 8 * j : 32 + 8 * j] * u_next)

    def tile_pass(t, hook):
        slot, tile, lanes = t % 2, tile_of(t), lanes_of(t)
        for copy in inputs(t):
            copy.wait()
        if t + 1 < n_a:
            for copy in inputs(t + 1):
                copy.start()
        small = jnp.concatenate([small_ref[2 * tile, :, 0:local_c], small_ref[2 * tile + 1, :, 0:local_c]], axis=1)
        taps = [jnp.broadcast_to(small[j : j + 1], (8, tile_c)) for j in range(KW)]

        def body(i, held):
            u, g1, g2, g3 = held[:4]
            sums = list(held[4:])
            base = pl.multiple_of((blocks - 1 - i) * rows, rows)

            @pl.when(i == blocks // 2)
            def _():
                hook()

            def dist(q, least):
                return wide(dbuf[pl.ds(pl.multiple_of(base + 8 * q, 8), 8)], tile_c) >= least

            for p in range(BP - 2, -2, -2):
                pair_at = pl.ds(pl.multiple_of(base + 8 * p, 16), 16)
                vals = vb[slot, pair_at].astype(F32)
                vgs, gpgs = [None, None], [None, None]
                for k in (1, 0):
                    q = p + k
                    at = pl.ds(pl.multiple_of(base + 8 * q, 8), 8)
                    gate = gb[slot, at]
                    carried = sgb[slot, at] + u
                    g0 = carried * gate
                    gp = g0 * zb[slot, at] * (1.0 - gate)
                    u = jnp.where(dist(q, 1.0), carried - g0, 0.0)
                    h1 = jnp.where(dist(q + 1, 1.0), g1, 0.0)
                    h2 = jnp.where(dist(q + 2, 2.0), g2, 0.0)
                    h3 = jnp.where(dist(q + 3, 3.0), g3, 0.0)
                    v = vals[8 * k : 8 * k + 8]
                    vgs[k] = taps[0] * g0 + taps[1] * h1 + taps[2] * h2 + taps[3] * h3
                    gpgs[k] = gp
                    for j, h in enumerate((g0, h1, h2, h3)):
                        sums[j] = sums[j] + v * h
                    sums[KW + 1] = sums[KW + 1] + g0
                    sums[KW] = sums[KW] + gp.astype(BF16).astype(F32)
                    g1, g2, g3 = g0, g1, g2
                vg[pair_at, lanes] = jnp.concatenate(vgs, axis=0).astype(BF16)
                gpg[pair_at, lanes] = jnp.concatenate(gpgs, axis=0).astype(BF16)
            return (u, g1, g2, g3, *sums)

        start = [u0_ref[:, lanes]] + [gn_ref[8 * j : 8 * j + 8, lanes] for j in range(3)]
        held = lax.fori_loop(0, blocks, body, (*start, *[jnp.zeros((8, tile_c), F32)] * (KW + 2)))
        for j in range(KW + 2):
            sm[j : j + 1, lanes] = jnp.sum(held[4 + j], axis=0, keepdims=True)
        dv = dot(n1t[...], vg[:, lanes]).astype(BF16)
        dg = dot(n1t[...], gpg[:, lanes]).astype(BF16)
        for s in range(2):
            cols = slice(s * local_c, (s + 1) * local_c)
            st[t, s] = jnp.concatenate([dv[:, cols], dg[:, cols]], axis=1).reshape(st.shape[2:])
        v_units[t].step1()
    stages = [[] for _ in range(2 * n_a)]
    final = [[] for _ in range(blocks)]

    def later(at, action):
        if at < 2 * n_a - 1:
            stages[at].append(action)
        else:
            final[min(at - (2 * n_a - 1), blocks - 1)].append(action)

    end = 2 * n_a - 1
    for t in range(n_a):
        later(t + 1, f_units[t].step3)
        later(t + 3, f_units[t].step4)
        late = t == n_a - 1
        later(end + 2 if late else 2 * t + 2, v_units[t].step2)
        later(end + 6 if late else 2 * t + 4, v_units[t].step3)
        later(end + 7 if late else 2 * t + 6 + (t == n_a - 2) * 2, v_units[t].step4)
    final[min(4, blocks - 1)].append(f_end.sum_line)

    def run(actions):
        for action in actions:
            action()

    for t in range(n_a):
        tile_pass(t, functools.partial(run, stages[2 * t]))
        if t < n_a - 1:
            run(stages[2 * t + 1])

    def sm_copy(k):
        return remote(sm, smr.at[here.dp], m_send.at[k], m_recv.at[k], (lax.rem(here.dp + k, n_dp), here.mp))

    def tile_copy(dm):
        tile = lax.rem(here.mp + dm, n_mp) // 2
        lanes = pl.ds(pl.multiple_of(tile * tile_c, tile_c), tile_c)
        return remote(sm.at[:, lanes], sm2.at[here.mp], k_send.at[dm], k_recv.at[dm], here.other(dm))

    def sm_round():
        for k in range(1, n_dp):
            sm_copy(k).wait()
        sm_sum = smr[0]
        for k in range(1, n_dp):
            sm_sum = sm_sum + smr[k]
        sm[...] = sm_sum
        for dm in range(1, n_mp):
            tile_copy(dm).start()

    for k in range(1, n_dp):
        sm_copy(k).start()
    smr[here.dp] = sm[...]
    final[min(2, blocks - 1)].append(sm_round)
    rg_copy.wait()

    @pl.loop(0, blocks)
    def _(i):
        at = pl.ds(pl.multiple_of(i * rows, rows), rows)
        ngrad = dot(vg[at], wv_ref[...]) + dot(gpg[at], wg_ref[...])
        unit, inv = unit_of(i)
        weighted = ngrad * gain
        inner = jnp.mean(weighted * unit, axis=1, keepdims=True)
        tg_ref[:, pl.ds(pl.multiple_of(i * BP, BP), BP), :] = to_row_major(rgb[at] + inv * (weighted - unit * inner))
        part = jnp.sum((ngrad * unit).reshape(BP, 8, -1), axis=0)
        dg1[...] = jnp.where(i == 0, part, dg1[...] + part)
        for k in range(blocks):
            if final[k]:

                @pl.when(i == k)
                def _():
                    run(final[k])

    for k, g in enumerate((dg1[...], dgain2_ref[...])):
        row = jnp.sum(g, axis=0, keepdims=True)
        for j in range(dim // 128):
            at = k * (dim // 128) + j
            ga[at : at + 1] = row[:, j * 128 : (j + 1) * 128]

    def ga_copy(k):
        return remote(ga, gar.at[here.dp], g_send.at[0, k], g_recv.at[0, k], (lax.rem(here.dp + k, n_dp), here.mp))

    def gb_copy(dm):
        return remote(gs, gbr.at[here.mp], g_send.at[1, dm], g_recv.at[1, dm], here.other(dm))

    for k in range(1, n_dp):
        ga_copy(k).start()
    gar[here.dp] = ga[...]
    v_end.sum_line()
    for k in range(1, n_dp):
        ga_copy(k).wait_recv()
    g_sum = gar[0]
    for k in range(1, n_dp):
        g_sum = g_sum + gar[k]
    gs[...] = g_sum
    for dm in range(1, n_mp):
        gb_copy(dm).start()
    gbr[here.mp] = g_sum
    own_lanes = pl.ds(pl.multiple_of(here.a * tile_c, tile_c), tile_c)
    sm2[here.mp] = sm[:, own_lanes]
    for dm in range(1, n_mp):
        tile_copy(dm).wait_recv()
    last_sum = sm2[0]
    for m in range(1, n_mp):
        last_sum = last_sum + sm2[m]
    small_grad[...] = last_sum
    f_end.write(f_grad)
    v_end.write(vg_grad)
    for dm in range(1, n_mp):
        gb_copy(dm).wait_recv()
    g_sum = gbr[0]
    for m in range(1, n_mp):
        g_sum = g_sum + gbr[m]
    gain_grad[...] = g_sum

    for unit in f_units + v_units + [f_end, v_end]:
        unit.close()
    for k in range(1, n_dp):
        ga_copy(k).wait_send()
    for dm in range(1, n_mp):
        tile_copy(dm).wait_send()
        gb_copy(dm).wait_send()

        @pl.when(here.mp - dm >= 0)
        def _():
            if dm == 1:
                msg_copy().wait_send()
            ba_copy(dm).wait_send()


def pack_kernel(vg_ref, f_ref, h_ref, small_ref, gains_ref, *outs):
    gain1_out, value_out, gate_out, gb_out, taps_out, cb_out, wo_out, gain2_out, up_out, down_out = outs
    local_c, local_h = value_out.shape[1], h_ref.shape[1] // 2
    value_out[...] = vg_ref[:, 0:local_c]
    gate_out[...] = vg_ref[:, local_c : 2 * local_c]
    up_out[:, 0:local_h] = h_ref[:, 0:local_h]
    up_out[:, local_h : 2 * local_h] = f_ref[:, 0:local_h]
    down_out[0:local_h] = h_ref[:, local_h : 2 * local_h].T
    down_out[local_h : 2 * local_h] = f_ref[:, local_h : 2 * local_h].T
    wo_out[...] = f_ref[:, 2 * local_h : 2 * local_h + local_c].T
    second = lax.axis_index("mp") % 2 == 1
    small = jnp.where(second, small_ref[:, local_c : 2 * local_c], small_ref[:, 0:local_c])
    taps_out[...] = small[0:KW]
    gb_out[...] = small[KW : KW + 1]
    cb_out[...] = small[KW + 1 : KW + 2]
    per = gains_ref.shape[0] // 2
    for j in range(per):
        lanes = slice(j * 128, (j + 1) * 128)
        gain1_out[:, lanes] = gains_ref[j : j + 1]
        gain2_out[:, lanes] = gains_ref[per + j : per + j + 1]


def whole(shape):
    return pl.BlockSpec(shape, lambda i: (0,) * len(shape))


def resident(shape):
    return pl.BlockSpec(shape, lambda i: (0,) * len(shape), pipeline_mode=pl.Buffered(1))


def per_device(tokens, lengths, cotangent, norm1_gain, value_proj, gate_proj, gate_bias, conv_taps, conv_bias, out_proj,
               norm2_gain, up_proj, down_proj):
    rows, span, dim = tokens.shape
    n_mp = lax.axis_size("mp")
    n_a = n_mp // 2
    total = rows * span
    blocks = span // BP
    tile = BP * 8
    local_c, local_f = value_proj.shape[1], up_proj.shape[1]
    width, units = local_c * n_mp, local_f * n_mp

    pad_c = max(local_c, 128)
    slots = lengths.shape[1]
    gains_f = jnp.stack([norm1_gain, norm2_gain]).astype(F32)
    slot_lengths = lengths.T
    gate_b, conv_b = gate_bias[None], conv_bias[None]

    def sds(shape, t=F32):
        return jax.ShapeDtypeStruct(shape, t)

    dma = pltpu.SemaphoreType.DMA
    vmem = pltpu.VMEM
    tile_c = 2 * local_c
    n_dp = lax.axis_size("dp")
    groups = n_dp // 4
    full = pl.BlockSpec(memory_space=pltpu.VMEM)
    quarter = dim // 4
    local_h = local_f // 2
    pad = -(-(2 * local_h + local_c) // 128) * 128

    def buffers(w):
        return [vmem((n_a, 2, 2, quarter, w), BF16), vmem((n_a, 2, quarter, w), BF16), vmem((n_a, quarter, w), BF16),
                vmem((n_a - 1, quarter, w), BF16), vmem((dim, w), BF16), vmem((groups, quarter, w), BF16)]

    cot_spec = pl.BlockSpec((rows, BP, dim), lambda i: (0, lax.rem(jnp.maximum(i - n_a, 0), blocks), 0))
    out_spec = pl.BlockSpec((rows, BP, dim), lambda i: (0, jnp.maximum(i - n_a - blocks, 0), 0))
    output, dgain2, b_msg, msg, a_all, smalls, h_grad, x_tm, gate, z, vals, sg, rg, wv, wg, f_grads = pl.pallas_call(
        functools.partial(front_kernel, span),
        grid=(n_a + 2 * blocks,),
        in_specs=[cot_spec, resident(value_proj.shape), resident(gate_proj.shape), resident(out_proj.shape),
                  resident(up_proj.shape), resident(down_proj.shape), resident(conv_taps.shape), resident((1, local_c)), resident((1, local_c)),
                  resident((2, dim)), resident(slot_lengths.shape), ANY],
        out_specs=[out_spec, resident((8, dim)), resident((16, width)), resident((48, width)), resident((n_mp, 8, width)),
                   resident((n_mp, 8, pad_c)),
                   resident((dim, 2 * local_h))] + [ANY] * 9,
        out_shape=[sds(tokens.shape, BF16), sds((8, dim)), sds((16, width), BF16), sds((48, width), BF16), sds((n_mp, 8, width)), sds((n_mp, 8, pad_c)),
                   sds((dim, 2 * local_h)), sds((total, dim), BF16), sds((total, width)), sds((total, width)), sds((total, width), BF16),
                   sds((total, width)), sds((total, dim)), sds((width, dim), BF16), sds((width, dim), BF16), sds((n_mp, 4, quarter, pad), BF16)],
        scratch_shapes=[
            vmem((3 * width + 2 * units, dim), BF16), vmem((total, dim), BF16), vmem((total + 32, dim), BF16), vmem((total, width), F32),
            vmem((total, width), F32), vmem((total, width), BF16), vmem((total, dim), F32), vmem((total, dim), F32),
            vmem((tile + 32, tile_c), F32), vmem((tile, tile_c), F32), vmem((tile, 128), F32),
            vmem((n_mp, 8, pad_c), F32), vmem((32, dim), BF16), vmem((n_mp, 16, width), F32), vmem((8, width), F32),
            vmem((8, width), F32), vmem((8, width), F32), vmem((16, width), F32),
            vmem((slots, 8, 128), F32), vmem((1, dim), F32), vmem((1, dim), F32),
            vmem((tile, min(FT, units // 2)), F32), vmem((tile, min(FT, units // 2)), F32), vmem((tile, units // 2), BF16),
            vmem((tile, units // 2), BF16),
            vmem((dim, width), F32), vmem((dim, units // 2), F32), vmem((dim, units // 2), F32), vmem((2, 4, quarter, pad), BF16),
            vmem((n_mp, 4, quarter, 2 * local_h), BF16), *buffers(2 * local_h),
            dma((7, 8 * n_a)), dma((7, 8 * n_a)), dma((n_mp,)), dma((n_mp,)), dma((2,)), dma((n_mp, n_a)), dma((n_mp, n_a)), dma((3,)),
            dma((2, n_a)), dma((blocks,)), dma((blocks,)), dma((blocks,)), dma((2,)), dma((8,)), dma((n_a, 4)), dma((n_a, 4)),
            dma((2 + groups,)), dma((2 + groups,)), dma((n_mp,)), dma((n_mp,)),
        ],
        compiler_params=pltpu.CompilerParams(collective_id=0, has_side_effects=True, vmem_limit_bytes=60 * MIB),
        name="front",
    )(cotangent, value_proj, gate_proj, out_proj, up_proj, down_proj, conv_taps, gate_b, conv_b, gains_f, slot_lengths, tokens)

    tokens_grad, vg_grad, f_grad, small_grad, gain_grad = pl.pallas_call(
        functools.partial(back_kernel, span),
        in_specs=[full] * 7 + [ANY] * 9,
        out_specs=[full] * 5,
        out_shape=[sds(tokens.shape), sds((dim, tile_c)), sds((dim, pad)), sds((8, tile_c)), sds((8, 128))],
        scratch_shapes=[
            vmem((2, total, tile_c), F32), vmem((2, total, tile_c), F32), vmem((2, total, tile_c), F32), vmem((2, total, tile_c), BF16),
            vmem((total, width), BF16), vmem((total, width), BF16), vmem((dim, total), BF16), vmem((total, dim), F32),
            vmem((total + 32, 128), F32), vmem((n_mp, 16, width), BF16), vmem((48, width), BF16), vmem((8, width), F32),
            vmem((24, width), F32), vmem((8, width), F32), vmem((n_dp, 8, width), F32), vmem((n_mp, 8, tile_c), F32),
            vmem((n_a, 2, 4, quarter, tile_c), BF16), *buffers(tile_c), vmem((n_a, 2, 2, quarter, pad), BF16), *buffers(pad),
            vmem((8, dim), F32), vmem((8, 128), F32), vmem((n_dp, 8, 128), F32), vmem((8, 128), F32), vmem((n_mp, 8, 128), F32),
            vmem((slots, 8, 128), F32), vmem((1, dim), F32), vmem((total, dim), BF16), vmem((width, dim), BF16), vmem((width, dim), BF16), dma((3,)),
            dma((n_mp,)), dma((n_mp,)), dma((2, 4)), dma((n_a,)), dma, dma((n_a, 4)), dma((n_a, 4)), dma((n_a, 4)), dma((n_a, 4)),
            dma((2 + groups,)), dma((2 + groups,)), dma((2 + groups,)), dma((2 + groups,)), dma((n_dp,)), dma((n_dp,)),
            dma((n_mp,)), dma((n_mp,)), dma((2, max(n_mp, n_dp))), dma((2, max(n_mp, n_dp))),
        ],
        compiler_params=pltpu.CompilerParams(collective_id=1, has_side_effects=True, vmem_limit_bytes=60 * MIB),
        name="back",
    )(smalls, dgain2, b_msg, msg, a_all, gains_f, slot_lengths, x_tm, wv, wg, sg, gate, z, vals, rg, f_grads)

    gain1_grad, value_grad, gate_grad, gb_grad, taps_grad, cb_grad, wo_grad, gain2_grad, up_grad, down_grad = pl.pallas_call(
        pack_kernel,
        out_shape=[sds((1, dim)), sds(value_proj.shape), sds(gate_proj.shape), sds((1, local_c)), sds(conv_taps.shape),
                   sds((1, local_c)), sds(out_proj.shape), sds((1, dim)), sds(up_proj.shape), sds(down_proj.shape)],
        name="pack",
    )(vg_grad, f_grad, h_grad, small_grad, gain_grad)
    return (output, tokens_grad, gain1_grad[0], value_grad, gate_grad, gb_grad[0], taps_grad, cb_grad[0], wo_grad, gain2_grad[0],
            up_grad, down_grad)


def solution(mesh):
    in_specs = (
        P("dp", "mp", None),
        P("dp", None),
        P("dp", "mp", None),
        P(),
        P(None, "mp"),
        P(None, "mp"),
        P("mp"),
        P(None, "mp"),
        P("mp"),
        P("mp", None),
        P(),
        P(None, "mp"),
        P("mp", None),
    )
    out_specs = (
        P("dp", "mp", None),
        P("dp", "mp", None),
        P(),
        P(None, "mp"),
        P(None, "mp"),
        P("mp"),
        P(None, "mp"),
        P("mp"),
        P("mp", None),
        P(),
        P(None, "mp"),
        P("mp", None),
    )
    return jax.shard_map(per_device, mesh=mesh, in_specs=in_specs, out_specs=out_specs, check_vma=False)
```

```python
import functools

import jax
import jax.numpy as jnp
from jax import lax
from jax.experimental import pallas as pl
from jax.experimental.pallas import tpu as pltpu
from jax.sharding import PartitionSpec as P

KW = 4
NORM_EPS = 1e-06
BP = 32
BF = 32
ST = 1024
CT = 256
FT = 512
MIB = 2**20
F32 = jnp.float32
BF16 = jnp.bfloat16
MESH = pl.DeviceIdType.MESH
ANY = pl.BlockSpec(memory_space=pl.ANY)

ERF_A = (0.254829592, -0.284496736, 1.421413741, -1.453152027, 1.061405429)
ERF_P = 0.3275911 * 0.7071067811865476
INV_ROOT_TWO_PI = 0.3989422804014327


def gelu_parts(x):
    t = 1.0 / (1.0 + ERF_P * jnp.abs(x))
    e = jnp.exp(-0.5 * (x * x))
    poly = 0.5 * ERF_A[4]
    for a in (ERF_A[3], ERF_A[2], ERF_A[1], ERF_A[0]):
        poly = poly * t + 0.5 * a
    tail = poly * t * e
    cdf = jnp.where(x >= 0, 1.0 - tail, tail)
    return x * cdf, cdf + x * (e * INV_ROOT_TWO_PI)


def dist_of(bounds_ref, first, count):
    place = (lax.broadcasted_iota(jnp.int32, (count, 8, 128), 0) + first).astype(F32)
    start = jnp.zeros((count, 8, 128), F32)
    for s in range(bounds_ref.shape[0]):
        b = bounds_ref[s][None]
        start = jnp.where(b <= place, jnp.maximum(start, b), start)
    return (place - start).reshape(count * 8, 128)


def wide(d, width=CT):
    return jnp.concatenate([d] * (width // 128), axis=1)


def dot(a, b):
    return jnp.dot(a, b, preferred_element_type=F32)


def dot_nt(a, b):
    return lax.dot_general(a, b, (((1,), (1,)), ((), ())), preferred_element_type=F32)


def dot_tn(a, b):
    return lax.dot_general(a, b, (((0,), (0,)), ((), ())), preferred_element_type=F32)


class Place:
    def __init__(self):
        self.n_mp, self.n_dp = lax.axis_size("mp"), lax.axis_size("dp")
        self.n_a = self.n_mp // 2
        self.dp, self.mp = lax.axis_index("dp"), lax.axis_index("mp")
        self.a, self.b = self.mp // 2, self.mp % 2
        self.y, self.c = (self.dp // 2) % 2, self.dp % 2
        self.base = self.dp - self.y * 2 - self.c
        self.q = self.c * 2 + self.y

    def line(self, da):
        return (self.dp, (self.a ^ da) * 2 + self.b)

    def diagonal(self, da):
        return (self.dp, (self.a ^ da) * 2 + 1 - self.b)

    def pair(self):
        return (self.dp, self.a * 2 + 1 - self.b)

    def beside(self):
        return (self.base + (1 - self.y) * 2 + self.c, self.mp)

    def twin(self):
        return (self.base + self.y * 2 + 1 - self.c, self.mp)

    def across(self):
        return (self.base + (1 - self.y) * 2 + 1 - self.c, self.mp)

    def other(self, dm):
        return (self.dp, lax.rem(self.mp + dm, self.n_mp))

    def partners(self):
        group = [(lax.rem(self.dp + k, self.n_dp), self.mp) for k in range(1, self.n_dp)]
        return group + [self.other(dm) for dm in range(1, self.n_mp)]

    def greet(self):
        for d in self.partners():
            pl.semaphore_signal(pltpu.get_barrier_semaphore(), inc=1, device_id=d, device_id_type=MESH)

    def await_all(self):
        pl.semaphore_wait(pltpu.get_barrier_semaphore(), len(self.partners()))


def remote(src, dst, send, recv, device):
    return pltpu.make_async_remote_copy(src_ref=src, dst_ref=dst, send_sem=send, recv_sem=recv, device_id=device, device_id_type=MESH)


class Gather:
    def __init__(self, here, wall, first, rows, send, recv, direct=False, routed=False):
        self.direct = direct
        self.routed = routed
        self.h, self.wall, self.first, self.rows, self.send, self.recv = here, wall, first, rows, send, recv
        n_a = here.n_a
        self.z0, self.x0, self.y0, self.t0 = 0, n_a, 2 * n_a, 4 * n_a
        self.used = []

    def span(self, shard, q, count=1):
        n = self.rows // 4
        return self.wall.at[pl.ds(pl.multiple_of(self.first + shard * self.rows + q * n, 16), count * n)]

    def move(self, sem, shard, q, device, count=1):
        s = self.span(shard, q, count)
        remote(s, s, self.send.at[sem], self.recv.at[sem], device).start()
        self.used.append((sem, count))

    def landed(self, sem, shard, q, count=1):
        s = self.span(shard, q, count)
        remote(s, s, self.send.at[sem], self.recv.at[sem], self.h.pair()).wait_recv()

    def shard(self, da, other):
        h = self.h
        return (h.a ^ da) * 2 + ((1 - h.b) if other else h.b)

    def slot(self, da, other):
        return 2 * da + (1 if other else 0)

    def open(self):
        h = self.h
        self.move(self.x0, h.mp, h.q, h.pair())
        for da in range(1, h.n_a):
            if self.direct:
                self.move(self.z0 + da, h.mp, 2 * h.c, h.line(da), 2)
            else:
                self.move(self.z0 + da, h.mp, h.q, h.line(da))
            if self.routed:
                self.move(self.x0 + da, h.mp, h.q, h.diagonal(da))

    def spread(self, da, other):
        h, s = self.h, self.shard(da, other)
        self.move(self.y0 + self.slot(da, other), s, h.q, h.beside())
        self.move(self.t0 + 2 * self.slot(da, other), s, h.q, h.twin())

    def from_line(self, da):
        h, s = self.h, self.shard(da, False)
        if self.direct:
            self.landed(self.z0 + da, s, 2 * h.c, 2)
            self.move(self.x0 + da, s, h.q, h.pair())
            self.move(self.t0 + 2 * self.slot(da, False), s, 2 * h.c, h.twin(), 2)
        else:
            self.landed(self.z0 + da, s, h.q)
            if not self.routed:
                self.move(self.x0 + da, s, h.q, h.pair())
            self.spread(da, False)

    def from_pair(self, da):
        self.landed(self.x0 + da, self.shard(da, True), self.h.q)
        self.spread(da, True)

    def from_beside(self, da, other):
        if self.direct and not other:
            return
        h, s = self.h, self.shard(da, other)
        q = h.c * 2 + 1 - h.y
        self.landed(self.y0 + self.slot(da, other), s, q)
        self.move(self.t0 + 2 * self.slot(da, other) + 1, s, q, h.twin())

    def from_twin(self, da, other):
        h, s = self.h, self.shard(da, other)
        if self.direct and not other:
            self.landed(self.t0 + 2 * self.slot(da, other), s, 2 * (1 - h.c), 2)
            return
        self.landed(self.t0 + 2 * self.slot(da, other), s, (1 - h.c) * 2 + h.y)
        self.landed(self.t0 + 2 * self.slot(da, other) + 1, s, (1 - h.c) * 2 + 1 - h.y)

    def close(self):
        for sem, count in self.used:
            s = self.wall.at[pl.ds(self.first, count * self.rows // 4)]
            remote(s, s, self.send.at[sem], self.recv.at[sem], self.h.pair()).wait_send()


class Reduce:
    def __init__(self, here, other_half, own_half, r1, r2, r3, line_slot, da, send, recv, pair_first=False):
        self.h, self.other_half, self.own_half, self.pair_first = here, other_half, own_half, pair_first
        self.r1, self.r2, self.r3, self.line_slot, self.da, self.send, self.recv = r1, r2, r3, line_slot, da, send, recv
        self.quarter = r2.shape[1]

    def copy(self, k):
        h = self.h
        if k == 0:
            src, dst, device = self.other_half(), self.r1, h.twin()
        elif k == 1 and self.pair_first:
            src, dst, device = self.r1.at[1 - h.b], self.r2, h.pair()
        elif k == 1:
            src, dst, device = self.r1.at[:, 1 - h.y], self.r2, h.beside()
        elif k == 2 and self.pair_first:
            src, dst, device = self.r2.at[1 - h.y], self.r3, h.beside()
        elif k == 2:
            src, dst, device = self.r2.at[1 - h.b], self.r3, h.pair()
        else:
            src, dst, device = self.r3, self.line_slot, h.line(self.da)
        return remote(src, dst, self.send.at[k], self.recv.at[k], device)

    def add(self, dst, src):
        step = 32

        @pl.loop(0, self.quarter // step)
        def _(i):
            at = pl.ds(pl.multiple_of(i * step, step), step)
            dst[at] = (dst[at].astype(F32) + src[at].astype(F32)).astype(BF16)

    def step1(self):
        self.copy(0).start()

    def step2(self):
        self.copy(0).wait_recv()
        own = self.own_half()
        for s in range(2):
            for y in range(2):
                self.add(self.r1.at[s, y], own.at[s, y])
        self.copy(1).start()

    def step3(self):
        self.copy(1).wait_recv()
        for s in range(2):
            self.add(self.r2.at[s], self.r1.at[self.h.b, s] if self.pair_first else self.r1.at[s, self.h.y])
        self.copy(2).start()

    def step4(self):
        self.copy(2).wait_recv()
        self.add(self.r3, self.r2.at[self.h.y if self.pair_first else self.h.b])
        if self.da:
            self.copy(3).start()

    def close(self):
        for k in range(4 if self.da else 3):
            self.copy(k).wait_send()


class Finish:
    def __init__(self, here, units, slots, groups, whole_sum, send, recv):
        self.h, self.units, self.slots, self.groups, self.whole, self.send, self.recv = here, units, slots, groups, whole_sum, send, recv
        self.n = units[0].quarter

    def rows(self, q):
        return self.whole.at[pl.ds(pl.multiple_of(q * self.n, self.n), self.n)]

    def copy(self, k):
        h = self.h
        part = self.rows(h.q)
        return remote(part, part, self.send.at[k], self.recv.at[k], (h.twin(), h.beside(), h.across())[k])

    def group_copy(self, k):
        h = self.h
        mine = h.dp // 4
        block = self.groups.at[mine]
        device = (lax.rem(h.dp + 4 * k, h.n_dp), h.mp)
        return remote(block, block, self.send.at[2 + k], self.recv.at[2 + k], device)

    def sum_line(self):
        h = self.h
        n_groups = h.n_dp // 4
        for unit in self.units:
            if unit.da:
                unit.copy(3).wait_recv()
        step = 32
        dst = self.rows(h.q) if n_groups == 1 else self.groups.at[h.dp // 4]
        own = self.units[-1].r3

        @pl.loop(0, self.n // step)
        def _(i):
            at = pl.ds(pl.multiple_of(i * step, step), step)
            total = own[at].astype(F32)
            for k in range(h.n_a - 1):
                total = total + self.slots[k, at].astype(F32)
            dst[at] = total.astype(BF16)

        if n_groups > 1:
            for k in range(1, n_groups):
                self.group_copy(k).start()
            for k in range(1, n_groups):
                self.group_copy(k).wait_recv()
            mine = self.rows(h.q)

            @pl.loop(0, self.n // step)
            def _(i):
                at = pl.ds(pl.multiple_of(i * step, step), step)
                total = self.groups[0, at].astype(F32)
                for k in range(1, n_groups):
                    total = total + self.groups[k, at].astype(F32)
                mine[at] = total.astype(BF16)

        for k in range(3):
            self.copy(k).start()

    def gathered(self):
        for k in range(3):
            self.copy(k).wait_recv()

    def write(self, out):
        self.gathered()
        step = 32

        @pl.loop(0, 4 * self.n // step)
        def _(i):
            at = pl.ds(pl.multiple_of(i * step, step), step)
            out[at] = self.whole[at].astype(F32)

    def close(self):
        for k in range(3):
            self.copy(k).wait_send()
        for k in range(1, self.h.n_dp // 4):
            self.group_copy(k).wait_send()


def fill_bounds(bounds_ref, len_in):
    diagonal = lax.broadcasted_iota(jnp.int32, (8, 8), 0) == lax.broadcasted_iota(jnp.int32, (8, 8), 1)
    end = jnp.zeros((8, 1), F32)
    for s in range(bounds_ref.shape[0]):
        end = end + jnp.sum(jnp.where(diagonal, len_in[s : s + 1].astype(F32), 0.0), axis=1, keepdims=True)
        bounds_ref[s] = jnp.broadcast_to(end, (8, 128))


def to_time_major(parts):
    block = jnp.stack([p.astype(F32) for p in parts], axis=0)
    return jnp.swapaxes(block, 0, 1).reshape(-1, block.shape[-1])


def to_row_major(block):
    return jnp.swapaxes(block.reshape(-1, 8, block.shape[-1]), 0, 1)


def front_kernel(span, cot_ref, wv_in, wg_in, wo_in, wu_in, wd_in, taps_in, gb_in, cb_in, gain_in, len_in, x_in,
                 out_ref, dgain_ref, b_ref, msg_ref, small_out, a_out, h_grad, x_out, g_out, z_out, v_out, sg_out, rg_out, wv_out, wg_out,
                 f_out,
                 wall, x_tm, nbuf, gsc, msc, vsc, rbuf, ngp, vbuf, gbuf, dbuf, smalls, halo, carry, state_ref, acc_ref, c2_ref,
                 sg_head, bounds_ref, gain1_ref, gain2_ref, hp, dh, hb, hg, dwo, du, dd, stage, st, r1, r2, r3, r4, rw, rgroups,
                 w_send, w_recv, s_send, s_recv, h_sem, c_send, c_recv, l_sem, t_sem, z_sem, sg_sem, rg_sem, st_sem, x_sem,
                 r_send, r_recv, e_send, e_recv, d_send, d_recv):
    here = Place()
    n_mp, n_a = here.n_mp, here.n_a
    dim = x_tm.shape[1]
    local_c, local_h = wv_in.shape[1], wu_in.shape[1] // 2
    width, units = local_c * n_mp, local_h * n_mp
    tile_c = 2 * local_c
    rows, rows_f = BP * 8, BF * 8
    blocks, blocks_f = span // BP, span // BF
    step = pl.program_id(0)
    sections, first = {}, 0
    for k, (name, count) in enumerate((("wu1", local_h), ("wd1", local_h), ("wu2", local_h), ("wd2", local_h),
                                       ("wv", local_c), ("wg", local_c), ("wo", local_c))):
        sections[name] = Gather(here, wall, first, count, w_send.at[k], w_recv.at[k], routed=name == "wo")
        first += count * n_mp
    wv, wg, wo = (sections[name] for name in ("wv", "wg", "wo"))
    ffn1, ffn2 = [sections["wu1"], sections["wd1"]], [sections["wu2"], sections["wd2"]]
    far = range(1, n_a)

    def tile_of(da):
        return here.a ^ da

    def lanes_of(t):
        return pl.ds(pl.multiple_of(tile_of(t) * tile_c, tile_c), tile_c)

    def small_copy(dm):
        return remote(smalls.at[here.mp], smalls.at[here.mp], s_send.at[dm], s_recv.at[dm], here.other(dm))

    def halo_copy():
        return remote(x_tm.at[pl.ds(span * 8 - 32, 32)], halo, h_sem.at[0], h_sem.at[1], here.other(1))

    def carry_copy(dm, t):
        block = carry.at[here.mp, :, lanes_of(t)]
        return remote(block, block, c_send.at[dm, t], c_recv.at[dm, t], (here.dp, here.mp + dm))

    def decay_copy(dm):
        block = carry.at[here.mp, 8:16]
        return remote(block, block, d_send.at[dm], d_recv.at[dm], (here.dp, here.mp - dm))

    def raw_copies():
        return [pltpu.make_async_copy(x_in.at[r], vsc.at[pl.ds(r * span, span), pl.ds(0, dim)], x_sem.at[r]) for r in range(8)]

    def tile_copies(t):
        lanes = lanes_of(t)
        return [pltpu.make_async_copy(gsc.at[:, lanes], g_out.at[:, lanes], t_sem.at[0, t]),
                pltpu.make_async_copy(vsc.at[:, lanes], v_out.at[:, lanes], t_sem.at[1, t])]

    def weight_copies():
        return [pltpu.make_async_copy(wall.at[pl.ds(s.first, width)], o, l_sem.at[1 + i]) for i, (s, o) in enumerate(((wv, wv_out), (wg, wg_out)))]

    def x_copy():
        return pltpu.make_async_copy(x_tm, x_out, l_sem.at[0])

    def block_copy(src, dst, sem, i):
        at = pl.ds(pl.multiple_of(i * rows_f, rows_f), rows_f)
        return pltpu.make_async_copy(src.at[at], dst.at[at], sem.at[i])

    z_copy = functools.partial(block_copy, msc, z_out, z_sem)
    sg_copy = functools.partial(block_copy, msc, sg_out, sg_sem)
    rg_copy = functools.partial(block_copy, ngp, rg_out, rg_sem)

    own_rows, other_rows = pl.ds(2 * here.c, 2), pl.ds(2 * (1 - here.c), 2)

    def shards(t):
        return pl.ds(pl.multiple_of(2 * (here.a ^ further(t)), 2), 2)

    def further(t):
        return (t + 1) % n_a

    h_units = [
        Reduce(here, (lambda t=t: st.at[shards(t), other_rows]), (lambda t=t: st.at[shards(t), own_rows]),
               r1.at[t], r2.at[t], r3.at[t], r4.at[further(t) - 1] if further(t) else None, further(t), r_send.at[t], r_recv.at[t], t % 2 == 1)
        for t in range(n_a)
    ]
    h_end = Finish(here, h_units, r4, rgroups, rw, e_send, e_recv)

    parts = min(4, blocks)
    moves = [[[] for _ in range(n_a)] for _ in range(parts)]

    def plan(t, i, *actions):
        moves[min(i, parts - 1)][min(t, n_a - 1)].extend(actions)

    def each(group, method, *args):
        return [functools.partial(getattr(s, method), *args) for s in group]

    mixer = (wv, wg)
    for da in far:
        plan(0, da - 1, *each(mixer, "from_pair", da))
        plan(0, da, *each(mixer, "from_beside", da, False))
        plan(0 if da < 2 else 1, 3 if da < 2 else 2 * da - 4, *each(mixer, "from_beside", da, True))
        plan(1, 1, *each([wo], "from_line", da), *each([wo], "from_pair", da))
        plan(1, 3, *each(ffn1, "from_line", da))
        plan(2, 1, *each([wo], "from_beside", da, False), *each([wo], "from_beside", da, True))
        plan(2, 3, *each(ffn1, "from_pair", da))
        plan(3, 1, *each(ffn1, "from_beside", da, False))
        plan(3, 3, *each(ffn1, "from_beside", da, True))
    plan(0, 1, *each([wo], "open"))
    plan(0, 3, *each(ffn1, "open"))
    plan(1, 1, *each([wo], "from_pair", 0))
    plan(1, 3, *each(ffn1, "from_pair", 0))
    plan(2, 1, *each([wo], "from_beside", 0, True))
    plan(3, 1, *each(ffn1, "from_beside", 0, True))
    plan(3, 3, *each(ffn2, "open"))

    def advance(i):
        for t in range(n_a):
            if moves[i][t]:

                @pl.when(step == t)
                def _():
                    for action in moves[i][t]:
                        action()

    def normed(x):
        inv = lax.rsqrt(jnp.mean(x * x, axis=1, keepdims=True) + NORM_EPS)
        return (x * inv * gain1_ref[...]).astype(BF16)

    @pl.when(step == 0)
    def _():
        for copy in raw_copies():
            copy.start()
        here.greet()
        fill_bounds(bounds_ref, len_in)
        gain1_ref[...] = gain_in[0:1]
        gain2_ref[...] = gain_in[1:2]
        for s, w in ((wv, wv_in), (wg, wg_in)):
            wall[pl.ds(pl.multiple_of(s.first + here.mp * s.rows, 16), s.rows)] = w[...].astype(F32).T.astype(BF16)
        here.await_all()
        wv.open()
        wg.open()
        smalls[here.mp] = jnp.zeros(smalls.shape[1:], F32)
        smalls[here.mp, 0:KW, 0:local_c] = taps_in[...]
        smalls[here.mp, KW : KW + 1, 0:local_c] = gb_in[...]
        smalls[here.mp, KW + 1 : KW + 2, 0:local_c] = cb_in[...]
        for dm in range(1, n_mp):
            small_copy(dm).start()

        def put(s, block):
            wall[pl.ds(pl.multiple_of(s.first + here.mp * s.rows, 16), s.rows)] = block

        put(wo, wo_in[...])
        up = wu_in[...].astype(F32).T.astype(BF16)
        for k, both in enumerate((ffn1, ffn2)):
            put(both[0], up[k * local_h : (k + 1) * local_h])
            put(both[1], wd_in[k * local_h : (k + 1) * local_h])

        def take(i):
            block = to_time_major([vsc[pl.ds(pl.multiple_of(r * span + i * BP, BP), BP), 0:dim] for r in range(8)])
            x_tm[pl.ds(pl.multiple_of(i * rows, rows), rows)] = block.astype(BF16)
            nbuf[pl.ds(pl.multiple_of(32 + i * rows, 16), rows)] = normed(block)

        for copy in raw_copies():
            copy.wait()
        take(blocks - 1)
        halo_copy().start()

        @pl.loop(0, blocks - 1)
        def _(i):
            take(i)

            @pl.when(i == min(2, blocks - 2))
            def _():
                for action in each(mixer, "from_pair", 0):
                    action()

        for action in each(mixer, "from_beside", 0, True):
            action()
        for da in far:
            for action in each(mixer, "from_line", da):
                action()
        x_copy().start()
        halo_copy().wait_recv()
        nbuf[0:32] = normed(halo[...].astype(F32))
        for dm in range(1, n_mp):
            small_copy(dm).wait_recv()

    @pl.when(step < n_a)
    def _():
        for s in (wv, wg):
            s.from_twin(step, True)

            @pl.when(step > 0)
            def _():
                s.from_twin(step, False)

        tile, lanes = tile_of(step), lanes_of(step)
        wv_t = wall[pl.ds(pl.multiple_of(wv.first + tile * tile_c, tile_c), tile_c)]
        wg_t = wall[pl.ds(pl.multiple_of(wg.first + tile * tile_c, tile_c), tile_c)]
        small = jnp.concatenate([smalls[2 * tile, :, 0:local_c], smalls[2 * tile + 1, :, 0:local_c]], axis=1)
        taps = [jnp.broadcast_to(small[j : j + 1], (8, tile_c)) for j in range(KW)]
        bias = jnp.broadcast_to(small[KW : KW + 1], (8, tile_c))
        cb = jnp.broadcast_to(small[KW + 1 : KW + 2], (8, tile_c))
        vbuf[0:32] = dot_nt(nbuf[0:32], wv_t)

        def body(i, held):
            state, decay = held
            at = pl.ds(pl.multiple_of(32 + i * rows, 16), rows)
            vbuf[32 : 32 + rows] = dot_nt(nbuf[at], wv_t)
            gbuf[...] = dot_nt(nbuf[at], wg_t)
            dbuf[0:rows] = dist_of(bounds_ref, here.mp * span + i * BP, BP)
            v1, v2, v3 = vbuf[24:32], vbuf[16:24], vbuf[8:16]
            values = []
            for p in range(BP):
                at = slice(8 * p, 8 * p + 8)
                out_at = pl.ds(pl.multiple_of(i * rows + 8 * p, 8), 8)
                v0 = vbuf[32 + 8 * p : 40 + 8 * p]
                gate = jax.nn.sigmoid(gbuf[at] + bias)
                d = wide(dbuf[at], tile_c)
                mixed = cb + taps[0] * v0
                mixed = mixed + jnp.where(d >= 1.0, taps[1] * v1, 0.0)
                mixed = mixed + jnp.where(d >= 2.0, taps[2] * v2, 0.0)
                mixed = mixed + jnp.where(d >= 3.0, taps[3] * v3, 0.0)
                linked = jnp.where(d >= 1.0, state, 0.0)
                state = linked + gate * (mixed - linked)
                decay = jnp.where(d >= 1.0, decay * (1.0 - gate), 0.0)
                gsc[out_at, lanes] = gate
                msc[out_at, lanes] = mixed
                values.append(v0)
                if p % 2:
                    pair_at = pl.ds(pl.multiple_of(i * rows + 8 * p - 8, 16), 16)
                    vsc[pair_at, lanes] = jnp.concatenate(values, axis=0).astype(BF16)
                    values = []
                v1, v2, v3 = v0, v1, v2
            vbuf[0:32] = vbuf[rows : rows + 32]
            return state, decay

        held = (jnp.zeros((8, tile_c), F32), jnp.ones((8, tile_c), F32))
        for part_no in range(parts):
            held = lax.fori_loop(part_no * blocks // parts, (part_no + 1) * blocks // parts, body, held)
            if part_no < parts - 1:
                advance(part_no)
        state, decay = held
        carry[here.mp, 0:8, lanes] = state
        carry[here.mp, 8:16, lanes] = decay
        for dm in range(1, n_mp):

            @pl.when(here.mp + dm < n_mp)
            def _():
                carry_copy(dm, step).start()

        for copy in tile_copies(step):
            copy.start()
        advance(parts - 1)

        @pl.when(step == n_a - 1)
        def _():
            for dm in range(1, n_mp):

                @pl.when(here.mp - dm >= 0)
                def _():
                    decay_copy(dm).start()

    def from_twin(s):
        s.from_twin(0, True)
        for da in far:
            s.from_twin(da, True)
            s.from_twin(da, False)

    @pl.when(step == n_a)
    def _():
        for copy in weight_copies():
            copy.start()
        for dm in range(1, n_mp):

            @pl.when(here.mp - dm >= 0)
            def _():
                for t in range(n_a):
                    carry_copy(dm, t).wait_recv()

        start = jnp.zeros((8, width), F32)
        state_ref[...] = lax.fori_loop(0, here.mp, lambda i, s: carry[i, 0:8] + carry[i, 8:16] * s, start)
        for s in [wo] + ffn1:
            from_twin(s)
        for t in range(n_a):
            for copy in tile_copies(t):
                copy.wait()
        x_copy().wait()
        halo_copy().wait_send()
        dwo[...] = jnp.zeros_like(dwo)
        du[...] = jnp.zeros_like(du)
        dd[...] = jnp.zeros_like(dd)
        dgain_ref[...] = jnp.zeros_like(dgain_ref)
        acc_ref[...] = jnp.zeros_like(acc_ref)
        c2_ref[...] = jnp.ones_like(c2_ref)
        small_out[...] = smalls[...]

    def part(s, lo=0, hi=None):
        return wall[s.first + lo : s.first + (s.rows * n_mp if hi is None else hi)]

    def inside_of(i):
        place = (lax.broadcasted_iota(jnp.int32, (BF, 8, 128), 0) + (here.mp * span + i * BF)).astype(F32)
        last = bounds_ref.shape[0] - 1
        return jnp.where(place < bounds_ref[last][None], 1.0, 0.0).reshape(rows_f, 128)[:, 0:1]

    def feed(n2, fg, up, down):
        tile_f = min(FT, units)
        for f in range(0, units, tile_f):
            cols = slice(f, f + tile_f)
            hp[...] = dot_nt(n2, part(up, f, f + tile_f))
            dh[...] = dot_nt(fg, part(down, f, f + tile_f))
            for r in range(0, rows_f, 16):
                at = slice(r, r + 16)
                hidden, slope = gelu_parts(hp[at])
                hb[at, cols] = hidden.astype(BF16)
                hg[at, cols] = (dh[at] * slope).astype(BF16)
        out, ngrad = dot(hb[...], part(down)), dot(hg[...], part(up))
        dd[...] += dot_tn(fg, hb[...])
        du[...] += dot_tn(n2, hg[...])
        return out, ngrad

    @pl.when((step >= n_a) & (step < n_a + blocks_f))
    def _():
        i = step - n_a
        base = pl.multiple_of(i * rows_f, rows_f)
        dbuf[0:rows_f] = dist_of(bounds_ref, here.mp * span + i * BF, BF)
        for c in range(0, width, ST):
            lanes = slice(c, c + ST)
            state = state_ref[:, lanes]
            for p in range(0, BF, 2):
                pair = []
                for q in (p, p + 1):
                    at = pl.ds(pl.multiple_of(base + 8 * q, 8), 8)
                    linked = jnp.where(wide(dbuf[8 * q : 8 * q + 8], ST) >= 1.0, state, 0.0)
                    z = msc[at, lanes] - linked
                    state = linked + gsc[at, lanes] * z
                    msc[at, lanes] = z
                    pair.append(state)
                vsc[pl.ds(pl.multiple_of(base + 8 * p, 16), 16), lanes] = jnp.concatenate(pair, axis=0).astype(BF16)
            state_ref[:, lanes] = state
        z_copy(i).start()
        at = pl.ds(base, rows_f)
        residual = x_tm[at].astype(F32) + dot(vsc[at], part(wo))
        resid_b = residual.astype(BF16)
        x_tm[at] = resid_b
        resid = resid_b.astype(F32)
        inv = lax.rsqrt(jnp.mean(resid * resid, axis=1, keepdims=True) + NORM_EPS)
        n2 = (resid * inv * gain2_ref[...]).astype(BF16)
        nbuf[pl.ds(pl.multiple_of(32 + base, 16), rows_f)] = n2
        fg = (to_time_major([cot_ref[r] for r in range(8)]) * inside_of(i)).astype(BF16)
        out, ngrad = feed(n2, fg, *ffn1)
        rbuf[at] = residual + out
        ngp[at] = ngrad

        def when_a(k, *calls):
            @pl.when(i == k * blocks_f // 8)
            def _():
                for method, *args in calls:
                    for action in each(ffn2, method, *args):
                        action()

        when_a(2, ("from_pair", 0), *[("from_line", da) for da in far])
        when_a(4, *[("from_pair", da) for da in far])
        when_a(6, ("from_beside", 0, True), *[("from_beside", da, False) for da in far], *[("from_beside", da, True) for da in far])

    @pl.when(step == n_a + blocks_f - 1)
    def _():
        for s in range(n_mp):
            cols = slice(s * local_h, (s + 1) * local_h)
            both = jnp.concatenate([du[:, cols].astype(BF16), dd[:, cols].astype(BF16)], axis=1)
            st[s] = both.reshape(st.shape[1:])
        for unit in h_units:
            unit.step1()
        du[...] = jnp.zeros_like(du)
        dd[...] = jnp.zeros_like(dd)
        for s in ffn2:
            from_twin(s)

    @pl.when(step >= n_a + blocks_f)
    def _():
        i = step - n_a - blocks_f
        base = pl.multiple_of(i * rows_f, rows_f)
        at = pl.ds(base, rows_f)
        dbuf[0:rows_f] = dist_of(bounds_ref, here.mp * span + i * BF, BF)
        inside = inside_of(i)
        grad_out = to_time_major([cot_ref[r] for r in range(8)]) * inside
        fg = grad_out.astype(BF16)
        out, ngrad = feed(nbuf[pl.ds(pl.multiple_of(32 + base, 16), rows_f)], fg, *ffn2)
        out_ref[...] = to_row_major((rbuf[at] + out) * inside).astype(BF16)
        ngrad = ngp[at] + ngrad
        resid = x_tm[at].astype(F32)
        inv = lax.rsqrt(jnp.mean(resid * resid, axis=1, keepdims=True) + NORM_EPS)
        unit = resid * inv
        weighted = ngrad * gain2_ref[...]
        inner = jnp.mean(weighted * unit, axis=1, keepdims=True)
        rgrad = grad_out + inv * (weighted - unit * inner)
        ngp[at] = rgrad
        rg_copy(i).start()
        dgain_ref[...] += jnp.sum((ngrad * unit).reshape(BF, 8, -1), axis=0)
        mix = rgrad.astype(BF16)
        dwo[...] += dot_tn(mix, vsc[at])
        z_copy(i).wait()
        msc[at] = dot_nt(mix, part(wo))
        sg_copy(i).start()

        @pl.when(i == 0)
        def _():
            sg_head[...] = msc[0:16]

        for c in range(0, width, ST):
            lanes = slice(c, c + ST)
            acc, decay = acc_ref[:, lanes], c2_ref[:, lanes]
            for p in range(BF):
                one = pl.ds(pl.multiple_of(base + 8 * p, 8), 8)
                keep = jnp.where(wide(dbuf[8 * p : 8 * p + 8], ST) >= 1.0, 1.0 - gsc[one, lanes], 0.0)
                if p < 3:
                    keep = jnp.where(i == 0, 1.0, keep)
                decay = decay * keep
                term = decay * msc[one, lanes]
                if p < 2:
                    term = jnp.where(i == 0, 0.0, term)
                acc = acc + term
            acc_ref[:, lanes], c2_ref[:, lanes] = acc, decay

        def when(k, actions):
            @pl.when(i == min(k * blocks_f // 8, blocks_f - 2))
            def _():
                for action in actions:
                    action()

        when(0, [unit.step2 for unit in h_units])
        when(2, [unit.step3 for unit in h_units[: n_a // 2]])
        when(3, [unit.step3 for unit in h_units[n_a // 2 :]] + [unit.step4 for unit in h_units[: n_a // 2]])
        when(4, [unit.step4 for unit in h_units[n_a // 2 :]])
        when(6, [h_end.sum_line])

    @pl.when(step == n_a + 2 * blocks_f - 1)
    def _():
        d3 = dist_of(bounds_ref, here.mp * span, 3)
        for c in range(0, width, CT):
            lanes = slice(c, c + CT)
            g3 = [gsc[8 * j : 8 * j + 8, lanes] for j in range(3)]
            k3 = [jnp.where(wide(d3[8 * j : 8 * j + 8]) >= 1.0, 1.0 - g3[j], 0.0) for j in range(3)]
            acc2, c2 = acc_ref[:, lanes], c2_ref[:, lanes]
            acc1, c1 = sg_head[8:16, lanes] + k3[2] * acc2, k3[2] * c2
            acc0, c0 = sg_head[0:8, lanes] + k3[1] * acc1, k3[1] * c1
            b_ref[0:16, lanes] = jnp.concatenate([k3[0] * acc0, jnp.zeros_like(acc0)], axis=0).astype(BF16)
            parts = [g3[0] * acc0, g3[1] * acc1, g3[2] * acc2, g3[0] * c0, g3[1] * c1, g3[2] * c2]
            for j in range(0, 6, 2):
                msg_ref[8 * j : 8 * j + 16, lanes] = jnp.concatenate(parts[j : j + 2], axis=0).astype(BF16)

        def out_copy(s):
            return pltpu.make_async_copy(stage.at[s % 2], f_out.at[s], st_sem.at[s % 2])

        for s in range(n_mp):
            if s >= 2:
                out_copy(s - 2).wait()
            for k, (acc, local) in enumerate(((du, local_h), (dd, local_h), (dwo, local_c))):
                block = acc[:, s * local : (s + 1) * local].astype(BF16)
                stage[s % 2, :, :, k * local_h : k * local_h + local] = block.reshape(4, dim // 4, local)
            out_copy(s).start()
        h_end.gathered()
        for dm in range(1, n_mp):

            @pl.when(here.mp + dm < n_mp)
            def _():
                decay_copy(dm).wait_recv()

        tail = [pltpu.make_async_copy(rw, h_grad, l_sem.at[0]), pltpu.make_async_copy(carry.at[:, pl.ds(8, 8)], a_out, l_sem.at[3])]
        for copy in tail:
            copy.start()
        for s in (n_mp - 2, n_mp - 1):
            out_copy(s).wait()
        for copy in weight_copies():
            copy.wait()
        for i in range(blocks_f):
            sg_copy(i).wait()
            rg_copy(i).wait()
        for s in [wv, wg, wo] + ffn1 + ffn2:
            s.close()
        for unit in h_units:
            unit.close()
        h_end.close()
        for dm in range(1, n_mp):
            small_copy(dm).wait_send()

            @pl.when(here.mp - dm >= 0)
            def _():
                decay_copy(dm).wait_send()

            @pl.when(here.mp + dm < n_mp)
            def _():
                for t in range(n_a):
                    carry_copy(dm, t).wait_send()

        for copy in tail:
            copy.wait()


def back_kernel(span, small_ref, dgain2_ref, b_ref, msg_ref, a_ref, gain_in, len_in, x_in, wv_in, wg_in,
                sg_in, g_in, z_in, v_in, rg_in, f_in,
                tg_ref, vg_grad, f_grad, small_grad, gain_grad,
                sgb, gb, zb, vb, vg, gpg, n1t, rgb, dbuf, bar_buf, msg_buf, u0_ref, gn_ref, sm, smr, sm2,
                st, v1, v2, v3, v4, vw, vgroups, fown, f1, f2, f3, f4, fw, fgroups,
                dg1, ga, gar, gs, gbr, bounds_ref, gain_ref, x_ref, wv_ref, wg_ref, w_sem,
                e_send, e_recv, in_sem, own_sem, rg_sem, f_send, f_recv, v_send, v_recv, ff_send, ff_recv, vf_send, vf_recv,
                m_send, m_recv, k_send, k_recv, g_send, g_recv):
    here = Place()
    n_mp, n_a, n_dp = here.n_mp, here.n_a, here.n_dp
    total, dim = x_ref.shape
    width = wv_ref.shape[0]
    local_c = width // n_mp
    tile_c = 2 * local_c
    rows = BP * 8
    blocks = span // BP
    own_rows, other_rows = pl.ds(2 * here.c, 2), pl.ds(2 * (1 - here.c), 2)

    def tile_of(t):
        return here.a ^ far(t)

    def lanes_of(t):
        return pl.ds(pl.multiple_of(tile_of(t) * tile_c, tile_c), tile_c)

    def ba_copy(dm):
        return remote(b_ref, bar_buf.at[here.mp], e_send.at[dm], e_recv.at[dm], (here.dp, here.mp - dm))

    def msg_copy():
        return remote(msg_ref, msg_buf, e_send.at[0], e_recv.at[0], (here.dp, here.mp - 1))

    def inputs(t):
        slot, lanes = t % 2, lanes_of(t)
        pairs = ((sg_in, sgb), (g_in, gb), (z_in, zb), (v_in, vb))
        return [pltpu.make_async_copy(src.at[:, lanes], dst.at[slot], in_sem.at[slot, k]) for k, (src, dst) in enumerate(pairs)]

    def own_copy(t):
        return pltpu.make_async_copy(f_in.at[pl.ds(pl.multiple_of(2 * tile_of(t), 2), 2), own_rows], fown.at[t], own_sem.at[t])

    rg_copy = pltpu.make_async_copy(rg_in, rgb, rg_sem)

    def far(t):
        return (t + 1) % n_a

    f_units = [
        Reduce(here, (lambda t=t: f_in.at[pl.ds(pl.multiple_of(2 * tile_of(t), 2), 2), other_rows]), (lambda t=t: fown.at[t]),
               f1.at[t], f2.at[t], f3.at[t], f4.at[far(t) - 1] if far(t) else None, far(t), f_send.at[t], f_recv.at[t], t % 2 == 1)
        for t in range(n_a)
    ]
    v_units = [
        Reduce(here, (lambda t=t: st.at[t, :, other_rows]), (lambda t=t: st.at[t, :, own_rows]),
               v1.at[t], v2.at[t], v3.at[t], v4.at[far(t) - 1] if far(t) else None, far(t), v_send.at[t], v_recv.at[t], True)
        for t in range(n_a)
    ]
    f_end = Finish(here, f_units, f4, fgroups, fw, ff_send, ff_recv)
    v_end = Finish(here, v_units, v4, vgroups, vw, vf_send, vf_recv)

    here.greet()
    weight_copies = [pltpu.make_async_copy(src, dst, w_sem.at[k]) for k, (src, dst) in enumerate(((x_in, x_ref), (wv_in, wv_ref), (wg_in, wg_ref)))]
    for copy in weight_copies:
        copy.start()
    fill_bounds(bounds_ref, len_in)
    gain_ref[...] = gain_in[0:1]
    here.await_all()
    for dm in range(1, n_mp):

        @pl.when(here.mp - dm >= 0)
        def _():
            ba_copy(dm).start()
            if dm == 1:
                msg_copy().start()

    for copy in inputs(0):
        copy.start()
    for unit in f_units:
        unit.step1()
    for t in range(n_a):
        own_copy(t).start()
    rg_copy.start()

    sm[...] = jnp.zeros_like(sm)
    gain = gain_ref[...]
    dbuf[...] = dist_of(bounds_ref, here.mp * span, span + 4)

    def unit_of(i):
        x = x_ref[pl.ds(pl.multiple_of(i * rows, rows), rows)].astype(F32)
        inv = lax.rsqrt(jnp.mean(x * x, axis=1, keepdims=True) + NORM_EPS)
        return x * inv, inv

    for copy in weight_copies:
        copy.wait()
    for i in range(blocks):
        unit, _ = unit_of(i)
        n1t[:, i * rows : (i + 1) * rows] = (unit * gain).astype(BF16).astype(F32).T.astype(BF16)

    for t, unit in enumerate(f_units):
        own_copy(t).wait()
        unit.step2()

    for dm in range(1, n_mp):

        @pl.when(here.mp + dm < n_mp)
        def _():
            if dm == 1:
                msg_copy().wait_recv()
            ba_copy(dm).wait_recv()

    zero = jnp.zeros((8, width), F32)
    last = here.mp >= n_mp - 1
    def start_of(m):
        return bar_buf[m].astype(F32)[0:8]

    u_next = lax.fori_loop(0, n_mp - 2 - here.mp, lambda j, u: start_of(n_mp - 1 - j) + a_ref[n_mp - 1 - j] * u, zero)
    right = jnp.minimum(here.mp + 1, n_mp - 1)
    u0_ref[...] = jnp.where(last, 0.0, start_of(right) + a_ref[right] * u_next)
    msg = msg_buf[...].astype(F32)
    for j in range(3):
        gn_ref[8 * j : 8 * j + 8] = jnp.where(last, 0.0, msg[8 * j : 8 * j + 8] + msg[24 + 8 * j : 32 + 8 * j] * u_next)

    def tile_pass(t, hook):
        slot, tile, lanes = t % 2, tile_of(t), lanes_of(t)
        for copy in inputs(t):
            copy.wait()
        if t + 1 < n_a:
            for copy in inputs(t + 1):
                copy.start()
        small = jnp.concatenate([small_ref[2 * tile, :, 0:local_c], small_ref[2 * tile + 1, :, 0:local_c]], axis=1)
        taps = [jnp.broadcast_to(small[j : j + 1], (8, tile_c)) for j in range(KW)]

        def body(i, held):
            u, g1, g2, g3 = held[:4]
            sums = list(held[4:])
            base = pl.multiple_of((blocks - 1 - i) * rows, rows)

            @pl.when(i == blocks // 2)
            def _():
                hook()

            def dist(q, least):
                return wide(dbuf[pl.ds(pl.multiple_of(base + 8 * q, 8), 8)], tile_c) >= least

            for p in range(BP - 2, -2, -2):
                pair_at = pl.ds(pl.multiple_of(base + 8 * p, 16), 16)
                vals = vb[slot, pair_at].astype(F32)
                vgs, gpgs = [None, None], [None, None]
                for k in (1, 0):
                    q = p + k
                    at = pl.ds(pl.multiple_of(base + 8 * q, 8), 8)
                    gate = gb[slot, at]
                    carried = sgb[slot, at] + u
                    g0 = carried * gate
                    gp = g0 * zb[slot, at] * (1.0 - gate)
                    u = jnp.where(dist(q, 1.0), carried - g0, 0.0)
                    h1 = jnp.where(dist(q + 1, 1.0), g1, 0.0)
                    h2 = jnp.where(dist(q + 2, 2.0), g2, 0.0)
                    h3 = jnp.where(dist(q + 3, 3.0), g3, 0.0)
                    v = vals[8 * k : 8 * k + 8]
                    vgs[k] = taps[0] * g0 + taps[1] * h1 + taps[2] * h2 + taps[3] * h3
                    gpgs[k] = gp
                    for j, h in enumerate((g0, h1, h2, h3)):
                        sums[j] = sums[j] + v * h
                    sums[KW + 1] = sums[KW + 1] + g0
                    sums[KW] = sums[KW] + gp.astype(BF16).astype(F32)
                    g1, g2, g3 = g0, g1, g2
                vg[pair_at, lanes] = jnp.concatenate(vgs, axis=0).astype(BF16)
                gpg[pair_at, lanes] = jnp.concatenate(gpgs, axis=0).astype(BF16)
            return (u, g1, g2, g3, *sums)

        start = [u0_ref[:, lanes]] + [gn_ref[8 * j : 8 * j + 8, lanes] for j in range(3)]
        held = lax.fori_loop(0, blocks, body, (*start, *[jnp.zeros((8, tile_c), F32)] * (KW + 2)))
        for j in range(KW + 2):
            sm[j : j + 1, lanes] = jnp.sum(held[4 + j], axis=0, keepdims=True)
        dv = dot(n1t[...], vg[:, lanes]).astype(BF16)
        dg = dot(n1t[...], gpg[:, lanes]).astype(BF16)
        for s in range(2):
            cols = slice(s * local_c, (s + 1) * local_c)
            st[t, s] = jnp.concatenate([dv[:, cols], dg[:, cols]], axis=1).reshape(st.shape[2:])
        v_units[t].step1()
    stages = [[] for _ in range(2 * n_a)]
    final = [[] for _ in range(blocks)]

    def later(at, action):
        if at < 2 * n_a - 1:
            stages[at].append(action)
        else:
            final[min(at - (2 * n_a - 1), blocks - 1)].append(action)

    end = 2 * n_a - 1
    for t in range(n_a):
        later(t + 1, f_units[t].step3)
        later(t + 3, f_units[t].step4)
        late = t == n_a - 1
        later(end + 2 if late else 2 * t + 2, v_units[t].step2)
        later(end + 6 if late else 2 * t + 4, v_units[t].step3)
        later(end + 7 if late else 2 * t + 6 + (t == n_a - 2) * 2, v_units[t].step4)
    final[min(4, blocks - 1)].append(f_end.sum_line)

    def run(actions):
        for action in actions:
            action()

    for t in range(n_a):
        tile_pass(t, functools.partial(run, stages[2 * t]))
        if t < n_a - 1:
            run(stages[2 * t + 1])

    def sm_copy(k):
        return remote(sm, smr.at[here.dp], m_send.at[k], m_recv.at[k], (lax.rem(here.dp + k, n_dp), here.mp))

    def tile_copy(dm):
        tile = lax.rem(here.mp + dm, n_mp) // 2
        lanes = pl.ds(pl.multiple_of(tile * tile_c, tile_c), tile_c)
        return remote(sm.at[:, lanes], sm2.at[here.mp], k_send.at[dm], k_recv.at[dm], here.other(dm))

    def sm_round():
        for k in range(1, n_dp):
            sm_copy(k).wait()
        sm_sum = smr[0]
        for k in range(1, n_dp):
            sm_sum = sm_sum + smr[k]
        sm[...] = sm_sum
        for dm in range(1, n_mp):
            tile_copy(dm).start()

    for k in range(1, n_dp):
        sm_copy(k).start()
    smr[here.dp] = sm[...]
    final[min(2, blocks - 1)].append(sm_round)
    rg_copy.wait()

    @pl.loop(0, blocks)
    def _(i):
        at = pl.ds(pl.multiple_of(i * rows, rows), rows)
        ngrad = dot(vg[at], wv_ref[...]) + dot(gpg[at], wg_ref[...])
        unit, inv = unit_of(i)
        weighted = ngrad * gain
        inner = jnp.mean(weighted * unit, axis=1, keepdims=True)
        tg_ref[:, pl.ds(pl.multiple_of(i * BP, BP), BP), :] = to_row_major(rgb[at] + inv * (weighted - unit * inner))
        part = jnp.sum((ngrad * unit).reshape(BP, 8, -1), axis=0)
        dg1[...] = jnp.where(i == 0, part, dg1[...] + part)
        for k in range(blocks):
            if final[k]:

                @pl.when(i == k)
                def _():
                    run(final[k])

    for k, g in enumerate((dg1[...], dgain2_ref[...])):
        row = jnp.sum(g, axis=0, keepdims=True)
        for j in range(dim // 128):
            at = k * (dim // 128) + j
            ga[at : at + 1] = row[:, j * 128 : (j + 1) * 128]

    def ga_copy(k):
        return remote(ga, gar.at[here.dp], g_send.at[0, k], g_recv.at[0, k], (lax.rem(here.dp + k, n_dp), here.mp))

    def gb_copy(dm):
        return remote(gs, gbr.at[here.mp], g_send.at[1, dm], g_recv.at[1, dm], here.other(dm))

    for k in range(1, n_dp):
        ga_copy(k).start()
    gar[here.dp] = ga[...]
    v_end.sum_line()
    for k in range(1, n_dp):
        ga_copy(k).wait_recv()
    g_sum = gar[0]
    for k in range(1, n_dp):
        g_sum = g_sum + gar[k]
    gs[...] = g_sum
    for dm in range(1, n_mp):
        gb_copy(dm).start()
    gbr[here.mp] = g_sum
    own_lanes = pl.ds(pl.multiple_of(here.a * tile_c, tile_c), tile_c)
    sm2[here.mp] = sm[:, own_lanes]
    for dm in range(1, n_mp):
        tile_copy(dm).wait_recv()
    last_sum = sm2[0]
    for m in range(1, n_mp):
        last_sum = last_sum + sm2[m]
    small_grad[...] = last_sum
    f_end.write(f_grad)
    v_end.write(vg_grad)
    for dm in range(1, n_mp):
        gb_copy(dm).wait_recv()
    g_sum = gbr[0]
    for m in range(1, n_mp):
        g_sum = g_sum + gbr[m]
    gain_grad[...] = g_sum

    for unit in f_units + v_units + [f_end, v_end]:
        unit.close()
    for k in range(1, n_dp):
        ga_copy(k).wait_send()
    for dm in range(1, n_mp):
        tile_copy(dm).wait_send()
        gb_copy(dm).wait_send()

        @pl.when(here.mp - dm >= 0)
        def _():
            if dm == 1:
                msg_copy().wait_send()
            ba_copy(dm).wait_send()


def pack_kernel(vg_ref, f_ref, h_ref, small_ref, gains_ref, *outs):
    gain1_out, value_out, gate_out, gb_out, taps_out, cb_out, wo_out, gain2_out, up_out, down_out = outs
    local_c, local_h = value_out.shape[1], h_ref.shape[1] // 2
    value_out[...] = vg_ref[:, 0:local_c]
    gate_out[...] = vg_ref[:, local_c : 2 * local_c]
    up_out[:, 0:local_h] = h_ref[:, 0:local_h].astype(F32)
    up_out[:, local_h : 2 * local_h] = f_ref[:, 0:local_h]
    down_out[0:local_h] = h_ref[:, local_h : 2 * local_h].astype(F32).T
    down_out[local_h : 2 * local_h] = f_ref[:, local_h : 2 * local_h].T
    wo_out[...] = f_ref[:, 2 * local_h : 2 * local_h + local_c].T
    second = lax.axis_index("mp") % 2 == 1
    small = jnp.where(second, small_ref[:, local_c : 2 * local_c], small_ref[:, 0:local_c])
    taps_out[...] = small[0:KW]
    gb_out[...] = small[KW : KW + 1]
    cb_out[...] = small[KW + 1 : KW + 2]
    per = gains_ref.shape[0] // 2
    for j in range(per):
        lanes = slice(j * 128, (j + 1) * 128)
        gain1_out[:, lanes] = gains_ref[j : j + 1]
        gain2_out[:, lanes] = gains_ref[per + j : per + j + 1]


def whole(shape):
    return pl.BlockSpec(shape, lambda i: (0,) * len(shape))


def resident(shape):
    return pl.BlockSpec(shape, lambda i: (0,) * len(shape), pipeline_mode=pl.Buffered(1))


def per_device(tokens, lengths, cotangent, norm1_gain, value_proj, gate_proj, gate_bias, conv_taps, conv_bias, out_proj,
               norm2_gain, up_proj, down_proj):
    rows, span, dim = tokens.shape
    n_mp = lax.axis_size("mp")
    n_a = n_mp // 2
    total = rows * span
    blocks = span // BP
    tile, tile_f = BP * 8, BF * 8
    blocks_f = span // BF
    local_c, local_f = value_proj.shape[1], up_proj.shape[1]
    width, units = local_c * n_mp, local_f * n_mp

    pad_c = max(local_c, 128)
    slots = lengths.shape[1]
    gains_f = jnp.stack([norm1_gain, norm2_gain]).astype(F32)
    slot_lengths = lengths.T
    gate_b, conv_b = gate_bias[None], conv_bias[None]

    def sds(shape, t=F32):
        return jax.ShapeDtypeStruct(shape, t)

    dma = pltpu.SemaphoreType.DMA
    vmem = pltpu.VMEM
    tile_c = 2 * local_c
    n_dp = lax.axis_size("dp")
    groups = n_dp // 4
    full = pl.BlockSpec(memory_space=pltpu.VMEM)
    quarter = dim // 4
    local_h = local_f // 2
    pad = -(-(2 * local_h + local_c) // 128) * 128

    def buffers(w):
        return [vmem((n_a, 2, 2, quarter, w), BF16), vmem((n_a, 2, quarter, w), BF16), vmem((n_a, quarter, w), BF16),
                vmem((n_a - 1, quarter, w), BF16), vmem((dim, w), BF16), vmem((groups, quarter, w), BF16)]

    cot_spec = pl.BlockSpec((rows, BF, dim), lambda i: (0, lax.rem(jnp.maximum(i - n_a, 0), blocks_f), 0))
    out_spec = pl.BlockSpec((rows, BF, dim), lambda i: (0, jnp.maximum(i - n_a - blocks_f, 0), 0))
    output, dgain2, b_msg, msg, smalls, a_all, h_grad, x_tm, gate, z, vals, sg, rg, wv, wg, f_grads = pl.pallas_call(
        functools.partial(front_kernel, span),
        grid=(n_a + 2 * blocks_f,),
        in_specs=[cot_spec, resident(value_proj.shape), resident(gate_proj.shape), resident(out_proj.shape),
                  resident(up_proj.shape), resident(down_proj.shape), resident(conv_taps.shape), resident((1, local_c)), resident((1, local_c)),
                  resident((2, dim)), resident(slot_lengths.shape), ANY],
        out_specs=[out_spec, resident((8, dim)), resident((16, width)), resident((48, width)), resident((n_mp, 8, pad_c))] + [ANY] * 11,
        out_shape=[sds(tokens.shape, BF16), sds((8, dim)), sds((16, width), BF16), sds((48, width), BF16), sds((n_mp, 8, pad_c)), sds((n_mp, 8, width)),
                   sds((dim, 2 * local_h), BF16), sds((total, dim), BF16), sds((total, width)), sds((total, width)), sds((total, width), BF16),
                   sds((total, width)), sds((total, dim)), sds((width, dim), BF16), sds((width, dim), BF16), sds((n_mp, 4, quarter, pad), BF16)],
        scratch_shapes=[
            vmem((3 * width + 2 * units, dim), BF16), vmem((total, dim), BF16), vmem((total + 32, dim), BF16), vmem((total, width), F32),
            vmem((total, width), F32), vmem((total, width), BF16), vmem((total, dim), F32), vmem((total, dim), F32),
            vmem((tile + 32, tile_c), F32), vmem((tile, tile_c), F32), vmem((tile_f, 128), F32),
            vmem((n_mp, 8, pad_c), F32), vmem((32, dim), BF16), vmem((n_mp, 16, width), F32), vmem((8, width), F32),
            vmem((8, width), F32), vmem((8, width), F32), vmem((16, width), F32),
            vmem((slots, 8, 128), F32), vmem((1, dim), F32), vmem((1, dim), F32),
            vmem((tile_f, min(FT, units // 2)), F32), vmem((tile_f, min(FT, units // 2)), F32), vmem((tile_f, units // 2), BF16),
            vmem((tile_f, units // 2), BF16),
            vmem((dim, width), F32), vmem((dim, units // 2), F32), vmem((dim, units // 2), F32), vmem((2, 4, quarter, pad), BF16),
            vmem((n_mp, 4, quarter, 2 * local_h), BF16), *buffers(2 * local_h),
            dma((7, 8 * n_a)), dma((7, 8 * n_a)), dma((n_mp,)), dma((n_mp,)), dma((2,)), dma((n_mp, n_a)), dma((n_mp, n_a)), dma((4,)),
            dma((2, n_a)), dma((blocks_f,)), dma((blocks_f,)), dma((blocks_f,)), dma((2,)), dma((8,)), dma((n_a, 4)), dma((n_a, 4)),
            dma((2 + groups,)), dma((2 + groups,)), dma((n_mp,)), dma((n_mp,)),
        ],
        compiler_params=pltpu.CompilerParams(collective_id=0, has_side_effects=True, vmem_limit_bytes=60 * MIB),
        name="front",
    )(cotangent, value_proj, gate_proj, out_proj, up_proj, down_proj, conv_taps, gate_b, conv_b, gains_f, slot_lengths, tokens)

    tokens_grad, vg_grad, f_grad, small_grad, gain_grad = pl.pallas_call(
        functools.partial(back_kernel, span),
        in_specs=[full] * 7 + [ANY] * 9,
        out_specs=[full] * 5,
        out_shape=[sds(tokens.shape), sds((dim, tile_c)), sds((dim, pad)), sds((8, tile_c)), sds((8, 128))],
        scratch_shapes=[
            vmem((2, total, tile_c), F32), vmem((2, total, tile_c), F32), vmem((2, total, tile_c), F32), vmem((2, total, tile_c), BF16),
            vmem((total, width), BF16), vmem((total, width), BF16), vmem((dim, total), BF16), vmem((total, dim), F32),
            vmem((total + 32, 128), F32), vmem((n_mp, 16, width), BF16), vmem((48, width), BF16), vmem((8, width), F32),
            vmem((24, width), F32), vmem((8, width), F32), vmem((n_dp, 8, width), F32), vmem((n_mp, 8, tile_c), F32),
            vmem((n_a, 2, 4, quarter, tile_c), BF16), *buffers(tile_c), vmem((n_a, 2, 2, quarter, pad), BF16), *buffers(pad),
            vmem((8, dim), F32), vmem((8, 128), F32), vmem((n_dp, 8, 128), F32), vmem((8, 128), F32), vmem((n_mp, 8, 128), F32),
            vmem((slots, 8, 128), F32), vmem((1, dim), F32), vmem((total, dim), BF16), vmem((width, dim), BF16), vmem((width, dim), BF16), dma((3,)),
            dma((n_mp,)), dma((n_mp,)), dma((2, 4)), dma((n_a,)), dma, dma((n_a, 4)), dma((n_a, 4)), dma((n_a, 4)), dma((n_a, 4)),
            dma((2 + groups,)), dma((2 + groups,)), dma((2 + groups,)), dma((2 + groups,)), dma((n_dp,)), dma((n_dp,)),
            dma((n_mp,)), dma((n_mp,)), dma((2, max(n_mp, n_dp))), dma((2, max(n_mp, n_dp))),
        ],
        compiler_params=pltpu.CompilerParams(collective_id=1, has_side_effects=True, vmem_limit_bytes=60 * MIB),
        name="back",
    )(smalls, dgain2, b_msg, msg, a_all, gains_f, slot_lengths, x_tm, wv, wg, sg, gate, z, vals, rg, f_grads)

    gain1_grad, value_grad, gate_grad, gb_grad, taps_grad, cb_grad, wo_grad, gain2_grad, up_grad, down_grad = pl.pallas_call(
        pack_kernel,
        out_shape=[sds((1, dim)), sds(value_proj.shape), sds(gate_proj.shape), sds((1, local_c)), sds(conv_taps.shape),
                   sds((1, local_c)), sds(out_proj.shape), sds((1, dim)), sds(up_proj.shape), sds(down_proj.shape)],
        name="pack",
    )(vg_grad, f_grad, h_grad, small_grad, gain_grad)
    return (output, tokens_grad, gain1_grad[0], value_grad, gate_grad, gb_grad[0], taps_grad, cb_grad[0], wo_grad, gain2_grad[0],
            up_grad, down_grad)


def solution(mesh):
    in_specs = (
        P("dp", "mp", None),
        P("dp", None),
        P("dp", "mp", None),
        P(),
        P(None, "mp"),
        P(None, "mp"),
        P("mp"),
        P(None, "mp"),
        P("mp"),
        P("mp", None),
        P(),
        P(None, "mp"),
        P("mp", None),
    )
    out_specs = (
        P("dp", "mp", None),
        P("dp", "mp", None),
        P(),
        P(None, "mp"),
        P(None, "mp"),
        P("mp"),
        P(None, "mp"),
        P("mp"),
        P("mp", None),
        P(),
        P(None, "mp"),
        P("mp", None),
    )
    return jax.shard_map(per_device, mesh=mesh, in_specs=in_specs, out_specs=out_specs, check_vma=False)
```

```python
import functools

import jax
import jax.numpy as jnp
from jax import lax
from jax.experimental import pallas as pl
from jax.experimental.pallas import tpu as pltpu
from jax.sharding import PartitionSpec as P

KW = 4
NORM_EPS = 1e-06
BP = 32
BF = 32
ST = 1024
CT = 256
FT = 512
MIB = 2**20
F32 = jnp.float32
BF16 = jnp.bfloat16
MESH = pl.DeviceIdType.MESH
ANY = pl.BlockSpec(memory_space=pl.ANY)

ERF_A = (0.254829592, -0.284496736, 1.421413741, -1.453152027, 1.061405429)
ERF_P = 0.3275911 * 0.7071067811865476
INV_ROOT_TWO_PI = 0.3989422804014327


def gelu_parts(x):
    t = 1.0 / (1.0 + ERF_P * jnp.abs(x))
    e = jnp.exp(-0.5 * (x * x))
    poly = 0.5 * ERF_A[4]
    for a in (ERF_A[3], ERF_A[2], ERF_A[1], ERF_A[0]):
        poly = poly * t + 0.5 * a
    tail = poly * t * e
    cdf = jnp.where(x >= 0, 1.0 - tail, tail)
    return x * cdf, cdf + x * (e * INV_ROOT_TWO_PI)


def dist_of(bounds_ref, first, count):
    place = (lax.broadcasted_iota(jnp.int32, (count, 8, 128), 0) + first).astype(F32)
    start = jnp.zeros((count, 8, 128), F32)
    for s in range(bounds_ref.shape[0]):
        b = bounds_ref[s][None]
        start = jnp.where(b <= place, jnp.maximum(start, b), start)
    return (place - start).reshape(count * 8, 128)


def wide(d, width=CT):
    return jnp.concatenate([d] * (width // 128), axis=1)


def dot(a, b):
    return jnp.dot(a, b, preferred_element_type=F32)


def dot_nt(a, b):
    return lax.dot_general(a, b, (((1,), (1,)), ((), ())), preferred_element_type=F32)


def dot_tn(a, b):
    return lax.dot_general(a, b, (((0,), (0,)), ((), ())), preferred_element_type=F32)


class Place:
    def __init__(self):
        self.n_mp, self.n_dp = lax.axis_size("mp"), lax.axis_size("dp")
        self.n_a = self.n_mp // 2
        self.dp, self.mp = lax.axis_index("dp"), lax.axis_index("mp")
        self.a, self.b = self.mp // 2, self.mp % 2
        self.y, self.c = (self.dp // 2) % 2, self.dp % 2
        self.base = self.dp - self.y * 2 - self.c
        self.q = self.c * 2 + self.y

    def line(self, da):
        return (self.dp, (self.a ^ da) * 2 + self.b)

    def diagonal(self, da):
        return (self.dp, (self.a ^ da) * 2 + 1 - self.b)

    def pair(self):
        return (self.dp, self.a * 2 + 1 - self.b)

    def beside(self):
        return (self.base + (1 - self.y) * 2 + self.c, self.mp)

    def twin(self):
        return (self.base + self.y * 2 + 1 - self.c, self.mp)

    def across(self):
        return (self.base + (1 - self.y) * 2 + 1 - self.c, self.mp)

    def other(self, dm):
        return (self.dp, lax.rem(self.mp + dm, self.n_mp))

    def partners(self):
        group = [(lax.rem(self.dp + k, self.n_dp), self.mp) for k in range(1, self.n_dp)]
        return group + [self.other(dm) for dm in range(1, self.n_mp)]

    def greet(self):
        for d in self.partners():
            pl.semaphore_signal(pltpu.get_barrier_semaphore(), inc=1, device_id=d, device_id_type=MESH)

    def await_all(self):
        pl.semaphore_wait(pltpu.get_barrier_semaphore(), len(self.partners()))


def remote(src, dst, send, recv, device):
    return pltpu.make_async_remote_copy(src_ref=src, dst_ref=dst, send_sem=send, recv_sem=recv, device_id=device, device_id_type=MESH)


class Gather:
    def __init__(self, here, wall, first, rows, send, recv, direct=False, routed=False):
        self.direct = direct
        self.routed = routed
        self.h, self.wall, self.first, self.rows, self.send, self.recv = here, wall, first, rows, send, recv
        n_a = here.n_a
        self.z0, self.x0, self.y0, self.t0 = 0, n_a, 2 * n_a, 4 * n_a
        self.used = []

    def span(self, shard, q, count=1):
        n = self.rows // 4
        return self.wall.at[pl.ds(pl.multiple_of(self.first + shard * self.rows + q * n, 16), count * n)]

    def move(self, sem, shard, q, device, count=1):
        s = self.span(shard, q, count)
        remote(s, s, self.send.at[sem], self.recv.at[sem], device).start()
        self.used.append((sem, count))

    def landed(self, sem, shard, q, count=1):
        s = self.span(shard, q, count)
        remote(s, s, self.send.at[sem], self.recv.at[sem], self.h.pair()).wait_recv()

    def shard(self, da, other):
        h = self.h
        return (h.a ^ da) * 2 + ((1 - h.b) if other else h.b)

    def slot(self, da, other):
        return 2 * da + (1 if other else 0)

    def open(self):
        h = self.h
        self.move(self.x0, h.mp, h.q, h.pair())
        for da in range(1, h.n_a):
            if self.direct:
                self.move(self.z0 + da, h.mp, 2 * h.c, h.line(da), 2)
            else:
                self.move(self.z0 + da, h.mp, h.q, h.line(da))
            if self.routed:
                self.move(self.x0 + da, h.mp, h.q, h.diagonal(da))

    def spread(self, da, other):
        h, s = self.h, self.shard(da, other)
        self.move(self.y0 + self.slot(da, other), s, h.q, h.beside())
        self.move(self.t0 + 2 * self.slot(da, other), s, h.q, h.twin())

    def from_line(self, da):
        h, s = self.h, self.shard(da, False)
        if self.direct:
            self.landed(self.z0 + da, s, 2 * h.c, 2)
            self.move(self.x0 + da, s, h.q, h.pair())
            self.move(self.t0 + 2 * self.slot(da, False), s, 2 * h.c, h.twin(), 2)
        else:
            self.landed(self.z0 + da, s, h.q)
            if not self.routed:
                self.move(self.x0 + da, s, h.q, h.pair())
            self.spread(da, False)

    def from_pair(self, da):
        self.landed(self.x0 + da, self.shard(da, True), self.h.q)
        self.spread(da, True)

    def from_beside(self, da, other):
        if self.direct and not other:
            return
        h, s = self.h, self.shard(da, other)
        q = h.c * 2 + 1 - h.y
        self.landed(self.y0 + self.slot(da, other), s, q)
        self.move(self.t0 + 2 * self.slot(da, other) + 1, s, q, h.twin())

    def from_twin(self, da, other):
        h, s = self.h, self.shard(da, other)
        if self.direct and not other:
            self.landed(self.t0 + 2 * self.slot(da, other), s, 2 * (1 - h.c), 2)
            return
        self.landed(self.t0 + 2 * self.slot(da, other), s, (1 - h.c) * 2 + h.y)
        self.landed(self.t0 + 2 * self.slot(da, other) + 1, s, (1 - h.c) * 2 + 1 - h.y)

    def close(self):
        for sem, count in self.used:
            s = self.wall.at[pl.ds(self.first, count * self.rows // 4)]
            remote(s, s, self.send.at[sem], self.recv.at[sem], self.h.pair()).wait_send()


class Reduce:
    def __init__(self, here, other_half, own_half, r1, r2, r3, line_slot, da, send, recv, pair_first=False):
        self.h, self.other_half, self.own_half, self.pair_first = here, other_half, own_half, pair_first
        self.r1, self.r2, self.r3, self.line_slot, self.da, self.send, self.recv = r1, r2, r3, line_slot, da, send, recv
        self.quarter = r2.shape[1]

    def copy(self, k):
        h = self.h
        if k == 0:
            src, dst, device = self.other_half(), self.r1, h.twin()
        elif k == 1 and self.pair_first:
            src, dst, device = self.r1.at[1 - h.b], self.r2, h.pair()
        elif k == 1:
            src, dst, device = self.r1.at[:, 1 - h.y], self.r2, h.beside()
        elif k == 2 and self.pair_first:
            src, dst, device = self.r2.at[1 - h.y], self.r3, h.beside()
        elif k == 2:
            src, dst, device = self.r2.at[1 - h.b], self.r3, h.pair()
        else:
            src, dst, device = self.r3, self.line_slot, h.line(self.da)
        return remote(src, dst, self.send.at[k], self.recv.at[k], device)

    def add(self, dst, src):
        step = 32

        @pl.loop(0, self.quarter // step)
        def _(i):
            at = pl.ds(pl.multiple_of(i * step, step), step)
            dst[at] = (dst[at].astype(F32) + src[at].astype(F32)).astype(BF16)

    def step1(self):
        self.copy(0).start()

    def step2(self):
        self.copy(0).wait_recv()
        own = self.own_half()
        for s in range(2):
            for y in range(2):
                self.add(self.r1.at[s, y], own.at[s, y])
        self.copy(1).start()

    def step3(self):
        self.copy(1).wait_recv()
        for s in range(2):
            self.add(self.r2.at[s], self.r1.at[self.h.b, s] if self.pair_first else self.r1.at[s, self.h.y])
        self.copy(2).start()

    def step4(self):
        self.copy(2).wait_recv()
        self.add(self.r3, self.r2.at[self.h.y if self.pair_first else self.h.b])
        if self.da:
            self.copy(3).start()

    def close(self):
        for k in range(4 if self.da else 3):
            self.copy(k).wait_send()


class Finish:
    def __init__(self, here, units, slots, groups, whole_sum, send, recv):
        self.h, self.units, self.slots, self.groups, self.whole, self.send, self.recv = here, units, slots, groups, whole_sum, send, recv
        self.n = units[0].quarter

    def rows(self, q):
        return self.whole.at[pl.ds(pl.multiple_of(q * self.n, self.n), self.n)]

    def copy(self, k):
        h = self.h
        part = self.rows(h.q)
        return remote(part, part, self.send.at[k], self.recv.at[k], (h.twin(), h.beside(), h.across())[k])

    def group_copy(self, k):
        h = self.h
        mine = h.dp // 4
        block = self.groups.at[mine]
        device = (lax.rem(h.dp + 4 * k, h.n_dp), h.mp)
        return remote(block, block, self.send.at[2 + k], self.recv.at[2 + k], device)

    def sum_line(self):
        h = self.h
        n_groups = h.n_dp // 4
        for unit in self.units:
            if unit.da:
                unit.copy(3).wait_recv()
        step = 32
        dst = self.rows(h.q) if n_groups == 1 else self.groups.at[h.dp // 4]
        own = self.units[-1].r3

        @pl.loop(0, self.n // step)
        def _(i):
            at = pl.ds(pl.multiple_of(i * step, step), step)
            total = own[at].astype(F32)
            for k in range(h.n_a - 1):
                total = total + self.slots[k, at].astype(F32)
            dst[at] = total.astype(BF16)

        if n_groups > 1:
            for k in range(1, n_groups):
                self.group_copy(k).start()
            for k in range(1, n_groups):
                self.group_copy(k).wait_recv()
            mine = self.rows(h.q)

            @pl.loop(0, self.n // step)
            def _(i):
                at = pl.ds(pl.multiple_of(i * step, step), step)
                total = self.groups[0, at].astype(F32)
                for k in range(1, n_groups):
                    total = total + self.groups[k, at].astype(F32)
                mine[at] = total.astype(BF16)

        for k in range(3):
            self.copy(k).start()

    def gathered(self):
        for k in range(3):
            self.copy(k).wait_recv()

    def write(self, out):
        self.gathered()
        step = 32

        @pl.loop(0, 4 * self.n // step)
        def _(i):
            at = pl.ds(pl.multiple_of(i * step, step), step)
            out[at] = self.whole[at]

    def close(self):
        for k in range(3):
            self.copy(k).wait_send()
        for k in range(1, self.h.n_dp // 4):
            self.group_copy(k).wait_send()


def fill_bounds(bounds_ref, len_in):
    diagonal = lax.broadcasted_iota(jnp.int32, (8, 8), 0) == lax.broadcasted_iota(jnp.int32, (8, 8), 1)
    end = jnp.zeros((8, 1), F32)
    for s in range(bounds_ref.shape[0]):
        end = end + jnp.sum(jnp.where(diagonal, len_in[s : s + 1].astype(F32), 0.0), axis=1, keepdims=True)
        bounds_ref[s] = jnp.broadcast_to(end, (8, 128))


def to_time_major(parts):
    block = jnp.stack([p.astype(F32) for p in parts], axis=0)
    return jnp.swapaxes(block, 0, 1).reshape(-1, block.shape[-1])


def to_row_major(block):
    return jnp.swapaxes(block.reshape(-1, 8, block.shape[-1]), 0, 1)


def front_kernel(span, cot_ref, wv_in, wg_in, wo_in, wu_in, wd_in, taps_in, gb_in, cb_in, gain_in, len_in, x_in,
                 out_ref, dgain_ref, b_ref, msg_ref, small_out, a_out, h_grad, x_out, g_out, z_out, v_out, sg_out, rg_out, wv_out, wg_out,
                 f_out,
                 wall, x_tm, nbuf, gsc, msc, vsc, rbuf, ngp, vbuf, gbuf, dbuf, smalls, halo, carry, state_ref, acc_ref, c2_ref,
                 sg_head, bounds_ref, gain1_ref, gain2_ref, hp, dh, hb, hg, dwo, du, dd, stage, st, r1, r2, r3, r4, rw, rgroups,
                 w_send, w_recv, s_send, s_recv, h_sem, c_send, c_recv, l_sem, t_sem, z_sem, sg_sem, rg_sem, st_sem, x_sem,
                 r_send, r_recv, e_send, e_recv, d_send, d_recv):
    here = Place()
    n_mp, n_a = here.n_mp, here.n_a
    dim = x_tm.shape[1]
    local_c, local_h = wv_in.shape[1], wu_in.shape[1] // 2
    width, units = local_c * n_mp, local_h * n_mp
    tile_c = 2 * local_c
    rows, rows_f = BP * 8, BF * 8
    blocks, blocks_f = span // BP, span // BF
    step = pl.program_id(0)
    sections, first = {}, 0
    for k, (name, count) in enumerate((("wu1", local_h), ("wd1", local_h), ("wu2", local_h), ("wd2", local_h),
                                       ("wv", local_c), ("wg", local_c), ("wo", local_c))):
        sections[name] = Gather(here, wall, first, count, w_send.at[k], w_recv.at[k], routed=name in ("wo", "wu2", "wd2"))
        first += count * n_mp
    wv, wg, wo = (sections[name] for name in ("wv", "wg", "wo"))
    ffn1, ffn2 = [sections["wu1"], sections["wd1"]], [sections["wu2"], sections["wd2"]]
    far = range(1, n_a)

    def tile_of(da):
        return here.a ^ da

    def lanes_of(t):
        return pl.ds(pl.multiple_of(tile_of(t) * tile_c, tile_c), tile_c)

    def small_copy(dm):
        return remote(smalls.at[here.mp], smalls.at[here.mp], s_send.at[dm], s_recv.at[dm], here.other(dm))

    def halo_copy():
        return remote(x_tm.at[pl.ds(span * 8 - 32, 32)], halo, h_sem.at[0], h_sem.at[1], here.other(1))

    def carry_copy(dm, t):
        block = carry.at[here.mp, :, lanes_of(t)]
        return remote(block, block, c_send.at[dm, t], c_recv.at[dm, t], (here.dp, here.mp + dm))

    def decay_copy(dm):
        block = carry.at[here.mp, 8:16]
        return remote(block, block, d_send.at[dm], d_recv.at[dm], (here.dp, here.mp - dm))

    def raw_copies():
        return [pltpu.make_async_copy(x_in.at[r], vsc.at[pl.ds(r * span, span), pl.ds(0, dim)], x_sem.at[r]) for r in range(8)]

    def tile_copies(t):
        lanes = lanes_of(t)
        return [pltpu.make_async_copy(gsc.at[:, lanes], g_out.at[:, lanes], t_sem.at[0, t]),
                pltpu.make_async_copy(vsc.at[:, lanes], v_out.at[:, lanes], t_sem.at[1, t])]

    def weight_copies():
        return [pltpu.make_async_copy(wall.at[pl.ds(s.first, width)], o, l_sem.at[1 + i]) for i, (s, o) in enumerate(((wv, wv_out), (wg, wg_out)))]

    def x_copy():
        return pltpu.make_async_copy(x_tm, x_out, l_sem.at[0])

    def block_copy(src, dst, sem, i):
        at = pl.ds(pl.multiple_of(i * rows_f, rows_f), rows_f)
        return pltpu.make_async_copy(src.at[at], dst.at[at], sem.at[i])

    z_copy = functools.partial(block_copy, msc, z_out, z_sem)
    sg_copy = functools.partial(block_copy, msc, sg_out, sg_sem)
    rg_copy = functools.partial(block_copy, ngp, rg_out, rg_sem)

    own_rows, other_rows = pl.ds(2 * here.c, 2), pl.ds(2 * (1 - here.c), 2)

    def shards(t):
        return pl.ds(pl.multiple_of(2 * (here.a ^ further(t)), 2), 2)

    def further(t):
        return (t + 1) % n_a

    h_units = [
        Reduce(here, (lambda t=t: st.at[shards(t), other_rows]), (lambda t=t: st.at[shards(t), own_rows]),
               r1.at[t], r2.at[t], r3.at[t], r4.at[further(t) - 1] if further(t) else None, further(t), r_send.at[t], r_recv.at[t], t % 2 == 1)
        for t in range(n_a)
    ]
    h_end = Finish(here, h_units, r4, rgroups, rw, e_send, e_recv)

    parts = min(4, blocks)
    moves = [[[] for _ in range(n_a)] for _ in range(parts)]

    def plan(t, i, *actions):
        moves[min(i, parts - 1)][min(t, n_a - 1)].extend(actions)

    def each(group, method, *args):
        return [functools.partial(getattr(s, method), *args) for s in group]

    mixer = (wv, wg)
    for da in far:
        plan(0, da - 1, *each(mixer, "from_pair", da))
        plan(0, da, *each(mixer, "from_beside", da, False))
        plan(0 if da < 2 else 1, 3 if da < 2 else 2 * da - 4, *each(mixer, "from_beside", da, True))
        plan(1, 1, *each([wo], "from_line", da), *each([wo], "from_pair", da))
        plan(1, 3, *each(ffn1, "from_line", da))
        plan(2, 1, *each([wo], "from_beside", da, False), *each([wo], "from_beside", da, True))
        plan(2, 3, *each(ffn1, "from_pair", da))
        plan(3, 1, *each(ffn1, "from_beside", da, False))
        plan(3, 3, *each(ffn1, "from_beside", da, True))
    plan(0, 1, *each([wo], "open"))
    plan(0, 3, *each(ffn1, "open"))
    plan(1, 1, *each([wo], "from_pair", 0))
    plan(1, 3, *each(ffn1, "from_pair", 0))
    plan(2, 1, *each([wo], "from_beside", 0, True))
    plan(3, 1, *each(ffn1, "from_beside", 0, True))
    plan(3, 3, *each(ffn2, "open"))

    def advance(i):
        for t in range(n_a):
            if moves[i][t]:

                @pl.when(step == t)
                def _():
                    for action in moves[i][t]:
                        action()

    def normed(x):
        inv = lax.rsqrt(jnp.mean(x * x, axis=1, keepdims=True) + NORM_EPS)
        return (x * inv * gain1_ref[...]).astype(BF16)

    @pl.when(step == 0)
    def _():
        for copy in raw_copies():
            copy.start()
        here.greet()
        fill_bounds(bounds_ref, len_in)
        gain1_ref[...] = gain_in[0:1]
        gain2_ref[...] = gain_in[1:2]
        for s, w in ((wv, wv_in), (wg, wg_in)):
            wall[pl.ds(pl.multiple_of(s.first + here.mp * s.rows, 16), s.rows)] = w[...].astype(F32).T.astype(BF16)
        here.await_all()
        wv.open()
        wg.open()
        smalls[here.mp] = jnp.zeros(smalls.shape[1:], F32)
        smalls[here.mp, 0:KW, 0:local_c] = taps_in[...]
        smalls[here.mp, KW : KW + 1, 0:local_c] = gb_in[...]
        smalls[here.mp, KW + 1 : KW + 2, 0:local_c] = cb_in[...]
        for dm in range(1, n_mp):
            small_copy(dm).start()

        def put(s, block):
            wall[pl.ds(pl.multiple_of(s.first + here.mp * s.rows, 16), s.rows)] = block

        put(wo, wo_in[...])
        up = wu_in[...].astype(F32).T.astype(BF16)
        for k, both in enumerate((ffn1, ffn2)):
            put(both[0], up[k * local_h : (k + 1) * local_h])
            put(both[1], wd_in[k * local_h : (k + 1) * local_h])

        def take(i):
            block = to_time_major([vsc[pl.ds(pl.multiple_of(r * span + i * BP, BP), BP), 0:dim] for r in range(8)])
            x_tm[pl.ds(pl.multiple_of(i * rows, rows), rows)] = block.astype(BF16)
            nbuf[pl.ds(pl.multiple_of(32 + i * rows, 16), rows)] = normed(block)

        for copy in raw_copies():
            copy.wait()
        take(blocks - 1)
        halo_copy().start()

        @pl.loop(0, blocks - 1)
        def _(i):
            take(i)

            @pl.when(i == min(2, blocks - 2))
            def _():
                for action in each(mixer, "from_pair", 0):
                    action()

        for action in each(mixer, "from_beside", 0, True):
            action()
        for da in far:
            for action in each(mixer, "from_line", da):
                action()
        x_copy().start()
        halo_copy().wait_recv()
        nbuf[0:32] = normed(halo[...].astype(F32))
        for dm in range(1, n_mp):
            small_copy(dm).wait_recv()

    @pl.when(step < n_a)
    def _():
        for s in (wv, wg):
            s.from_twin(step, True)

            @pl.when(step > 0)
            def _():
                s.from_twin(step, False)

        tile, lanes = tile_of(step), lanes_of(step)
        wv_t = wall[pl.ds(pl.multiple_of(wv.first + tile * tile_c, tile_c), tile_c)]
        wg_t = wall[pl.ds(pl.multiple_of(wg.first + tile * tile_c, tile_c), tile_c)]
        small = jnp.concatenate([smalls[2 * tile, :, 0:local_c], smalls[2 * tile + 1, :, 0:local_c]], axis=1)
        taps = [jnp.broadcast_to(small[j : j + 1], (8, tile_c)) for j in range(KW)]
        bias = jnp.broadcast_to(small[KW : KW + 1], (8, tile_c))
        cb = jnp.broadcast_to(small[KW + 1 : KW + 2], (8, tile_c))
        vbuf[0:32] = dot_nt(nbuf[0:32], wv_t)

        def body(i, held):
            state, decay = held
            at = pl.ds(pl.multiple_of(32 + i * rows, 16), rows)
            vbuf[32 : 32 + rows] = dot_nt(nbuf[at], wv_t)
            gbuf[...] = dot_nt(nbuf[at], wg_t)
            dbuf[0:rows] = dist_of(bounds_ref, here.mp * span + i * BP, BP)
            v1, v2, v3 = vbuf[24:32], vbuf[16:24], vbuf[8:16]
            values = []
            for p in range(BP):
                at = slice(8 * p, 8 * p + 8)
                out_at = pl.ds(pl.multiple_of(i * rows + 8 * p, 8), 8)
                v0 = vbuf[32 + 8 * p : 40 + 8 * p]
                gate = jax.nn.sigmoid(gbuf[at] + bias)
                d = wide(dbuf[at], tile_c)
                mixed = cb + taps[0] * v0
                mixed = mixed + jnp.where(d >= 1.0, taps[1] * v1, 0.0)
                mixed = mixed + jnp.where(d >= 2.0, taps[2] * v2, 0.0)
                mixed = mixed + jnp.where(d >= 3.0, taps[3] * v3, 0.0)
                linked = jnp.where(d >= 1.0, state, 0.0)
                state = linked + gate * (mixed - linked)
                decay = jnp.where(d >= 1.0, decay * (1.0 - gate), 0.0)
                gsc[out_at, lanes] = gate
                msc[out_at, lanes] = mixed
                values.append(v0)
                if p % 2:
                    pair_at = pl.ds(pl.multiple_of(i * rows + 8 * p - 8, 16), 16)
                    vsc[pair_at, lanes] = jnp.concatenate(values, axis=0).astype(BF16)
                    values = []
                v1, v2, v3 = v0, v1, v2
            vbuf[0:32] = vbuf[rows : rows + 32]
            return state, decay

        held = (jnp.zeros((8, tile_c), F32), jnp.ones((8, tile_c), F32))
        for part_no in range(parts):
            held = lax.fori_loop(part_no * blocks // parts, (part_no + 1) * blocks // parts, body, held)
            if part_no < parts - 1:
                advance(part_no)
        state, decay = held
        carry[here.mp, 0:8, lanes] = state
        carry[here.mp, 8:16, lanes] = decay
        for dm in range(1, n_mp):

            @pl.when(here.mp + dm < n_mp)
            def _():
                carry_copy(dm, step).start()

        for copy in tile_copies(step):
            copy.start()
        advance(parts - 1)

        @pl.when(step == n_a - 1)
        def _():
            for dm in range(1, n_mp):

                @pl.when(here.mp - dm >= 0)
                def _():
                    decay_copy(dm).start()

    def from_twin(s):
        s.from_twin(0, True)
        for da in far:
            s.from_twin(da, True)
            s.from_twin(da, False)

    @pl.when(step == n_a)
    def _():
        for copy in weight_copies():
            copy.start()
        for dm in range(1, n_mp):

            @pl.when(here.mp - dm >= 0)
            def _():
                for t in range(n_a):
                    carry_copy(dm, t).wait_recv()

        start = jnp.zeros((8, width), F32)
        state_ref[...] = lax.fori_loop(0, here.mp, lambda i, s: carry[i, 0:8] + carry[i, 8:16] * s, start)
        for s in [wo] + ffn1:
            from_twin(s)
        for t in range(n_a):
            for copy in tile_copies(t):
                copy.wait()
        x_copy().wait()
        halo_copy().wait_send()
        dwo[...] = jnp.zeros_like(dwo)
        du[...] = jnp.zeros_like(du)
        dd[...] = jnp.zeros_like(dd)
        dgain_ref[...] = jnp.zeros_like(dgain_ref)
        acc_ref[...] = jnp.zeros_like(acc_ref)
        c2_ref[...] = jnp.ones_like(c2_ref)
        small_out[...] = smalls[...]

    def part(s, lo=0, hi=None):
        return wall[s.first + lo : s.first + (s.rows * n_mp if hi is None else hi)]

    def inside_of(i):
        place = (lax.broadcasted_iota(jnp.int32, (BF, 8, 128), 0) + (here.mp * span + i * BF)).astype(F32)
        last = bounds_ref.shape[0] - 1
        return jnp.where(place < bounds_ref[last][None], 1.0, 0.0).reshape(rows_f, 128)[:, 0:1]

    def feed(n2, fg, up, down):
        tile_f = min(FT, units)
        for f in range(0, units, tile_f):
            cols = slice(f, f + tile_f)
            hp[...] = dot_nt(n2, part(up, f, f + tile_f))
            dh[...] = dot_nt(fg, part(down, f, f + tile_f))
            for r in range(0, rows_f, 16):
                at = slice(r, r + 16)
                hidden, slope = gelu_parts(hp[at])
                hb[at, cols] = hidden.astype(BF16)
                hg[at, cols] = (dh[at] * slope).astype(BF16)
        out, ngrad = dot(hb[...], part(down)), dot(hg[...], part(up))
        dd[...] += dot_tn(fg, hb[...])
        du[...] += dot_tn(n2, hg[...])
        return out, ngrad

    @pl.when((step >= n_a) & (step < n_a + blocks_f))
    def _():
        i = step - n_a
        base = pl.multiple_of(i * rows_f, rows_f)
        dbuf[0:rows_f] = dist_of(bounds_ref, here.mp * span + i * BF, BF)
        for c in range(0, width, ST):
            lanes = slice(c, c + ST)
            state = state_ref[:, lanes]
            for p in range(0, BF, 2):
                pair = []
                for q in (p, p + 1):
                    at = pl.ds(pl.multiple_of(base + 8 * q, 8), 8)
                    linked = jnp.where(wide(dbuf[8 * q : 8 * q + 8], ST) >= 1.0, state, 0.0)
                    z = msc[at, lanes] - linked
                    state = linked + gsc[at, lanes] * z
                    msc[at, lanes] = z
                    pair.append(state)
                vsc[pl.ds(pl.multiple_of(base + 8 * p, 16), 16), lanes] = jnp.concatenate(pair, axis=0).astype(BF16)
            state_ref[:, lanes] = state
        z_copy(i).start()
        at = pl.ds(base, rows_f)
        residual = x_tm[at].astype(F32) + dot(vsc[at], part(wo))
        resid_b = residual.astype(BF16)
        x_tm[at] = resid_b
        resid = resid_b.astype(F32)
        inv = lax.rsqrt(jnp.mean(resid * resid, axis=1, keepdims=True) + NORM_EPS)
        n2 = (resid * inv * gain2_ref[...]).astype(BF16)
        nbuf[pl.ds(pl.multiple_of(32 + base, 16), rows_f)] = n2
        fg = (to_time_major([cot_ref[r] for r in range(8)]) * inside_of(i)).astype(BF16)
        out, ngrad = feed(n2, fg, *ffn1)
        rbuf[at] = residual + out
        ngp[at] = ngrad

        def when_a(k, *calls):
            @pl.when(i == k * blocks_f // 8)
            def _():
                for method, *args in calls:
                    for action in each(ffn2, method, *args):
                        action()

        when_a(2, ("from_pair", 0), *[("from_line", da) for da in far])
        when_a(4, *[("from_pair", da) for da in far])
        when_a(6, ("from_beside", 0, True), *[("from_beside", da, False) for da in far], *[("from_beside", da, True) for da in far])

    @pl.when(step == n_a + blocks_f - 1)
    def _():
        for s in range(n_mp):
            cols = slice(s * local_h, (s + 1) * local_h)
            both = jnp.concatenate([du[:, cols].astype(BF16), dd[:, cols].astype(BF16)], axis=1)
            st[s] = both.reshape(st.shape[1:])
        for unit in h_units:
            unit.step1()
        du[...] = jnp.zeros_like(du)
        dd[...] = jnp.zeros_like(dd)
        for s in ffn2:
            from_twin(s)

    @pl.when(step >= n_a + blocks_f)
    def _():
        i = step - n_a - blocks_f
        base = pl.multiple_of(i * rows_f, rows_f)
        at = pl.ds(base, rows_f)
        dbuf[0:rows_f] = dist_of(bounds_ref, here.mp * span + i * BF, BF)
        inside = inside_of(i)
        grad_out = to_time_major([cot_ref[r] for r in range(8)]) * inside
        fg = grad_out.astype(BF16)
        out, ngrad = feed(nbuf[pl.ds(pl.multiple_of(32 + base, 16), rows_f)], fg, *ffn2)
        out_ref[...] = to_row_major((rbuf[at] + out) * inside).astype(BF16)
        ngrad = ngp[at] + ngrad
        resid = x_tm[at].astype(F32)
        inv = lax.rsqrt(jnp.mean(resid * resid, axis=1, keepdims=True) + NORM_EPS)
        unit = resid * inv
        weighted = ngrad * gain2_ref[...]
        inner = jnp.mean(weighted * unit, axis=1, keepdims=True)
        rgrad = grad_out + inv * (weighted - unit * inner)
        ngp[at] = rgrad
        rg_copy(i).start()
        dgain_ref[...] += jnp.sum((ngrad * unit).reshape(BF, 8, -1), axis=0)
        mix = rgrad.astype(BF16)
        dwo[...] += dot_tn(mix, vsc[at])
        z_copy(i).wait()
        msc[at] = dot_nt(mix, part(wo))
        sg_copy(i).start()

        @pl.when(i == 0)
        def _():
            sg_head[...] = msc[0:16]

        for c in range(0, width, ST):
            lanes = slice(c, c + ST)
            acc, decay = acc_ref[:, lanes], c2_ref[:, lanes]
            for p in range(BF):
                one = pl.ds(pl.multiple_of(base + 8 * p, 8), 8)
                keep = jnp.where(wide(dbuf[8 * p : 8 * p + 8], ST) >= 1.0, 1.0 - gsc[one, lanes], 0.0)
                if p < 3:
                    keep = jnp.where(i == 0, 1.0, keep)
                decay = decay * keep
                term = decay * msc[one, lanes]
                if p < 2:
                    term = jnp.where(i == 0, 0.0, term)
                acc = acc + term
            acc_ref[:, lanes], c2_ref[:, lanes] = acc, decay

        def when(k, actions):
            @pl.when(i == min(k * blocks_f // 8, blocks_f - 2))
            def _():
                for action in actions:
                    action()

        when(0, [unit.step2 for unit in h_units])
        when(2, [unit.step3 for unit in h_units[: n_a // 2]])
        when(3, [unit.step3 for unit in h_units[n_a // 2 :]] + [unit.step4 for unit in h_units[: n_a // 2]])
        when(4, [unit.step4 for unit in h_units[n_a // 2 :]])
        when(6, [h_end.sum_line])

    @pl.when(step == n_a + 2 * blocks_f - 1)
    def _():
        d3 = dist_of(bounds_ref, here.mp * span, 3)
        for c in range(0, width, CT):
            lanes = slice(c, c + CT)
            g3 = [gsc[8 * j : 8 * j + 8, lanes] for j in range(3)]
            k3 = [jnp.where(wide(d3[8 * j : 8 * j + 8]) >= 1.0, 1.0 - g3[j], 0.0) for j in range(3)]
            acc2, c2 = acc_ref[:, lanes], c2_ref[:, lanes]
            acc1, c1 = sg_head[8:16, lanes] + k3[2] * acc2, k3[2] * c2
            acc0, c0 = sg_head[0:8, lanes] + k3[1] * acc1, k3[1] * c1
            b_ref[0:16, lanes] = jnp.concatenate([k3[0] * acc0, jnp.zeros_like(acc0)], axis=0).astype(BF16)
            parts = [g3[0] * acc0, g3[1] * acc1, g3[2] * acc2, g3[0] * c0, g3[1] * c1, g3[2] * c2]
            for j in range(0, 6, 2):
                msg_ref[8 * j : 8 * j + 16, lanes] = jnp.concatenate(parts[j : j + 2], axis=0).astype(BF16)

        def out_copy(s):
            return pltpu.make_async_copy(stage.at[s % 2], f_out.at[s], st_sem.at[s % 2])

        for s in range(n_mp):
            if s >= 2:
                out_copy(s - 2).wait()
            for k, (acc, local) in enumerate(((du, local_h), (dd, local_h), (dwo, local_c))):
                block = acc[:, s * local : (s + 1) * local].astype(BF16)
                stage[s % 2, :, :, k * local_h : k * local_h + local] = block.reshape(4, dim // 4, local)
            out_copy(s).start()
        h_end.gathered()
        for dm in range(1, n_mp):

            @pl.when(here.mp + dm < n_mp)
            def _():
                decay_copy(dm).wait_recv()

        tail = [pltpu.make_async_copy(rw, h_grad, l_sem.at[0]), pltpu.make_async_copy(carry.at[:, pl.ds(8, 8)], a_out, l_sem.at[3])]
        for copy in tail:
            copy.start()
        for s in (n_mp - 2, n_mp - 1):
            out_copy(s).wait()
        for copy in weight_copies():
            copy.wait()
        for i in range(blocks_f):
            sg_copy(i).wait()
            rg_copy(i).wait()
        for s in [wv, wg, wo] + ffn1 + ffn2:
            s.close()
        for unit in h_units:
            unit.close()
        h_end.close()
        for dm in range(1, n_mp):
            small_copy(dm).wait_send()

            @pl.when(here.mp - dm >= 0)
            def _():
                decay_copy(dm).wait_send()

            @pl.when(here.mp + dm < n_mp)
            def _():
                for t in range(n_a):
                    carry_copy(dm, t).wait_send()

        for copy in tail:
            copy.wait()


def back_kernel(span, small_ref, dgain2_ref, b_ref, msg_ref, a_ref, gain_in, len_in, x_in, wv_in, wg_in,
                sg_in, g_in, z_in, v_in, rg_in, f_in,
                tg_ref, vg_grad, f_grad, small_grad, gain_grad,
                sgb, gb, zb, vb, vg, gpg, n1t, rgb, dbuf, bar_buf, msg_buf, u0_ref, gn_ref, sm, smr, sm2,
                st, v1, v2, v3, v4, vw, vgroups, fown, f1, f2, f3, f4, fw, fgroups,
                dg1, ga, gar, gs, gbr, bounds_ref, gain_ref, x_ref, wv_ref, wg_ref, w_sem,
                e_send, e_recv, in_sem, own_sem, rg_sem, f_send, f_recv, v_send, v_recv, ff_send, ff_recv, vf_send, vf_recv,
                m_send, m_recv, k_send, k_recv, g_send, g_recv):
    here = Place()
    n_mp, n_a, n_dp = here.n_mp, here.n_a, here.n_dp
    total, dim = x_ref.shape
    width = wv_ref.shape[0]
    local_c = width // n_mp
    tile_c = 2 * local_c
    rows = BP * 8
    blocks = span // BP
    own_rows, other_rows = pl.ds(2 * here.c, 2), pl.ds(2 * (1 - here.c), 2)

    def tile_of(t):
        return here.a ^ far(t)

    def lanes_of(t):
        return pl.ds(pl.multiple_of(tile_of(t) * tile_c, tile_c), tile_c)

    def ba_copy(dm):
        return remote(b_ref, bar_buf.at[here.mp], e_send.at[dm], e_recv.at[dm], (here.dp, here.mp - dm))

    def msg_copy():
        return remote(msg_ref, msg_buf, e_send.at[0], e_recv.at[0], (here.dp, here.mp - 1))

    def inputs(t):
        slot, lanes = t % 2, lanes_of(t)
        pairs = ((sg_in, sgb), (g_in, gb), (z_in, zb), (v_in, vb))
        return [pltpu.make_async_copy(src.at[:, lanes], dst.at[slot], in_sem.at[slot, k]) for k, (src, dst) in enumerate(pairs)]

    def own_copy(t):
        return pltpu.make_async_copy(f_in.at[pl.ds(pl.multiple_of(2 * tile_of(t), 2), 2), own_rows], fown.at[t], own_sem.at[t])

    rg_copy = pltpu.make_async_copy(rg_in, rgb, rg_sem)

    def far(t):
        return (t + 1) % n_a

    f_units = [
        Reduce(here, (lambda t=t: f_in.at[pl.ds(pl.multiple_of(2 * tile_of(t), 2), 2), other_rows]), (lambda t=t: fown.at[t]),
               f1.at[t], f2.at[t], f3.at[t], f4.at[far(t) - 1] if far(t) else None, far(t), f_send.at[t], f_recv.at[t], t % 2 == 1)
        for t in range(n_a)
    ]
    v_units = [
        Reduce(here, (lambda t=t: st.at[t, :, other_rows]), (lambda t=t: st.at[t, :, own_rows]),
               v1.at[t], v2.at[t], v3.at[t], v4.at[far(t) - 1] if far(t) else None, far(t), v_send.at[t], v_recv.at[t], True)
        for t in range(n_a)
    ]
    f_end = Finish(here, f_units, f4, fgroups, fw, ff_send, ff_recv)
    v_end = Finish(here, v_units, v4, vgroups, vw, vf_send, vf_recv)

    here.greet()
    weight_copies = [pltpu.make_async_copy(src, dst, w_sem.at[k]) for k, (src, dst) in enumerate(((x_in, x_ref), (wv_in, wv_ref), (wg_in, wg_ref)))]
    for copy in weight_copies:
        copy.start()
    fill_bounds(bounds_ref, len_in)
    gain_ref[...] = gain_in[0:1]
    here.await_all()
    for dm in range(1, n_mp):

        @pl.when(here.mp - dm >= 0)
        def _():
            ba_copy(dm).start()
            if dm == 1:
                msg_copy().start()

    for copy in inputs(0):
        copy.start()
    for unit in f_units:
        unit.step1()
    for t in range(n_a):
        own_copy(t).start()
    rg_copy.start()

    sm[...] = jnp.zeros_like(sm)
    gain = gain_ref[...]
    dbuf[...] = dist_of(bounds_ref, here.mp * span, span + 4)

    def unit_of(i):
        x = x_ref[pl.ds(pl.multiple_of(i * rows, rows), rows)].astype(F32)
        inv = lax.rsqrt(jnp.mean(x * x, axis=1, keepdims=True) + NORM_EPS)
        return x * inv, inv

    for copy in weight_copies:
        copy.wait()
    for i in range(blocks):
        unit, _ = unit_of(i)
        n1t[:, i * rows : (i + 1) * rows] = (unit * gain).astype(BF16).astype(F32).T.astype(BF16)

    for t, unit in enumerate(f_units):
        own_copy(t).wait()
        unit.step2()

    for dm in range(1, n_mp):

        @pl.when(here.mp + dm < n_mp)
        def _():
            if dm == 1:
                msg_copy().wait_recv()
            ba_copy(dm).wait_recv()

    zero = jnp.zeros((8, width), F32)
    last = here.mp >= n_mp - 1
    def start_of(m):
        return bar_buf[m].astype(F32)[0:8]

    u_next = lax.fori_loop(0, n_mp - 2 - here.mp, lambda j, u: start_of(n_mp - 1 - j) + a_ref[n_mp - 1 - j] * u, zero)
    right = jnp.minimum(here.mp + 1, n_mp - 1)
    u0_ref[...] = jnp.where(last, 0.0, start_of(right) + a_ref[right] * u_next)
    msg = msg_buf[...].astype(F32)
    for j in range(3):
        gn_ref[8 * j : 8 * j + 8] = jnp.where(last, 0.0, msg[8 * j : 8 * j + 8] + msg[24 + 8 * j : 32 + 8 * j] * u_next)

    def tile_pass(t, hook):
        slot, tile, lanes = t % 2, tile_of(t), lanes_of(t)
        for copy in inputs(t):
            copy.wait()
        if t + 1 < n_a:
            for copy in inputs(t + 1):
                copy.start()
        small = jnp.concatenate([small_ref[2 * tile, :, 0:local_c], small_ref[2 * tile + 1, :, 0:local_c]], axis=1)
        taps = [jnp.broadcast_to(small[j : j + 1], (8, tile_c)) for j in range(KW)]

        def body(i, held):
            u, g1, g2, g3 = held[:4]
            sums = list(held[4:])
            base = pl.multiple_of((blocks - 1 - i) * rows, rows)

            @pl.when(i == blocks // 2)
            def _():
                hook()

            def dist(q, least):
                return wide(dbuf[pl.ds(pl.multiple_of(base + 8 * q, 8), 8)], tile_c) >= least

            for p in range(BP - 2, -2, -2):
                pair_at = pl.ds(pl.multiple_of(base + 8 * p, 16), 16)
                vals = vb[slot, pair_at].astype(F32)
                vgs, gpgs = [None, None], [None, None]
                for k in (1, 0):
                    q = p + k
                    at = pl.ds(pl.multiple_of(base + 8 * q, 8), 8)
                    gate = gb[slot, at]
                    carried = sgb[slot, at] + u
                    g0 = carried * gate
                    gp = g0 * zb[slot, at] * (1.0 - gate)
                    u = jnp.where(dist(q, 1.0), carried - g0, 0.0)
                    h1 = jnp.where(dist(q + 1, 1.0), g1, 0.0)
                    h2 = jnp.where(dist(q + 2, 2.0), g2, 0.0)
                    h3 = jnp.where(dist(q + 3, 3.0), g3, 0.0)
                    v = vals[8 * k : 8 * k + 8]
                    vgs[k] = taps[0] * g0 + taps[1] * h1 + taps[2] * h2 + taps[3] * h3
                    gpgs[k] = gp
                    for j, h in enumerate((g0, h1, h2, h3)):
                        sums[j] = sums[j] + v * h
                    sums[KW + 1] = sums[KW + 1] + g0
                    sums[KW] = sums[KW] + gp.astype(BF16).astype(F32)
                    g1, g2, g3 = g0, g1, g2
                vg[pair_at, lanes] = jnp.concatenate(vgs, axis=0).astype(BF16)
                gpg[pair_at, lanes] = jnp.concatenate(gpgs, axis=0).astype(BF16)
            return (u, g1, g2, g3, *sums)

        start = [u0_ref[:, lanes]] + [gn_ref[8 * j : 8 * j + 8, lanes] for j in range(3)]
        held = lax.fori_loop(0, blocks, body, (*start, *[jnp.zeros((8, tile_c), F32)] * (KW + 2)))
        for j in range(KW + 2):
            sm[j : j + 1, lanes] = jnp.sum(held[4 + j], axis=0, keepdims=True)
        dv = dot(n1t[...], vg[:, lanes]).astype(BF16)
        dg = dot(n1t[...], gpg[:, lanes]).astype(BF16)
        for s in range(2):
            cols = slice(s * local_c, (s + 1) * local_c)
            st[t, s] = jnp.concatenate([dv[:, cols], dg[:, cols]], axis=1).reshape(st.shape[2:])
        v_units[t].step1()
    stages = [[] for _ in range(2 * n_a)]
    final = [[] for _ in range(blocks)]

    def later(at, action):
        if at < 2 * n_a - 1:
            stages[at].append(action)
        else:
            final[min(at - (2 * n_a - 1), blocks - 1)].append(action)

    end = 2 * n_a - 1
    for t in range(n_a):
        later(t + 1, f_units[t].step3)
        later(t + 3, f_units[t].step4)
        late = t == n_a - 1
        later(end + 2 if late else 2 * t + 2, v_units[t].step2)
        later(end + 6 if late else 2 * t + 4, v_units[t].step3)
        later(end + 7 if late else 2 * t + 6 + (t == n_a - 2) * 2, v_units[t].step4)
    final[min(4, blocks - 1)].append(f_end.sum_line)

    def run(actions):
        for action in actions:
            action()

    for t in range(n_a):
        tile_pass(t, functools.partial(run, stages[2 * t]))
        if t < n_a - 1:
            run(stages[2 * t + 1])

    def sm_copy(k):
        return remote(sm, smr.at[here.dp], m_send.at[k], m_recv.at[k], (lax.rem(here.dp + k, n_dp), here.mp))

    def tile_copy(dm):
        tile = lax.rem(here.mp + dm, n_mp) // 2
        lanes = pl.ds(pl.multiple_of(tile * tile_c, tile_c), tile_c)
        return remote(sm.at[:, lanes], sm2.at[here.mp], k_send.at[dm], k_recv.at[dm], here.other(dm))

    def sm_round():
        for k in range(1, n_dp):
            sm_copy(k).wait()
        sm_sum = smr[0]
        for k in range(1, n_dp):
            sm_sum = sm_sum + smr[k]
        sm[...] = sm_sum
        for dm in range(1, n_mp):
            tile_copy(dm).start()

    for k in range(1, n_dp):
        sm_copy(k).start()
    smr[here.dp] = sm[...]
    final[min(2, blocks - 1)].append(sm_round)
    rg_copy.wait()

    @pl.loop(0, blocks)
    def _(i):
        at = pl.ds(pl.multiple_of(i * rows, rows), rows)
        ngrad = dot(vg[at], wv_ref[...]) + dot(gpg[at], wg_ref[...])
        unit, inv = unit_of(i)
        weighted = ngrad * gain
        inner = jnp.mean(weighted * unit, axis=1, keepdims=True)
        tg_ref[:, pl.ds(pl.multiple_of(i * BP, BP), BP), :] = to_row_major(rgb[at] + inv * (weighted - unit * inner))
        part = jnp.sum((ngrad * unit).reshape(BP, 8, -1), axis=0)
        dg1[...] = jnp.where(i == 0, part, dg1[...] + part)
        for k in range(blocks):
            if final[k]:

                @pl.when(i == k)
                def _():
                    run(final[k])

    for k, g in enumerate((dg1[...], dgain2_ref[...])):
        row = jnp.sum(g, axis=0, keepdims=True)
        for j in range(dim // 128):
            at = k * (dim // 128) + j
            ga[at : at + 1] = row[:, j * 128 : (j + 1) * 128]

    def ga_copy(k):
        return remote(ga, gar.at[here.dp], g_send.at[0, k], g_recv.at[0, k], (lax.rem(here.dp + k, n_dp), here.mp))

    def gb_copy(dm):
        return remote(gs, gbr.at[here.mp], g_send.at[1, dm], g_recv.at[1, dm], here.other(dm))

    for k in range(1, n_dp):
        ga_copy(k).start()
    gar[here.dp] = ga[...]
    v_end.sum_line()
    for k in range(1, n_dp):
        ga_copy(k).wait_recv()
    g_sum = gar[0]
    for k in range(1, n_dp):
        g_sum = g_sum + gar[k]
    gs[...] = g_sum
    for dm in range(1, n_mp):
        gb_copy(dm).start()
    gbr[here.mp] = g_sum
    own_lanes = pl.ds(pl.multiple_of(here.a * tile_c, tile_c), tile_c)
    sm2[here.mp] = sm[:, own_lanes]
    for dm in range(1, n_mp):
        tile_copy(dm).wait_recv()
    last_sum = sm2[0]
    for m in range(1, n_mp):
        last_sum = last_sum + sm2[m]
    small_grad[...] = last_sum
    f_end.write(f_grad)
    v_end.write(vg_grad)
    for dm in range(1, n_mp):
        gb_copy(dm).wait_recv()
    g_sum = gbr[0]
    for m in range(1, n_mp):
        g_sum = g_sum + gbr[m]
    gain_grad[...] = g_sum

    for unit in f_units + v_units + [f_end, v_end]:
        unit.close()
    for k in range(1, n_dp):
        ga_copy(k).wait_send()
    for dm in range(1, n_mp):
        tile_copy(dm).wait_send()
        gb_copy(dm).wait_send()

        @pl.when(here.mp - dm >= 0)
        def _():
            if dm == 1:
                msg_copy().wait_send()
            ba_copy(dm).wait_send()


def pack_kernel(vg_ref, f_ref, h_ref, small_ref, gains_ref, *outs):
    gain1_out, value_out, gate_out, gb_out, taps_out, cb_out, wo_out, gain2_out, up_out, down_out = outs
    local_c, local_h = value_out.shape[1], h_ref.shape[1] // 2
    value_out[...] = vg_ref[:, 0:local_c].astype(F32)
    gate_out[...] = vg_ref[:, local_c : 2 * local_c].astype(F32)
    up_out[:, 0:local_h] = h_ref[:, 0:local_h].astype(F32)
    up_out[:, local_h : 2 * local_h] = f_ref[:, 0:local_h].astype(F32)
    down_out[0:local_h] = h_ref[:, local_h : 2 * local_h].astype(F32).T
    down_out[local_h : 2 * local_h] = f_ref[:, local_h : 2 * local_h].astype(F32).T
    wo_out[...] = f_ref[:, 2 * local_h : 2 * local_h + local_c].astype(F32).T
    second = lax.axis_index("mp") % 2 == 1
    small = jnp.where(second, small_ref[:, local_c : 2 * local_c], small_ref[:, 0:local_c])
    taps_out[...] = small[0:KW]
    gb_out[...] = small[KW : KW + 1]
    cb_out[...] = small[KW + 1 : KW + 2]
    per = gains_ref.shape[0] // 2
    for j in range(per):
        lanes = slice(j * 128, (j + 1) * 128)
        gain1_out[:, lanes] = gains_ref[j : j + 1]
        gain2_out[:, lanes] = gains_ref[per + j : per + j + 1]


def whole(shape):
    return pl.BlockSpec(shape, lambda i: (0,) * len(shape))


def resident(shape):
    return pl.BlockSpec(shape, lambda i: (0,) * len(shape), pipeline_mode=pl.Buffered(1))


def per_device(tokens, lengths, cotangent, norm1_gain, value_proj, gate_proj, gate_bias, conv_taps, conv_bias, out_proj,
               norm2_gain, up_proj, down_proj):
    rows, span, dim = tokens.shape
    n_mp = lax.axis_size("mp")
    n_a = n_mp // 2
    total = rows * span
    blocks = span // BP
    tile, tile_f = BP * 8, BF * 8
    blocks_f = span // BF
    local_c, local_f = value_proj.shape[1], up_proj.shape[1]
    width, units = local_c * n_mp, local_f * n_mp

    pad_c = max(local_c, 128)
    slots = lengths.shape[1]
    gains_f = jnp.stack([norm1_gain, norm2_gain]).astype(F32)
    slot_lengths = lengths.T
    gate_b, conv_b = gate_bias[None], conv_bias[None]

    def sds(shape, t=F32):
        return jax.ShapeDtypeStruct(shape, t)

    dma = pltpu.SemaphoreType.DMA
    vmem = pltpu.VMEM
    tile_c = 2 * local_c
    n_dp = lax.axis_size("dp")
    groups = n_dp // 4
    full = pl.BlockSpec(memory_space=pltpu.VMEM)
    quarter = dim // 4
    local_h = local_f // 2
    pad = -(-(2 * local_h + local_c) // 128) * 128

    def buffers(w):
        return [vmem((n_a, 2, 2, quarter, w), BF16), vmem((n_a, 2, quarter, w), BF16), vmem((n_a, quarter, w), BF16),
                vmem((n_a - 1, quarter, w), BF16), vmem((dim, w), BF16), vmem((groups, quarter, w), BF16)]

    cot_spec = pl.BlockSpec((rows, BF, dim), lambda i: (0, lax.rem(jnp.maximum(i - n_a, 0), blocks_f), 0))
    out_spec = pl.BlockSpec((rows, BF, dim), lambda i: (0, jnp.maximum(i - n_a - blocks_f, 0), 0))
    output, dgain2, b_msg, msg, smalls, a_all, h_grad, x_tm, gate, z, vals, sg, rg, wv, wg, f_grads = pl.pallas_call(
        functools.partial(front_kernel, span),
        grid=(n_a + 2 * blocks_f,),
        in_specs=[cot_spec, resident(value_proj.shape), resident(gate_proj.shape), resident(out_proj.shape),
                  resident(up_proj.shape), resident(down_proj.shape), resident(conv_taps.shape), resident((1, local_c)), resident((1, local_c)),
                  resident((2, dim)), resident(slot_lengths.shape), ANY],
        out_specs=[out_spec, resident((8, dim)), resident((16, width)), resident((48, width)), resident((n_mp, 8, pad_c))] + [ANY] * 11,
        out_shape=[sds(tokens.shape, BF16), sds((8, dim)), sds((16, width), BF16), sds((48, width), BF16), sds((n_mp, 8, pad_c)), sds((n_mp, 8, width)),
                   sds((dim, 2 * local_h), BF16), sds((total, dim), BF16), sds((total, width)), sds((total, width)), sds((total, width), BF16),
                   sds((total, width)), sds((total, dim)), sds((width, dim), BF16), sds((width, dim), BF16), sds((n_mp, 4, quarter, pad), BF16)],
        scratch_shapes=[
            vmem((3 * width + 2 * units, dim), BF16), vmem((total, dim), BF16), vmem((total + 32, dim), BF16), vmem((total, width), F32),
            vmem((total, width), F32), vmem((total, width), BF16), vmem((total, dim), F32), vmem((total, dim), F32),
            vmem((tile + 32, tile_c), F32), vmem((tile, tile_c), F32), vmem((tile_f, 128), F32),
            vmem((n_mp, 8, pad_c), F32), vmem((32, dim), BF16), vmem((n_mp, 16, width), F32), vmem((8, width), F32),
            vmem((8, width), F32), vmem((8, width), F32), vmem((16, width), F32),
            vmem((slots, 8, 128), F32), vmem((1, dim), F32), vmem((1, dim), F32),
            vmem((tile_f, min(FT, units // 2)), F32), vmem((tile_f, min(FT, units // 2)), F32), vmem((tile_f, units // 2), BF16),
            vmem((tile_f, units // 2), BF16),
            vmem((dim, width), F32), vmem((dim, units // 2), F32), vmem((dim, units // 2), F32), vmem((2, 4, quarter, pad), BF16),
            vmem((n_mp, 4, quarter, 2 * local_h), BF16), *buffers(2 * local_h),
            dma((7, 8 * n_a)), dma((7, 8 * n_a)), dma((n_mp,)), dma((n_mp,)), dma((2,)), dma((n_mp, n_a)), dma((n_mp, n_a)), dma((4,)),
            dma((2, n_a)), dma((blocks_f,)), dma((blocks_f,)), dma((blocks_f,)), dma((2,)), dma((8,)), dma((n_a, 4)), dma((n_a, 4)),
            dma((2 + groups,)), dma((2 + groups,)), dma((n_mp,)), dma((n_mp,)),
        ],
        compiler_params=pltpu.CompilerParams(collective_id=0, has_side_effects=True, vmem_limit_bytes=60 * MIB),
        name="front",
    )(cotangent, value_proj, gate_proj, out_proj, up_proj, down_proj, conv_taps, gate_b, conv_b, gains_f, slot_lengths, tokens)

    tokens_grad, vg_grad, f_grad, small_grad, gain_grad = pl.pallas_call(
        functools.partial(back_kernel, span),
        in_specs=[full] * 7 + [ANY] * 9,
        out_specs=[full] * 5,
        out_shape=[sds(tokens.shape), sds((dim, tile_c), BF16), sds((dim, pad), BF16), sds((8, tile_c)), sds((8, 128))],
        scratch_shapes=[
            vmem((2, total, tile_c), F32), vmem((2, total, tile_c), F32), vmem((2, total, tile_c), F32), vmem((2, total, tile_c), BF16),
            vmem((total, width), BF16), vmem((total, width), BF16), vmem((dim, total), BF16), vmem((total, dim), F32),
            vmem((total + 32, 128), F32), vmem((n_mp, 16, width), BF16), vmem((48, width), BF16), vmem((8, width), F32),
            vmem((24, width), F32), vmem((8, width), F32), vmem((n_dp, 8, width), F32), vmem((n_mp, 8, tile_c), F32),
            vmem((n_a, 2, 4, quarter, tile_c), BF16), *buffers(tile_c), vmem((n_a, 2, 2, quarter, pad), BF16), *buffers(pad),
            vmem((8, dim), F32), vmem((8, 128), F32), vmem((n_dp, 8, 128), F32), vmem((8, 128), F32), vmem((n_mp, 8, 128), F32),
            vmem((slots, 8, 128), F32), vmem((1, dim), F32), vmem((total, dim), BF16), vmem((width, dim), BF16), vmem((width, dim), BF16), dma((3,)),
            dma((n_mp,)), dma((n_mp,)), dma((2, 4)), dma((n_a,)), dma, dma((n_a, 4)), dma((n_a, 4)), dma((n_a, 4)), dma((n_a, 4)),
            dma((2 + groups,)), dma((2 + groups,)), dma((2 + groups,)), dma((2 + groups,)), dma((n_dp,)), dma((n_dp,)),
            dma((n_mp,)), dma((n_mp,)), dma((2, max(n_mp, n_dp))), dma((2, max(n_mp, n_dp))),
        ],
        compiler_params=pltpu.CompilerParams(collective_id=1, has_side_effects=True, vmem_limit_bytes=60 * MIB),
        name="back",
    )(smalls, dgain2, b_msg, msg, a_all, gains_f, slot_lengths, x_tm, wv, wg, sg, gate, z, vals, rg, f_grads)

    gain1_grad, value_grad, gate_grad, gb_grad, taps_grad, cb_grad, wo_grad, gain2_grad, up_grad, down_grad = pl.pallas_call(
        pack_kernel,
        out_shape=[sds((1, dim)), sds(value_proj.shape), sds(gate_proj.shape), sds((1, local_c)), sds(conv_taps.shape),
                   sds((1, local_c)), sds(out_proj.shape), sds((1, dim)), sds(up_proj.shape), sds(down_proj.shape)],
        name="pack",
    )(vg_grad, f_grad, h_grad, small_grad, gain_grad)
    return (output, tokens_grad, gain1_grad[0], value_grad, gate_grad, gb_grad[0], taps_grad, cb_grad[0], wo_grad, gain2_grad[0],
            up_grad, down_grad)


def solution(mesh):
    in_specs = (
        P("dp", "mp", None),
        P("dp", None),
        P("dp", "mp", None),
        P(),
        P(None, "mp"),
        P(None, "mp"),
        P("mp"),
        P(None, "mp"),
        P("mp"),
        P("mp", None),
        P(),
        P(None, "mp"),
        P("mp", None),
    )
    out_specs = (
        P("dp", "mp", None),
        P("dp", "mp", None),
        P(),
        P(None, "mp"),
        P(None, "mp"),
        P("mp"),
        P(None, "mp"),
        P("mp"),
        P("mp", None),
        P(),
        P(None, "mp"),
        P("mp", None),
    )
    return jax.shard_map(per_device, mesh=mesh, in_specs=in_specs, out_specs=out_specs, check_vma=False)
```
